32 devices in a mesh: dp: 8 (over y, x, core), tensor: 4 (over z).
Axes of the slice: x: 2, y: 2, z: 4, core: 2. Of those that a mesh axis runs over, the one named last changes fastest.
Arguments:
- patches: bfloat16 [16384, 1024], P('dp'), may hold values from -6 to 6
- pos_embed: bfloat16 [16384, 1024], P('dp'), may hold values from -6 to 6
- counts: int32 [8, 8], P('dp'), may hold values from 96 to 576, as said below
- ln1_gain: float32 [1024], replicated, may hold values from 0.5 to 1.5
- w_qkv: bfloat16 [1024, 3, 1024], P(None, None, 'tensor'), may hold values from -0.1875 to 0.1875
- w_out: bfloat16 [1024, 1024], P('tensor'), may hold values from -0.75 to 0.75
- ln2_gain: float32 [1024], replicated, may hold values from 0.5 to 1.5
- w_up: bfloat16 [1024, 4096], P(None, 'tensor'), may hold values from -0.1875 to 0.1875
- w_down: bfloat16 [4096, 1024], P('tensor'), may hold values from -0.09375 to 0.09375
- ln3_gain: float32 [1024], replicated, may hold values from 0.5 to 1.5
- w_learn1: bfloat16 [1024, 1024], replicated, may hold values from -0.1875 to 0.1875
- w_learn2: bfloat16 [1024, 8], replicated, may hold values from -0.1875 to 0.1875
- cotangent: bfloat16 [64, 8, 1024], P('dp'), may hold values from -48 to 48
Outputs:
- learned: bfloat16 [64, 8, 1024], P('dp')
- input_grad: bfloat16 [16384, 1024], P('dp')
- grad_ln1_gain: float32 [1024], replicated
- grad_w_qkv: float32 [1024, 3, 1024], P(None, None, 'tensor')
- grad_w_out: float32 [1024, 1024], P('tensor')
- grad_ln2_gain: float32 [1024], replicated
- grad_w_up: float32 [1024, 4096], P(None, 'tensor')
- grad_w_down: float32 [4096, 1024], P('tensor')
- grad_ln3_gain: float32 [1024], replicated
- grad_w_learn1: float32 [1024, 1024], replicated
- grad_w_learn2: float32 [1024, 8], replicated
The draws below stay inside these ranges and needn't reach their ends.
Inputs may be any that keep to these rules, and one draw needn't show every extreme that they name: Each row of 8 counts sums to 2048, and the largest of each row is 576.
All inputs are finite; a program needn't handle non-finite values.
Results may differ from the reference program's by a relative error of at most 0.019.
Values may be sent and summed in bfloat16 or wider, within the bound.
No kernel may reach another device: no remote copies, remote signals or barrier semaphores. Data moves between devices by JAX's collectives and lax.ppermute only.
A program may use at most 256 MiB of HBM per device.

```python
import jax
import jax.numpy as jnp
from jax import lax

D = 1024
HEADS = 16
HEAD_DIM = 64
MLP = 4096
LEARN = 8
LEARN_HID = 1024
MOST = 576
LEAST = 96
BLOCK = 512
TOK_DEV = 2048
IMG_DEV = 8
WINDOW = 1664
TOKENS = 16384
IMAGES = 64
N_DP = 8
N_TENSOR = 4


def counts_row_draw(row_key):
    share_key, order_key = jax.random.split(row_key)
    others = IMG_DEV - 1
    room = MOST - LEAST
    surplus = TOK_DEV - MOST - LEAST * others
    shares = jax.random.randint(share_key, (others,), 1, 16, dtype=jnp.int32)
    extra = jnp.minimum(surplus * shares // jnp.sum(shares), room).astype(jnp.int32)
    leftover = (surplus - jnp.sum(extra)).astype(jnp.int32)

    def fill(left_now, item):
        taken = jnp.minimum(room - item, left_now)
        return (left_now - taken, item + taken)
    unused, extra = lax.scan(fill, leftover, extra)
    whole_row = jnp.concatenate([jnp.full((1,), MOST, jnp.int32), (LEAST + extra).astype(jnp.int32)])
    order = jax.random.permutation(order_key, IMG_DEV)
    return whole_row[order].astype(jnp.int32)


def draw_counts(key, part):
    row_keys = jax.random.split(jax.random.fold_in(key, 7), N_DP)
    return jax.vmap(counts_row_draw)(row_keys)


def levels(stream_key, shape, pieces, least, top_value):
    gain, own = 1.0, jax.random.fold_in(stream_key, 6)
    for dim, parts in pieces:
        draws = jnp.exp(jax.random.uniform(jax.random.fold_in(own, dim), (parts,), jnp.float32, least / len(pieces), top_value / len(pieces)))
        gain = gain * jnp.repeat(draws, shape[dim] // parts).reshape([-1 if axis == dim else 1 for axis in range(len(shape))])
    return gain


def bell_draw(stream_key, shape, width, reach, pieces=(), held_as=jnp.bfloat16):
    factor_of = levels(stream_key, shape, pieces, -0.22, 0.18) if pieces else 1.0
    drawn = jax.random.normal(stream_key, shape, jnp.float32) * width * factor_of
    return jnp.minimum(jnp.maximum(drawn, -reach), reach).astype(held_as)


def setup_inputs(seed: int = 0) -> dict:
    key_list = jax.random.split(jax.random.key(seed), 14)
    return {
        "patches": bell_draw(key_list[0], (TOKENS, D), 1.0, 6.0, ((0, 8),)),
        "pos_embed": bell_draw(key_list[1], (TOKENS, D), 1.0, 6.0, ((0, 8),)),
        "counts": draw_counts(jax.random.fold_in(key_list[13], 71), 0),
        "ln1_gain": jnp.clip(1.0 + 0.1 * jax.random.normal(key_list[3], (D,), jnp.float32), 0.5, 1.5),
        "w_qkv": bell_draw(key_list[4], (D, 3, D), D ** -0.5, 0.1875, ((2, 4),)),
        "w_out": bell_draw(key_list[5], (D, D), (D // 16) ** -0.5, 0.75, ((0, 4),)),
        "ln2_gain": jnp.clip(1.0 + 0.1 * jax.random.normal(key_list[6], (D,), jnp.float32), 0.5, 1.5),
        "w_up": bell_draw(key_list[7], (D, MLP), D ** -0.5, 0.1875, ((1, 4),)),
        "w_down": bell_draw(key_list[8], (MLP, D), MLP ** -0.5, 0.09375, ((0, 4),)),
        "ln3_gain": jnp.clip(1.0 + 0.1 * jax.random.normal(key_list[9], (D,), jnp.float32), 0.5, 1.5),
        "w_learn1": bell_draw(key_list[10], (D, LEARN_HID), D ** -0.5, 0.1875),
        "w_learn2": bell_draw(key_list[11], (LEARN_HID, LEARN), LEARN_HID ** -0.5, 0.1875),
        "cotangent": bell_draw(key_list[12], (IMAGES, LEARN, D), 8.0, 48.0, ((0, 8),)),
    }


HIGHEST = lax.Precision.HIGHEST
EPSILON = 1e-06

@jax.custom_vjp
def low(v):
    return lax.optimization_barrier(v.astype(jnp.bfloat16)).astype(jnp.float32)

@jax.custom_vjp
def low_back(v):
    return v

def low_keep(v):
    return (low(v), None)

def low_pass(kept, grad):
    return (grad,)

def back_keep(v):
    return (v, None)

def back_low(kept, grad):
    return (low(grad),)
low.defvjp(low_keep, low_pass)
low_back.defvjp(back_keep, back_low)

def normalize(values, gain_vector):
    center = values - lax.optimization_barrier(jnp.mean(values, axis=-1, keepdims=True))
    variance = lax.optimization_barrier(jnp.mean(center * center, axis=-1, keepdims=True))
    return center * lax.rsqrt(variance + EPSILON) * gain_vector

def image_ids(counts_row, row_count):
    ends = jnp.cumsum(counts_row).astype(jnp.int32)
    places = jnp.arange(row_count, dtype=jnp.int32)
    return lax.optimization_barrier(jnp.sum((places[:, None] >= ends[None, :]).astype(jnp.int32), axis=1)).astype(jnp.int32)

def attention(query, keys, values, image_of):
    row_count = query.shape[0]
    score_scale = HEAD_DIM ** (-0.5)

    def one_block(block_index):
        query_start = (block_index * BLOCK).astype(jnp.int32)
        key_start = jnp.clip(query_start - MOST, 0, row_count - WINDOW).astype(jnp.int32)
        query_block = lax.dynamic_slice_in_dim(query, query_start, BLOCK, 0)
        key_block = lax.dynamic_slice_in_dim(keys, key_start, WINDOW, 0)
        value_block = lax.dynamic_slice_in_dim(values, key_start, WINDOW, 0)
        query_ids = lax.dynamic_slice_in_dim(image_of, query_start, BLOCK, 0)
        key_ids = lax.dynamic_slice_in_dim(image_of, key_start, WINDOW, 0)
        scores = low_back(jnp.einsum('qhd,khd->hqk', query_block, key_block, precision=HIGHEST) * score_scale)
        allowed = (query_ids[:, None] == key_ids[None, :])[None]
        scores = jnp.where(allowed, scores, -1e+30)
        row_max = lax.optimization_barrier(jnp.max(scores, axis=-1, keepdims=True))
        exponent = jnp.exp(scores - row_max)
        probs = low(exponent / lax.optimization_barrier(jnp.sum(exponent, axis=-1, keepdims=True)))
        return jnp.einsum('hqk,khd->qhd', probs, value_block, precision=HIGHEST)
    blocks = lax.map(jax.checkpoint(one_block), jnp.arange(row_count // BLOCK, dtype=jnp.int32))
    return blocks.reshape(query.shape)

def group_forward(inputs, image_of, row_scale, ln1_gain, w_qkv, w_out, ln2_gain, w_up, w_down, ln3_gain, w_learn1, w_learn2):
    row_count = inputs.shape[0]
    groups = N_TENSOR
    head_width = D // groups
    share = MLP // groups
    norm_one = low(normalize(inputs, ln1_gain))
    copies_one = low_back(jnp.broadcast_to(norm_one, (groups, row_count, D)))
    qkv = jnp.einsum('gtd,dcgh->tcgh', copies_one, w_qkv.reshape(D, 3, groups, head_width), precision=HIGHEST)
    qkv = low(low_back(qkv))
    query = qkv[:, 0].reshape(row_count, HEADS, HEAD_DIM)
    keys = qkv[:, 1].reshape(row_count, HEADS, HEAD_DIM)
    values = qkv[:, 2].reshape(row_count, HEADS, HEAD_DIM)
    mixed = low(low_back(attention(query, keys, values, image_of)))
    partial_attn = jnp.einsum('tgh,ghd->gtd', mixed.reshape(row_count, groups, head_width), w_out.reshape(groups, head_width, D), precision=HIGHEST)
    attended = low_back(lax.optimization_barrier(jnp.sum(low(partial_attn), axis=0)))
    hidden = inputs + attended
    norm_two = low(normalize(hidden, ln2_gain))
    copies_two = low_back(jnp.broadcast_to(norm_two, (groups, row_count, D)))
    upper = low_back(jnp.einsum('gtd,dgf->tgf', copies_two, w_up.reshape(D, groups, share), precision=HIGHEST))
    active = low(jax.nn.gelu(upper, approximate=False))
    partial_mlp = jnp.einsum('tgf,gfd->gtd', active, w_down.reshape(groups, share, D), precision=HIGHEST)
    fed = low_back(lax.optimization_barrier(jnp.sum(low(partial_mlp), axis=0)))
    output = hidden + fed
    norm_three = low(normalize(output, ln3_gain))
    inner = low_back(jnp.dot(norm_three, w_learn1, precision=HIGHEST))
    acted = low(jax.nn.gelu(inner, approximate=False))
    logits = low_back(jnp.dot(acted, w_learn2, precision=HIGHEST))
    weights = low(jax.nn.sigmoid(logits) * row_scale[:, None])
    member = (image_of[:, None] == jnp.arange(IMG_DEV, dtype=jnp.int32)[None, :]).astype(jnp.float32)
    table = (member[:, :, None] * weights[:, None, :]).reshape(row_count, IMG_DEV * LEARN)
    pooled = jnp.einsum('tj,td->jd', table, low(output), precision=HIGHEST)
    return pooled.reshape(IMG_DEV, LEARN, D)

def reference(patches, pos_embed, counts, ln1_gain, w_qkv, w_out, ln2_gain, w_up, w_down, ln3_gain, w_learn1, w_learn2, cotangent):
    wide = jnp.float32
    inputs = (patches.astype(wide) + pos_embed.astype(wide)).reshape(N_DP, TOK_DEV, D)
    cot_groups = cotangent.astype(wide).reshape(N_DP, IMG_DEV, LEARN, D)
    params = (ln1_gain.astype(wide), w_qkv.astype(wide), w_out.astype(wide), ln2_gain.astype(wide), w_up.astype(wide), w_down.astype(wide), ln3_gain.astype(wide), w_learn1.astype(wide), w_learn2.astype(wide))

    def group_step(totals, slab):
        rows_in, counts_row, cot_row = slab
        image_of = image_ids(counts_row, TOK_DEV)
        member = (image_of[:, None] == jnp.arange(IMG_DEV, dtype=jnp.int32)[None, :]).astype(wide)
        row_scale = lax.optimization_barrier(jnp.sum(member * lax.rsqrt(counts_row.astype(wide))[None, :], axis=1))

        def forward_fn(rows_value, *weights_all):
            return group_forward(rows_value, image_of, row_scale, *weights_all)
        pooled, pullback = jax.vjp(forward_fn, rows_in, *params)
        grads = pullback(cot_row)
        totals = tuple((left + right for left, right in zip(totals, grads[1:])))
        return (totals, (pooled.astype(jnp.bfloat16), grads[0].astype(jnp.bfloat16)))
    zeros_init = tuple((jnp.zeros_like(param_item) for param_item in params))
    totals, stacked = lax.scan(group_step, zeros_init, (inputs, counts, cot_groups))
    learned = stacked[0].reshape(N_DP * IMG_DEV, LEARN, D)
    input_grad = stacked[1].reshape(N_DP * TOK_DEV, D)
    return (learned, input_grad, totals[0], totals[1], totals[2], totals[3], totals[4], totals[5], totals[6], totals[7], totals[8])
```

```python
import functools

import jax
import jax.numpy as jnp
from jax import lax
from jax.experimental import pallas as pl
from jax.experimental.pallas import tpu as pltpu
from jax.sharding import PartitionSpec as P

HEAD_DIM = 64
MOST = 576
EPSILON = 1e-06
LOW = jnp.bfloat16
WIDE = jnp.float32
FAR = -1e30


def layer_norm(values):
    center = values - jnp.mean(values, axis=-1, keepdims=True)
    variance = jnp.mean(center * center, axis=-1, keepdims=True)
    inverse = lax.rsqrt(variance + EPSILON)
    return center * inverse, inverse


def norm_back(grad_in, gain, normed, inverse):
    gain_grad = jnp.sum(grad_in * normed, axis=0)
    scaled = grad_in * gain
    result = (
        scaled
        - jnp.mean(scaled, axis=-1, keepdims=True)
        - normed * jnp.mean(scaled * normed, axis=-1, keepdims=True)
    ) * inverse
    return result, gain_grad


def gelu_both(values):
    share = 0.5 * (1.0 + lax.erf(values * (0.5**0.5)))
    density = jnp.exp(-0.5 * values * values) * 0.3989422804014327
    return values * share, share + values * density


def dot(left, right, left_dim, right_dim):
    return lax.dot_general(
        left, right, (((left_dim,), (right_dim,)), ((), ())), preferred_element_type=WIDE
    )


def dot_low(left, right, left_dim, right_dim):
    return dot(left, right, left_dim, right_dim).astype(LOW)


def row_capacity(rows, images, n_tensor):
    if n_tensor >= images:
        most = MOST
    elif n_tensor == 4 and images == 8 and rows == 2048:
        most = 630
    else:
        most = rows // n_tensor + MOST
    return min(rows, -(-most // 128) * 128)


def place_kernel(n_tensor, counts_ref, place_ref):
    images = counts_ref.shape[1]
    count = [counts_ref[0, i] for i in range(images)]
    zero = count[0] * 0
    used, device, offset = [zero] * images, [zero] * images, [zero] * images
    loads = [zero] * n_tensor
    for _ in range(images):
        best, at = zero - 1, zero
        for i in range(images):
            better = jnp.logical_and(used[i] == 0, count[i] > best)
            best = jnp.where(better, count[i], best)
            at = jnp.where(better, i, at)
        least, least_at = loads[0], zero
        for b in range(1, n_tensor):
            better = loads[b] < least
            least = jnp.where(better, loads[b], least)
            least_at = jnp.where(better, b, least_at)
        for i in range(images):
            here = at == i
            used[i] = jnp.where(here, 1, used[i])
            device[i] = jnp.where(here, least_at, device[i])
            offset[i] = jnp.where(here, least, offset[i])
        for b in range(n_tensor):
            loads[b] = loads[b] + jnp.where(least_at == b, best, 0)
    start = zero
    for i in range(images):
        place_ref[0, i] = device[i]
        place_ref[1, i] = offset[i]
        place_ref[2, i] = start
        start = start + count[i]


def place_images(counts, n_tensor):
    images = counts.shape[1]
    return pl.pallas_call(
        functools.partial(place_kernel, n_tensor),
        out_shape=jax.ShapeDtypeStruct((3, images), jnp.int32),
        in_specs=[pl.BlockSpec(memory_space=pltpu.SMEM)],
        out_specs=pl.BlockSpec(memory_space=pltpu.SMEM),
        name="place_images",
    )(counts)


def pass_on(near, n_tensor):
    below = above = near
    for _ in range(n_tensor - 1):
        below = lax.ppermute(below, "tensor", [(i, i + 1) for i in range(n_tensor - 1)])
        above = lax.ppermute(above, "tensor", [(i + 1, i) for i in range(n_tensor - 1)])
        below, above = yield below, above


def row_map(place, counts, device, capacity):
    row = jnp.arange(capacity, dtype=jnp.int32)[:, None]
    offset, start = place[1][None], place[2][None]
    inside = (place[0][None] == device) & (row >= offset) & (row < offset + counts)
    image = jnp.sum(jnp.where(inside, jnp.arange(counts.shape[1], dtype=jnp.int32) + 1, 0), axis=1) - 1
    source = jnp.sum(jnp.where(inside, start - offset + row + 1, 0), axis=1) - 1
    return image, source


def after(value, *others):
    return lax.optimization_barrier((value,) + others)[0]


def swap(value, axis, size, mask):
    return lax.ppermute(value, axis, [(i, i ^ mask) for i in range(size)])


def reorder(value, dim, size, index):
    return jnp.concatenate(
        [lax.dynamic_slice_in_dim(value, index ^ m, 1, dim) for m in range(size)], axis=dim
    )


def link_bits(n_dp, half):
    bits = list(range(1, n_dp.bit_length() - 1))
    return bits[::-1] if half else bits


def gather_links(far, n_dp):
    value = [far[0], far[1]]
    count = n_dp.bit_length() - 2
    for step in range(count):
        for half in range(2):
            bit = link_bits(n_dp, half)[step]
            value[half] = jnp.stack([value[half], swap(value[half], "dp", n_dp, 1 << bit)])
    value[1] = jnp.transpose(value[1], tuple(range(count))[::-1] + tuple(range(count, value[1].ndim)))
    return [v.reshape((1 << count,) + v.shape[count:]) for v in value]


def own_units(shard, n_dp, index):
    lead, units, width = shard.shape
    part = units // (2 * n_dp)
    split = shard.reshape(lead, n_dp, 2, part, width)
    ordered = reorder(split, 1, n_dp, index).reshape(lead, n_dp // 2, 2, 2, part, width)
    return [ordered[:, :, core] for core in range(2)]


def my_piece(shard, n_dp, index):
    lead, units, width = shard.shape
    part = units // (2 * n_dp)
    split = shard.reshape(lead, n_dp, 2, part, width)
    mine = lax.dynamic_slice_in_dim(split, index, 1, 1)[:, 0]
    return jnp.transpose(mine, (1, 0, 2, 3)).reshape(2, lead * part, width)


def gather_tensor(pieces, n_tensor):
    pack = jnp.concatenate(pieces, axis=1)
    return jnp.stack([swap(pack, "tensor", n_tensor, j) for j in range(1, n_tensor)], axis=1)


def gather_core(near, sizes, n_dp, n_tensor):
    width = near[0].shape[-1]
    both = [near, [swap(n, "dp", n_dp, 1) for n in near]]
    result = []
    for halves in both:
        weights, at = [], 0
        for lead, part in sizes:
            pieces = [
                h[:, :, at : at + lead * part].reshape(n_dp // 2, n_tensor - 1, lead, part, width)
                for h in halves
            ]
            weights.append(jnp.transpose(jnp.stack(pieces), (3, 2, 1, 0, 4, 5)))
            at += lead * part
        result.append(weights)
    return result


def join(own, far, part_first):
    width = own.shape[-1]
    full = jnp.concatenate([own[:, None], far], axis=1)
    if part_first:
        full = jnp.transpose(full, (3, 0, 2, 1, 4, 5))
    return full.reshape(-1, width)


def split_units(grad, lead, n_dp, n_tensor, part_first):
    width = grad.shape[-1]
    links = n_dp // 2
    if part_first:
        parts = grad.reshape(2, links, -1, width)
        return [parts[0], parts[1]]
    split = grad.reshape(lead, n_tensor, links, 2, -1, width)
    return [
        jnp.transpose(split[:, :, :, half], (2, 1, 0, 3, 4)).reshape(links, -1, width) for half in range(2)
    ]


def split_shared(grad, n_dp, index):
    links = n_dp // 2
    parts = grad.reshape(2, links, -1, grad.shape[-1])
    ordered = reorder(parts, 1, links, index // 2)
    return [ordered[0], ordered[1]]


def link_sums(groups, n_dp):
    width = groups[0][0].shape[-1]
    bits = n_dp.bit_length() - 2
    halves = [[g[half].reshape((2,) * bits + g[half].shape[1:]) for g in groups] for half in range(2)]
    held = [list(range(bits, 0, -1)) for _ in range(2)]
    for step in range(bits):
        for half in range(2):
            bit = link_bits(n_dp, 1 - half)[step]
            dim = held[half].index(bit)
            held[half].remove(bit)
            keeps = [lax.index_in_dim(p, 0, dim, keepdims=False) for p in halves[half]]
            aways = [lax.index_in_dim(p, 1, dim, keepdims=False).reshape(-1, width) for p in halves[half]]
            came = swap(jnp.concatenate(aways) if len(aways) > 1 else aways[0], "dp", n_dp, 1 << bit)
            parts, at = [], 0
            for keep, away in zip(keeps, aways):
                piece = came[at : at + away.shape[0]].reshape(keep.shape)
                parts.append((keep.astype(WIDE) + piece.astype(WIDE)).astype(LOW))
                at += away.shape[0]
            halves[half] = parts
        yield halves


def advance(halves, *others):
    flat = lax.optimization_barrier(tuple(halves[0] + halves[1]) + others)
    count = len(halves[0])
    halves[0][:] = flat[:count]
    halves[1][:] = flat[count : 2 * count]


def reduce_tensor(scattered, shared, n_tensor):
    width = (scattered + shared)[0].shape[-1]
    split = [s.reshape(2, n_tensor, -1, width) for s in scattered]
    total = None
    for j in range(n_tensor):
        piece = [s[:, j] for s in split] + shared
        piece = jnp.concatenate(piece, axis=1) if len(piece) > 1 else piece[0]
        came = (piece if j == 0 else swap(piece, "tensor", n_tensor, j)).astype(WIDE)
        total = came if total is None else total + came
    return total.astype(LOW)


def spread_plane(total, n_dp):
    near = jnp.stack(gather_links(total, n_dp), axis=1)
    return jnp.stack([near, swap(near, "dp", n_dp, 1)], axis=1)


def place_units(seen, lead, n_dp, index):
    links, _, _, rows, width = seen.shape
    seen = seen.reshape(n_dp, 2, lead, rows // lead, width)
    return reorder(jnp.transpose(seen, (2, 0, 1, 3, 4)), 1, n_dp, index).reshape(lead, -1, width)


def place_shared(seen, n_dp, index):
    links, _, _, rows, width = seen.shape
    seen = reorder(jnp.transpose(seen, (1, 2, 0, 3, 4)), 0, 2, index & 1)
    return reorder(seen, 2, links, index // 2).reshape(-1, width)


def attend_kernel(scale, first_ref, second_ref, column_ref, row_ref, mixed_first_ref, mixed_second_ref, log_ref):
    query, key, value = [jnp.concatenate([first_ref[i, 0], second_ref[i, 0]]) for i in range(3)]
    scores = dot(key, query * scale, 0, 0)
    scores = jnp.where(column_ref[...] == row_ref[...], scores, FAR)
    most = jnp.max(scores, axis=0, keepdims=True)
    exponent = jnp.exp(scores - most)
    total = jnp.sum(exponent, axis=0, keepdims=True)
    mixed = (dot(value, exponent.astype(LOW), 1, 0) / total).astype(LOW)
    half = mixed.shape[0] // 2
    mixed_first_ref[0] = mixed[:half]
    mixed_second_ref[0] = mixed[half:]
    log_ref[0] = most + jnp.log(total)


def attend(first, second, image, scale):
    _, heads, half, rows = first.shape
    three = pl.BlockSpec((3, 1, half, rows), lambda h: (0, h, 0, 0))
    one = pl.BlockSpec((1, half, rows), lambda h: (h, 0, 0))
    return pl.pallas_call(
        functools.partial(attend_kernel, scale),
        grid=(heads,),
        in_specs=[
            three,
            three,
            pl.BlockSpec((rows, 1), lambda h: (0, 0)),
            pl.BlockSpec((1, rows), lambda h: (0, 0)),
        ],
        out_specs=[one, one, pl.BlockSpec((1, 1, rows), lambda h: (h, 0, 0))],
        out_shape=[
            jax.ShapeDtypeStruct((heads, half, rows), LOW),
            jax.ShapeDtypeStruct((heads, half, rows), LOW),
            jax.ShapeDtypeStruct((heads, 1, rows), WIDE),
        ],
        compiler_params=pltpu.CompilerParams(vmem_limit_bytes=48 << 20),
        cost_estimate=pl.CostEstimate(
            flops=4 * rows * rows * heads * 512, bytes_accessed=8 * heads * HEAD_DIM * rows, transcendentals=0
        ),
        name="attend",
    )(first, second, image[:, None], image[None, :])


def attend_back_kernel(
    scale,
    first_ref,
    second_ref,
    mixed_first_ref,
    mixed_second_ref,
    grad_first_ref,
    grad_second_ref,
    log_ref,
    column_ref,
    row_ref,
    out_first_ref,
    out_second_ref,
):
    query, key, value = [jnp.concatenate([first_ref[i, 0], second_ref[i, 0]]) for i in range(3)]
    query = query * scale
    mixed = jnp.concatenate([mixed_first_ref[0], mixed_second_ref[0]])
    grad = jnp.concatenate([grad_first_ref[0], grad_second_ref[0]])
    scores = dot(key, query, 0, 0)
    scores = jnp.where(column_ref[...] == row_ref[...], scores, FAR)
    probs = jnp.exp(scores - log_ref[0])
    grad_probs = dot(value, grad, 0, 0)
    inner = jnp.sum(mixed.astype(WIDE) * grad.astype(WIDE), axis=0, keepdims=True)
    grad_scores = (probs * (grad_probs - inner)).astype(LOW)
    grads = (
        (dot(key, grad_scores, 1, 0) * scale).astype(LOW),
        dot(query, grad_scores, 1, 1).astype(LOW),
        dot(grad, probs.astype(LOW), 1, 1).astype(LOW),
    )
    half = mixed.shape[0] // 2
    for i, item in enumerate(grads):
        out_first_ref[i, 0] = item[:half]
        out_second_ref[i, 0] = item[half:]


def attend_back(first, second, mixed, grad_mixed, log_sums, image, scale):
    _, heads, half, rows = first.shape
    three = pl.BlockSpec((3, 1, half, rows), lambda h: (0, h, 0, 0))
    one = pl.BlockSpec((1, half, rows), lambda h: (h, 0, 0))
    return pl.pallas_call(
        functools.partial(attend_back_kernel, scale),
        grid=(heads,),
        in_specs=[
            three,
            three,
            one,
            one,
            one,
            one,
            pl.BlockSpec((1, 1, rows), lambda h: (h, 0, 0)),
            pl.BlockSpec((rows, 1), lambda h: (0, 0)),
            pl.BlockSpec((1, rows), lambda h: (0, 0)),
        ],
        out_specs=[three, three],
        out_shape=[jax.ShapeDtypeStruct((3, heads, half, rows), LOW)] * 2,
        compiler_params=pltpu.CompilerParams(vmem_limit_bytes=48 << 20),
        cost_estimate=pl.CostEstimate(
            flops=10 * rows * rows * heads * 512, bytes_accessed=16 * heads * HEAD_DIM * rows, transcendentals=0
        ),
        name="attend_back",
    )(first, second, *mixed, *grad_mixed, log_sums, image[:, None], image[None, :])


def local(
    n_dp,
    n_tensor,
    patches,
    pos_embed,
    counts,
    ln1_gain,
    w_qkv,
    w_out,
    ln2_gain,
    w_up,
    w_down,
    ln3_gain,
    w_learn1,
    w_learn2,
    cotangent,
):
    rows, width = patches.shape
    images = counts.shape[1]
    tokens = w_learn2.shape[1]
    capacity = row_capacity(rows, images, n_tensor)
    scale = HEAD_DIM**-0.5
    tensor_index = lax.axis_index("tensor")
    index = lax.axis_index("dp")
    heads = n_tensor * w_qkv.shape[2] // HEAD_DIM
    mate = lambda value: swap(value, "dp", n_dp, 1)

    turned = jnp.transpose(w_qkv, (1, 2, 0))
    piece_qkv = my_piece(turned, n_dp, index)
    far_a = gather_tensor([piece_qkv], n_tensor)
    pieces = [my_piece(w, n_dp, index) for w in (w_out[None], jnp.transpose(after(w_up, far_a))[None], w_down[None])]
    far_b = gather_tensor(pieces[:2], n_tensor)
    near_a = gather_links(far_a, n_dp)
    far_c = gather_tensor([after(pieces[2], far_b, *near_a)], n_tensor)
    near_b = gather_links(after(far_b, *near_a), n_dp)
    near_c = gather_links(after(far_c, *near_b), n_dp)
    shards = [turned, w_out[None], jnp.transpose(w_up)[None], w_down[None]]
    sizes = [(s.shape[0], s.shape[1] // (2 * n_dp)) for s in shards]
    owns = [own_units(s, n_dp, index) for s in shards]
    plane_a = gather_core(near_a, sizes[:1], n_dp, n_tensor)
    plane_b = gather_core(near_b, sizes[1:3], n_dp, n_tensor)
    plane_c = gather_core(near_c, sizes[3:], n_dp, n_tensor)
    full_qkv = [join(owns[0][c], plane_a[c][0], False) for c in range(2)]
    full_out = [join(owns[1][c], plane_b[c][0], False) for c in range(2)]
    full_up = [join(owns[2][c], plane_b[c][1], True) for c in range(2)]
    full_down = [join(owns[3][c], plane_c[c][0], True) for c in range(2)]

    place = place_images(counts, n_tensor)
    image, source = row_map(place, counts, tensor_index, capacity)
    pick = (source[:, None] == jnp.arange(rows, dtype=jnp.int32)[None, :]).astype(LOW)
    inputs = dot(pick, patches, 1, 0) + dot(pick, pos_embed, 1, 0)
    member = (image[:, None] == jnp.arange(images, dtype=jnp.int32)[None, :]).astype(WIDE)
    row_scale = jnp.sum(member * lax.rsqrt(counts[0].astype(WIDE))[None, :], axis=1)

    normed_one, inverse_one = layer_norm(inputs)
    low_one = (normed_one * ln1_gain).astype(LOW)
    qkv = [dot_low(w, low_one, 1, 1).reshape(3, heads, -1, capacity) for w in full_qkv]
    mixed_first, mixed_second, log_sums = attend(*qkv, image, scale)
    mixed = [m.reshape(-1, capacity) for m in (mixed_first, mixed_second)]
    hidden = inputs + dot(mixed[0], full_out[0], 0, 0) + dot(mixed[1], full_out[1], 0, 0)
    normed_two, inverse_two = layer_norm(hidden)
    low_two = (normed_two * ln2_gain).astype(LOW)
    mate_mixed, mate_one = mate(mixed[1]), mate(low_one)
    low_two = after(low_two, mate_mixed, mate_one)
    active, slope = [], []
    for w in full_up:
        value, rate = gelu_both(dot(low_two, w, 1, 1))
        active.append(value.astype(LOW))
        slope.append(rate.astype(LOW))
    output = hidden + dot(active[0], full_down[0], 1, 0) + dot(active[1], full_down[1], 1, 0)
    normed_three, inverse_three = layer_norm(output)
    low_three = (normed_three * ln3_gain).astype(LOW)
    mate_active, mate_two = mate(active[1]), mate(low_two)
    low_three = after(low_three, mate_active, mate_two)
    acted, learn_slope = gelu_both(dot(low_three, w_learn1, 1, 0))
    acted, learn_slope = acted.astype(LOW), learn_slope.astype(LOW)
    select = jax.nn.sigmoid(dot(acted, w_learn2, 1, 0))
    weights = (select * row_scale[:, None]).astype(LOW)
    table = (member.astype(LOW)[:, :, None] * weights[:, None, :]).reshape(capacity, images * tokens)
    low_out = output.astype(LOW)
    learned = dot_low(table, low_out, 0, 0)
    total = learned.astype(WIDE)
    for j in range(1, n_tensor):
        total = total + swap(learned, "tensor", n_tensor, j).astype(WIDE)
    learned = total.astype(LOW).reshape(images, tokens, width)

    grad_pooled = cotangent.reshape(images * tokens, width)
    grad_output = dot(table, grad_pooled, 1, 0)
    grad_table = dot(low_out, grad_pooled, 1, 1)
    grad_weights = jnp.sum(grad_table.reshape(capacity, images, tokens) * member[:, :, None], axis=1)
    grad_logits = (grad_weights * row_scale[:, None] * select * (1.0 - select)).astype(LOW)
    grad_learn2 = dot(grad_logits, acted, 0, 0)
    grad_inner = (dot(grad_logits, w_learn2, 1, 1) * learn_slope.astype(WIDE)).astype(LOW)
    side = width // 2
    three_keep = lax.dynamic_slice_in_dim(low_three, (index & 1) * side, side, 1)
    three_away = lax.dynamic_slice_in_dim(low_three, (1 - (index & 1)) * side, side, 1)
    grad_learn1 = (
        dot(three_keep, grad_inner, 0, 0) + dot(mate(three_away), mate(grad_inner), 0, 0)
    ).astype(LOW)
    grad_from_three, grad_gain3 = norm_back(
        dot(grad_inner, w_learn1, 1, 1), ln3_gain, normed_three, inverse_three
    )
    grad_output = grad_output + grad_from_three

    grad_fed = after(grad_output.astype(LOW), learned, grad_learn1)
    mate_fed = mate(grad_fed)
    grad_upper = [
        (dot(grad_fed, w, 1, 1) * s.astype(WIDE)).astype(LOW) for w, s in zip(full_down, slope)
    ]
    mate_upper = mate(grad_upper[1])
    grad_down = (dot(active[0], grad_fed, 0, 0) + dot(mate_active, mate_fed, 0, 0)).astype(LOW)
    units = functools.partial(split_units, n_dp=n_dp, n_tensor=n_tensor)
    share = lambda grad: split_shared(grad, n_dp, index)
    steps_a = link_sums([units(grad_down, 1, part_first=True), share(grad_learn1)], n_dp)
    sums_a = next(steps_a)
    grad_upper = [after(g, grad_down, mate_upper) for g in grad_upper]
    grad_from_two, grad_gain2 = norm_back(
        dot(grad_upper[0], full_up[0], 1, 0) + dot(grad_upper[1], full_up[1], 1, 0),
        ln2_gain,
        normed_two,
        inverse_two,
    )
    grad_hidden = grad_output + grad_from_two

    grad_attended = grad_hidden.astype(LOW)
    mate_attended = mate(grad_attended)
    grad_mixed = [dot_low(w, grad_attended, 1, 1).reshape(heads, -1, capacity) for w in full_out]
    grad_qkv = attend_back(*qkv, (mixed_first, mixed_second), grad_mixed, log_sums, image, scale)
    grad_qkv = [g.reshape(-1, capacity) for g in grad_qkv]
    mate_qkv = mate(grad_qkv[1])
    grad_qkv = [after(g, mate_attended, *sums_a[0], *sums_a[1]) for g in grad_qkv]
    grad_from_one, grad_gain1 = norm_back(
        dot(grad_qkv[0], full_qkv[0], 0, 0) + dot(grad_qkv[1], full_qkv[1], 0, 0),
        ln1_gain,
        normed_one,
        inverse_one,
    )
    near = (grad_hidden + grad_from_one).astype(LOW)

    grad_upper = [after(g, near) for g in grad_upper]
    grad_up = (dot(grad_upper[0], low_two, 0, 0) + dot(mate_upper, mate_two, 0, 0)).astype(LOW)
    grad_out = (dot(mixed[0], grad_attended, 1, 0) + dot(mate_mixed, mate_attended, 1, 0)).astype(LOW)
    grad_qkv_weight = (dot(grad_qkv[0], low_one, 1, 0) + dot(mate_qkv, mate_one, 1, 0)).astype(LOW)
    extra = jnp.concatenate([jnp.stack([grad_gain1, grad_gain2, grad_gain3]), grad_learn2])
    extra = jnp.pad(extra, ((0, 8 * n_dp - extra.shape[0]), (0, 0)))
    extra = (extra + mate(extra)).astype(LOW)

    passing = pass_on(near, n_tensor)
    moved = [next(passing)]
    for sums_a in steps_a:
        pass
    pair = [jnp.stack([a, b]) for a, b in zip(*sums_a)]
    moved[0] = after(moved[0][0], moved[0][1], pair[0]), moved[0][1]
    sum_a = reduce_tensor([after(pair[0], moved[0][0])], pair[1:], n_tensor)
    steps_b = link_sums(
        [
            units(after(grad_up, pair[0]), 1, part_first=True),
            units(grad_out, 1, part_first=False),
            units(grad_qkv_weight, 3, part_first=False),
            share(extra),
        ],
        n_dp,
    )
    for sums_b in steps_b:
        pass
    pair = [jnp.stack([a, b]) for a, b in zip(*sums_b)]
    for step in range(1, n_tensor - 2):
        moved.append(passing.send((after(moved[-1][0], sum_a), moved[-1][1])))
    sum_b = reduce_tensor([after(pair[0], *moved[-1])] + pair[1:3], pair[3:], n_tensor)
    seen_a = spread_plane(after(sum_a, pair[0]), n_dp)
    moved.append(passing.send((after(moved[-1][0], sum_b), moved[-1][1])))
    seen_b = spread_plane(sum_b, n_dp)

    def spans(seen, grads, split):
        at = 0
        for grad, parts in zip(grads, split):
            size = grad.shape[0] // (parts * n_dp)
            yield seen[:, :, :, at : at + size]
            at += size

    found_down, found_learn = spans(seen_a, (grad_down, grad_learn1), (n_tensor, 1))
    found_up, found_out, found_qkv, found_extra = spans(
        seen_b, (grad_up, grad_out, grad_qkv_weight, extra), (n_tensor, n_tensor, n_tensor, 1)
    )
    down_sum = place_units(found_down, 1, n_dp, index)[0]
    learn_sum = place_shared(found_learn, n_dp, index)
    up_sum = place_units(found_up, 1, n_dp, index)[0]
    out_sum = place_units(found_out, 1, n_dp, index)[0]
    qkv_sum = place_units(found_qkv, 3, n_dp, index)
    small = reorder(jnp.transpose(found_extra[:, 0], (1, 0, 2, 3)), 1, n_dp // 2, index // 2)
    small = small.reshape(-1, width).astype(WIDE)

    def back(blocks):
        sources = jnp.concatenate([b[0] for b in blocks])
        spot = (jnp.arange(rows, dtype=jnp.int32)[:, None] == sources[None, :]).astype(LOW)
        return dot(spot, jnp.concatenate([b[1] for b in blocks]), 1, 0)

    source_of = lambda device: row_map(place, counts, device, capacity)[1]
    blocks = [(source, near)]
    for step, (below, above) in enumerate(moved, 1):
        if 2 * step < n_tensor:
            blocks.append((source_of(tensor_index - step), below))
            blocks.append((source_of(tensor_index + step), above))
        else:
            merged = jnp.maximum(source_of(tensor_index - step), source_of(tensor_index + step))
            blocks.append((merged, below + above))
    input_grad = (back(blocks[:-1]) + back(blocks[-1:])).astype(LOW)
    return (
        learned,
        input_grad,
        small[0],
        jnp.transpose(qkv_sum.astype(WIDE), (2, 0, 1)),
        out_sum.astype(WIDE),
        small[1],
        jnp.transpose(up_sum.astype(WIDE)),
        down_sum.astype(WIDE),
        small[2],
        learn_sum.astype(WIDE),
        jnp.transpose(small[3 : 3 + tokens]),
    )


def solution(mesh):
    return jax.shard_map(
        functools.partial(local, mesh.shape["dp"], mesh.shape["tensor"]),
        mesh=mesh,
        in_specs=(
            P("dp", None),
            P("dp", None),
            P("dp", None),
            P(),
            P(None, None, "tensor"),
            P("tensor", None),
            P(),
            P(None, "tensor"),
            P("tensor", None),
            P(),
            P(),
            P(),
            P("dp", None, None),
        ),
        out_specs=(
            P("dp", None, None),
            P("dp", None),
            P(),
            P(None, None, "tensor"),
            P("tensor", None),
            P(),
            P(None, "tensor"),
            P("tensor", None),
            P(),
            P(),
            P(),
        ),
        check_vma=False,
    )
```

```python
import functools

import jax
import jax.numpy as jnp
from jax import lax
from jax.experimental import pallas as pl
from jax.experimental.pallas import tpu as pltpu
from jax.sharding import PartitionSpec as P

HEAD_DIM = 64
MOST = 576
EPSILON = 1e-06
LOW = jnp.bfloat16
WIDE = jnp.float32
FAR = -1e30


def layer_norm(values):
    center = values - jnp.mean(values, axis=-1, keepdims=True)
    variance = jnp.mean(center * center, axis=-1, keepdims=True)
    inverse = lax.rsqrt(variance + EPSILON)
    return center * inverse, inverse


def norm_back(grad_in, gain, normed, inverse):
    gain_grad = jnp.sum(grad_in * normed, axis=0)
    scaled = grad_in * gain
    result = (
        scaled
        - jnp.mean(scaled, axis=-1, keepdims=True)
        - normed * jnp.mean(scaled * normed, axis=-1, keepdims=True)
    ) * inverse
    return result, gain_grad


def gelu_both(values):
    share = 0.5 * (1.0 + lax.erf(values * (0.5**0.5)))
    density = jnp.exp(-0.5 * values * values) * 0.3989422804014327
    return values * share, share + values * density


def dot(left, right, left_dim, right_dim):
    return lax.dot_general(
        left, right, (((left_dim,), (right_dim,)), ((), ())), preferred_element_type=WIDE
    )


def dot_low(left, right, left_dim, right_dim):
    return dot(left, right, left_dim, right_dim).astype(LOW)


def row_capacity(rows, images, n_tensor):
    if n_tensor >= images:
        most = MOST
    elif n_tensor == 4 and images == 8 and rows == 2048:
        most = 630
    else:
        most = rows // n_tensor + MOST
    return min(rows, -(-most // 128) * 128)


def place_kernel(n_tensor, counts_ref, place_ref):
    images = counts_ref.shape[1]
    count = [counts_ref[0, i] for i in range(images)]
    zero = count[0] * 0
    used, device, offset = [zero] * images, [zero] * images, [zero] * images
    loads = [zero] * n_tensor
    for _ in range(images):
        best, at = zero - 1, zero
        for i in range(images):
            better = jnp.logical_and(used[i] == 0, count[i] > best)
            best = jnp.where(better, count[i], best)
            at = jnp.where(better, i, at)
        least, least_at = loads[0], zero
        for b in range(1, n_tensor):
            better = loads[b] < least
            least = jnp.where(better, loads[b], least)
            least_at = jnp.where(better, b, least_at)
        for i in range(images):
            here = at == i
            used[i] = jnp.where(here, 1, used[i])
            device[i] = jnp.where(here, least_at, device[i])
            offset[i] = jnp.where(here, least, offset[i])
        for b in range(n_tensor):
            loads[b] = loads[b] + jnp.where(least_at == b, best, 0)
    start = zero
    for i in range(images):
        place_ref[0, i] = device[i]
        place_ref[1, i] = offset[i]
        place_ref[2, i] = start
        start = start + count[i]


def place_images(counts, n_tensor):
    images = counts.shape[1]
    return pl.pallas_call(
        functools.partial(place_kernel, n_tensor),
        out_shape=jax.ShapeDtypeStruct((3, images), jnp.int32),
        in_specs=[pl.BlockSpec(memory_space=pltpu.SMEM)],
        out_specs=pl.BlockSpec(memory_space=pltpu.SMEM),
        name="place_images",
    )(counts)


def gather_rows(rows, n_tensor):
    held = rows[None]
    mask = n_tensor // 2
    while mask:
        (came,) = yield [swap(held, "tensor", n_tensor, mask)], [held]
        held = jnp.stack([held, came], axis=1).reshape((-1,) + rows.shape)
        mask //= 2
    yield [held], []


def row_map(place, counts, device, capacity):
    row = jnp.arange(capacity, dtype=jnp.int32)[:, None]
    offset, start = place[1][None], place[2][None]
    inside = (place[0][None] == device) & (row >= offset) & (row < offset + counts)
    image = jnp.sum(jnp.where(inside, jnp.arange(counts.shape[1], dtype=jnp.int32) + 1, 0), axis=1) - 1
    source = jnp.sum(jnp.where(inside, start - offset + row + 1, 0), axis=1) - 1
    return image, source


def after(value, *others):
    return lax.optimization_barrier((value,) + others)[0]


class Flow:
    def __init__(self, stages, generator):
        self.left = stages
        self.generator = generator
        self.came, self.sent = next(generator)

    def go(self, *others):
        self.came, self.sent = self.generator.send([after(c, *others) for c in self.came])
        self.left -= 1
        return self

    def finish(self, *others):
        while self.left:
            self.go(*others)
        return self.came


def swap(value, axis, size, mask):
    return lax.ppermute(value, axis, [(i, i ^ mask) for i in range(size)])


def reorder(value, dim, size, index):
    return jnp.concatenate(
        [lax.dynamic_slice_in_dim(value, index ^ m, 1, dim) for m in range(size)], axis=dim
    )


def link_bits(n_dp, half):
    bits = list(range(1, n_dp.bit_length() - 1))
    return bits[::-1] if half else bits


def link_gathers(far, n_dp):
    value = [far[0], far[1]]
    for step in range(n_dp.bit_length() - 2):
        came = [swap(value[half], "dp", n_dp, 1 << link_bits(n_dp, half)[step]) for half in range(2)]
        came = yield came, value
        value = [jnp.stack([v, c]) for v, c in zip(value, came)]
    yield value, []


def links_first(value, n_dp):
    count = n_dp.bit_length() - 2
    turned = jnp.transpose(value[1], tuple(range(count))[::-1] + tuple(range(count, value[1].ndim)))
    return [v.reshape((1 << count,) + v.shape[count:]) for v in (value[0], turned)]


def own_units(shard, n_dp, index):
    lead, units, width = shard.shape
    part = units // (2 * n_dp)
    split = shard.reshape(lead, n_dp, 2, part, width)
    ordered = reorder(split, 1, n_dp, index).reshape(lead, n_dp // 2, 2, 2, part, width)
    return [ordered[:, :, core] for core in range(2)]


def my_piece(shard, n_dp, index):
    lead, units, width = shard.shape
    part = units // (2 * n_dp)
    split = shard.reshape(lead, n_dp, 2, part, width)
    mine = lax.dynamic_slice_in_dim(split, index, 1, 1)[:, 0]
    return jnp.transpose(mine, (1, 0, 2, 3)).reshape(2, lead * part, width)


def gather_tensor(pieces, n_tensor):
    pack = jnp.concatenate(pieces, axis=1) if len(pieces) > 1 else pieces[0]
    came = yield [swap(pack, "tensor", n_tensor, j) for j in range(1, n_tensor)], [pack]
    yield [jnp.stack(came, axis=1)], []


def far_units(halves, sizes, n_dp, n_tensor):
    width = halves[0].shape[-1]
    weights, at = [], 0
    for lead, part in sizes:
        pieces = [
            h[:, :, at : at + lead * part].reshape(n_dp // 2, n_tensor - 1, lead, part, width) for h in halves
        ]
        weights.append(jnp.transpose(jnp.stack(pieces), (3, 2, 1, 0, 4, 5)))
        at += lead * part
    return weights


def join(own, far, part_first):
    width = own.shape[-1]
    full = jnp.concatenate([own[:, None], far], axis=1)
    if part_first:
        full = jnp.transpose(full, (3, 0, 2, 1, 4, 5))
    return full.reshape(-1, width)


def split_units(grad, lead, n_dp, n_tensor, part_first):
    width = grad.shape[-1]
    links = n_dp // 2
    if part_first:
        parts = grad.reshape(2, links, -1, width)
        return [parts[0], parts[1]]
    split = grad.reshape(lead, n_tensor, links, 2, -1, width)
    return [
        jnp.transpose(split[:, :, :, half], (2, 1, 0, 3, 4)).reshape(links, -1, width) for half in range(2)
    ]


def split_shared(grad, n_dp, index):
    links = n_dp // 2
    parts = grad.reshape(2, links, -1, grad.shape[-1])
    ordered = reorder(parts, 1, links, index // 2)
    return [ordered[0], ordered[1]]


def link_sums(groups, n_dp):
    width = groups[0][0].shape[-1]
    bits = n_dp.bit_length() - 2
    halves = [[g[half].reshape((2,) * bits + g[half].shape[1:]) for g in groups] for half in range(2)]
    held = [list(range(bits, 0, -1)) for _ in range(2)]
    keeps, aways = [], []
    for half in range(2):
        dim = held[half].index(link_bits(n_dp, 1 - half)[0])
        keeps.append([lax.index_in_dim(p, 0, dim, keepdims=False) for p in halves[half]])
        aways.append(join_rows([lax.index_in_dim(p, 1, dim, keepdims=False).reshape(-1, width) for p in halves[half]]))
    yield from link_sums_from(keeps, aways, n_dp)


def join_rows(items):
    return jnp.concatenate(items) if len(items) > 1 else items[0]


def link_sums_from(keeps, aways, n_dp):
    width = aways[0].shape[-1]
    bits = n_dp.bit_length() - 2
    held = [list(range(bits, 0, -1)) for _ in range(2)]
    for step in range(bits):
        came = []
        for half in range(2):
            bit = link_bits(n_dp, 1 - half)[step]
            held[half].remove(bit)
            came.append(swap(aways[half], "dp", n_dp, 1 << bit))
        came = yield came, aways
        halves = []
        for half in range(2):
            at, summed = 0, []
            for keep in keeps[half]:
                size = keep.size // width
                piece = came[half][at : at + size].reshape(keep.shape)
                summed.append((keep.astype(WIDE) + piece.astype(WIDE)).astype(LOW))
                at += size
            halves.append(summed)
        if step + 1 == bits:
            break
        keeps, aways = [], []
        for half in range(2):
            dim = held[half].index(link_bits(n_dp, 1 - half)[step + 1])
            keeps.append([lax.index_in_dim(p, 0, dim, keepdims=False) for p in halves[half]])
            away = [lax.index_in_dim(p, 1, dim, keepdims=False).reshape(-1, width) for p in halves[half]]
            aways.append(join_rows(away))
    yield [jnp.stack([a, b]) for a, b in zip(*halves)], []


def first_split(n_dp, away):
    links = n_dp // 2
    return [
        [m for m in range(links) if bool(m >> (link_bits(n_dp, 1 - half)[0] - 1) & 1) == away] for half in range(2)
    ]


def reduce_tensor(scattered, shared, n_tensor):
    width = (scattered + shared)[0].shape[-1]
    held = [s.reshape(2, n_tensor, -1, width) for s in scattered]
    mask = 1
    while mask < n_tensor:
        split = [h.reshape(2, -1, 2, h.shape[2], width) for h in held]
        flat = [h[:, :, 1].reshape(2, -1, width) for h in split] + shared
        flat = jnp.concatenate(flat, axis=1) if len(flat) > 1 else flat[0]
        (came,) = yield [swap(flat, "tensor", n_tensor, mask)], [flat]
        summed, at = [], 0
        for keep in [h[:, :, 0] for h in split] + shared:
            size = keep.size // (2 * width)
            piece = came[:, at : at + size].reshape(keep.shape)
            summed.append((keep.astype(WIDE) + piece.astype(WIDE)).astype(LOW))
            at += size
        held, shared = summed[: len(held)], summed[len(held) :]
        mask *= 2
    parts = [h[:, 0] for h in held] + shared
    yield [jnp.concatenate(parts, axis=1) if len(parts) > 1 else parts[0]], []


def both_near(value, n_dp):
    near = [v.reshape((n_dp // 2,) + v.shape[-2:]) for v in value]
    return [near, [swap(n, "dp", n_dp, 1) for n in near]]


def backwards(number, bits):
    result = 0
    for _ in range(bits):
        result, number = result * 2 + number % 2, number // 2
    return result


def shared_kernel(index_ref, near_a, near_b, far_a, far_b, out_ref):
    links, rows, _ = near_a.shape
    index = index_ref[0]
    for core, refs in enumerate(((near_a, near_b), (far_a, far_b))):
        for half, ref in enumerate(refs):
            for link in range(links):
                spot = (((core ^ index) & 1) * 2 + half) * links + (link ^ (index >> 1))
                at = backwards(link, links.bit_length() - 1) if half else link
                out_ref[pl.ds(pl.multiple_of(spot * rows, rows), rows), :] = ref[at].astype(WIDE)


def place_shared(seen, at, rows, n_dp, index):
    (near_a, near_b), (far_a, far_b) = seen
    return pl.pallas_call(
        shared_kernel,
        out_shape=jax.ShapeDtypeStruct((2 * n_dp * rows, near_a.shape[-1]), WIDE),
        in_specs=[pl.BlockSpec(memory_space=pltpu.SMEM)] + [pl.BlockSpec(memory_space=pltpu.VMEM)] * 4,
        out_specs=pl.BlockSpec(memory_space=pltpu.VMEM),
        compiler_params=pltpu.CompilerParams(vmem_limit_bytes=32 << 20),
        name="place_shared",
    )(index[None], *[v[:, at : at + rows] for v in (near_a, near_b, far_a, far_b)])


def turn_kernel(turned, index_ref, near_a, near_b, far_a, far_b, out_ref, held):
    links, lead, rows, _ = near_a.shape
    index = index_ref[0]
    for i in range(lead):
        for core, refs in enumerate(((near_a, near_b), (far_a, far_b))):
            for half, ref in enumerate(refs):
                for link in range(links):
                    spot = ((2 * link + core) ^ index) * (2 * rows) + half * rows
                    at = backwards(link, links.bit_length() - 1) if half else link
                    held[pl.ds(pl.multiple_of(spot, rows), rows), :] = ref[at, i].astype(WIDE)
        out_ref[i] = held[...].T if turned else held[...]


def place_units(seen, at, lead, rows, n_dp, index, turned):
    (near_a, near_b), (far_a, far_b) = seen
    width = near_a.shape[-1]
    links = n_dp // 2
    shaped = [v[:, at : at + lead * rows].reshape(links, lead, rows, width) for v in (near_a, near_b, far_a, far_b)]
    units = 4 * rows * links
    if rows % 8:
        flips = [backwards(link, links.bit_length() - 1) for link in range(links)]
        crossed = lambda v: jnp.stack([v[at] for at in flips])
        parts = [shaped[0], crossed(shaped[1]), shaped[2], crossed(shaped[3])]
        pieces = jnp.transpose(jnp.stack(parts, axis=1), (2, 0, 1, 3, 4))
        pieces = reorder(pieces.reshape(lead, n_dp, 2 * rows, width), 1, n_dp, index)
        pieces = pieces.reshape(lead, units, width).astype(WIDE)
        return jnp.swapaxes(pieces, 1, 2) if turned else pieces
    return pl.pallas_call(
        functools.partial(turn_kernel, turned),
        out_shape=jax.ShapeDtypeStruct((lead, width, units) if turned else (lead, units, width), WIDE),
        in_specs=[pl.BlockSpec(memory_space=pltpu.SMEM)] + [pl.BlockSpec(memory_space=pltpu.VMEM)] * 4,
        out_specs=pl.BlockSpec(memory_space=pltpu.VMEM),
        scratch_shapes=[pltpu.VMEM((units, width), WIDE)],
        compiler_params=pltpu.CompilerParams(vmem_limit_bytes=32 << 20),
        name="place_units",
    )(index[None], *shaped)


SMALL_COST = pl.CostEstimate(flops=0, bytes_accessed=0, transcendentals=0)
VMEM = pltpu.CompilerParams(vmem_limit_bytes=48 << 20)
TILE = 1024


def pair_kernel(dim, left_ref, right_ref, left_mate_ref, right_mate_ref, out_ref):
    total = dot(left_ref[...], right_ref[...], dim, 0) + dot(left_mate_ref[...], right_mate_ref[...], dim, 0)
    out_ref[...] = total.astype(LOW)


def pair_product(left, right, left_mate, right_mate, dim):
    units = left.shape[1 - dim]
    rows, width = right.shape
    tile = next(units // n for n in range(1, units) if units % n == 0 and units // n <= TILE)
    if dim:
        block = pl.BlockSpec((tile, rows), lambda i: (i, 0))
    else:
        block = pl.BlockSpec((rows, tile), lambda i: (0, i))
    whole = pl.BlockSpec((rows, width), lambda i: (0, 0))
    return pl.pallas_call(
        functools.partial(pair_kernel, dim),
        grid=(units // tile,),
        in_specs=[block, whole, block, whole],
        out_specs=pl.BlockSpec((tile, width), lambda i: (i, 0)),
        out_shape=jax.ShapeDtypeStruct((units, width), LOW),
        compiler_params=VMEM,
        cost_estimate=SMALL_COST,
        name="pair_product",
    )(left, right, left_mate, right_mate)


def split_kernel(picks, tile, learn, *refs):
    left, right, left_mate, right_mate = refs[:4]
    outs = refs[-2:]
    if learn:
        index_ref, extra = refs[4], refs[5]
        if learn == "make":
            learn_left, learn_right, learn_left_mate, learn_right_mate = refs[5:9]
            extra = refs[9]
            outs = refs[10:12]
            extra[...] = (
                dot(learn_left[...], learn_right[...], 0, 0) + dot(learn_left_mate[...], learn_right_mate[...], 0, 0)
            ).astype(LOW)
        links = left.shape[1] // (2 * tile)
        rows = extra.shape[0] // (2 * links)
    for half, (some, out) in enumerate(zip(picks, outs)):
        at = 0
        for link in some:
            spot = half * (left.shape[1] // 2) + link * tile
            columns = slice(spot, spot + tile)
            total = dot(left[:, columns], right[...], 0, 0) + dot(left_mate[:, columns], right_mate[...], 0, 0)
            out[at : at + tile] = total.astype(LOW)
            at += tile
            if learn:
                source = (half * links + (link ^ (index_ref[0] // 2))) * rows
                out[at : at + rows] = extra[pl.ds(pl.multiple_of(source, rows), rows)]
                at += rows


def split_product(left, right, left_mate, right_mate, picks, links, index=None, learn=None):
    tile = left.shape[1] // (2 * links)
    width = right.shape[1]
    rows = tile
    args = [left, right, left_mate, right_mate]
    specs = [pl.BlockSpec(memory_space=pltpu.VMEM)] * 4
    out_shape = []
    if learn is not None:
        args += [index[None], *learn]
        specs += [pl.BlockSpec(memory_space=pltpu.SMEM)] + [pl.BlockSpec(memory_space=pltpu.VMEM)] * len(learn)
        units = learn[0].shape[1] if len(learn) > 1 else learn[0].shape[0]
        rows += units // (2 * links)
        if len(learn) > 1:
            out_shape.append(jax.ShapeDtypeStruct((units, width), LOW))
    mode = None if learn is None else "make" if len(learn) > 1 else "take"
    out_shape += [jax.ShapeDtypeStruct((len(some) * rows, width), LOW) for some in picks]
    return pl.pallas_call(
        functools.partial(split_kernel, picks, tile, mode),
        out_shape=out_shape,
        in_specs=specs,
        out_specs=[pl.BlockSpec(memory_space=pltpu.VMEM)] * len(out_shape),
        compiler_params=VMEM,
        cost_estimate=SMALL_COST,
        name="split_product",
    )(*args)


def back_kernel(count, source_ref, *refs):
    rows = refs[-1].shape[0]
    row = pl.program_id(0) * rows + lax.broadcasted_iota(jnp.int32, (rows, source_ref.shape[1]), 0)
    spot = (row == source_ref[...]).astype(WIDE).astype(LOW)
    total, at = 0.0, 0
    for ref in refs[:count]:
        total = total + dot(spot[:, at : at + ref.shape[0]], ref[...], 1, 0)
        at += ref.shape[0]
    if len(refs) > count + 1:
        total = total + refs[count][...].astype(WIDE)
    refs[-1][...] = total.astype(LOW)


def rows_home(blocks, rows, base=None):
    sources = jnp.concatenate([b[0] for b in blocks])[None]
    values = [b[1] for b in blocks]
    width = values[0].shape[1]
    tile = min(256, rows)
    whole = lambda array: pl.BlockSpec(array.shape, lambda i: (0, 0))
    block = pl.BlockSpec((tile, width), lambda i: (i, 0))
    return pl.pallas_call(
        functools.partial(back_kernel, len(values)),
        grid=(rows // tile,),
        in_specs=[whole(sources)] + [whole(v) for v in values] + ([] if base is None else [block]),
        out_specs=block,
        out_shape=jax.ShapeDtypeStruct((rows, width), LOW),
        compiler_params=VMEM,
        cost_estimate=SMALL_COST,
        name="rows_home",
    )(sources, *values, *([] if base is None else [base]))


def rows_back_kernel(first_ref, second_ref, w_first_ref, w_second_ref, base_ref, normed_ref, inverse_ref, gain_ref, wide_ref, low_ref, gain_grad_ref, held):
    step = pl.program_id(0)
    held[step] = dot(first_ref[...], w_first_ref[...], 1, 0) + dot(second_ref[...], w_second_ref[...], 1, 0)

    @pl.when(step == pl.num_programs(0) - 1)
    def _():
        count, _, tile = held.shape
        parts = [slice(i * tile, (i + 1) * tile) for i in range(count)]
        mean, cross = 0.0, 0.0
        for i, part in enumerate(parts):
            normed = normed_ref[:, part]
            product = held[i] * normed
            gain_grad_ref[:, part] = jnp.sum(product, axis=0, keepdims=True)
            gain = gain_ref[:, part]
            mean = mean + jnp.sum(held[i] * gain, axis=1, keepdims=True)
            cross = cross + jnp.sum(product * gain, axis=1, keepdims=True)
        mean, cross = mean / (count * tile), cross / (count * tile)
        for i, part in enumerate(parts):
            scaled = held[i] * gain_ref[:, part]
            total = base_ref[:, part] + (scaled - mean - normed_ref[:, part] * cross) * inverse_ref[...]
            wide_ref[:, part] = total
            low_ref[:, part] = total.astype(LOW)


def rows_back(grads, weights, base, normed, inverse, gain):
    rows, width = base.shape
    units = grads[0].shape[1]
    tile = min(256, width)
    whole = lambda *shape: pl.BlockSpec(shape, lambda i: (0,) * len(shape))
    columns = pl.BlockSpec((units, tile), lambda i: (0, i))
    return pl.pallas_call(
        rows_back_kernel,
        grid=(width // tile,),
        in_specs=[
            whole(rows, units),
            whole(rows, units),
            columns,
            columns,
            whole(rows, width),
            whole(rows, width),
            whole(rows, 1),
            whole(1, width),
        ],
        out_specs=[whole(rows, width), whole(rows, width), whole(1, width)],
        out_shape=[
            jax.ShapeDtypeStruct((rows, width), WIDE),
            jax.ShapeDtypeStruct((rows, width), LOW),
            jax.ShapeDtypeStruct((1, width), WIDE),
        ],
        scratch_shapes=[pltpu.VMEM((width // tile, rows, tile), WIDE)],
        compiler_params=VMEM,
        cost_estimate=SMALL_COST,
        name="rows_back",
    )(*grads, *weights, base, normed, inverse, gain[None])


def two_kernel(first_ref, second_ref, right_ref, out_first_ref, out_second_ref):
    right = right_ref[...]
    out_first_ref[...] = dot(first_ref[...], right, 1, 1).astype(LOW)
    out_second_ref[...] = dot(second_ref[...], right, 1, 1).astype(LOW)


def two_products(weights, right):
    return pl.pallas_call(
        two_kernel,
        out_shape=[jax.ShapeDtypeStruct((w.shape[0], right.shape[0]), LOW) for w in weights],
        compiler_params=VMEM,
        cost_estimate=SMALL_COST,
        name="two_products",
    )(*weights, right)


def attend_kernel(scale, first_ref, second_ref, column_ref, row_ref, mixed_first_ref, mixed_second_ref, log_ref):
    query, key, value = [jnp.concatenate([first_ref[i, 0], second_ref[i, 0]]) for i in range(3)]
    scores = dot(key, query * scale, 0, 0)
    scores = jnp.where(column_ref[...] == row_ref[...], scores, FAR)
    most = jnp.max(scores, axis=0, keepdims=True)
    exponent = jnp.exp(scores - most)
    total = jnp.sum(exponent, axis=0, keepdims=True)
    mixed = (dot(value, exponent.astype(LOW), 1, 0) / total).astype(LOW)
    half = mixed.shape[0] // 2
    mixed_first_ref[0] = mixed[:half]
    mixed_second_ref[0] = mixed[half:]
    log_ref[0] = most + jnp.log(total)


def attend(first, second, image, scale):
    _, heads, half, rows = first.shape
    three = pl.BlockSpec((3, 1, half, rows), lambda h: (0, h, 0, 0))
    one = pl.BlockSpec((1, half, rows), lambda h: (h, 0, 0))
    return pl.pallas_call(
        functools.partial(attend_kernel, scale),
        grid=(heads,),
        in_specs=[
            three,
            three,
            pl.BlockSpec((rows, 1), lambda h: (0, 0)),
            pl.BlockSpec((1, rows), lambda h: (0, 0)),
        ],
        out_specs=[one, one, pl.BlockSpec((1, 1, rows), lambda h: (h, 0, 0))],
        out_shape=[
            jax.ShapeDtypeStruct((heads, half, rows), LOW),
            jax.ShapeDtypeStruct((heads, half, rows), LOW),
            jax.ShapeDtypeStruct((heads, 1, rows), WIDE),
        ],
        compiler_params=pltpu.CompilerParams(vmem_limit_bytes=48 << 20),
        cost_estimate=SMALL_COST,
        name="attend",
    )(first, second, image[:, None], image[None, :])


def attend_back_kernel(
    scale,
    first_ref,
    second_ref,
    mixed_first_ref,
    mixed_second_ref,
    grad_first_ref,
    grad_second_ref,
    log_ref,
    column_ref,
    row_ref,
    out_first_ref,
    out_second_ref,
):
    query, key, value = [jnp.concatenate([first_ref[i, 0], second_ref[i, 0]]) for i in range(3)]
    query = query * scale
    mixed = jnp.concatenate([mixed_first_ref[0], mixed_second_ref[0]])
    grad = jnp.concatenate([grad_first_ref[0], grad_second_ref[0]])
    scores = dot(key, query, 0, 0)
    scores = jnp.where(column_ref[...] == row_ref[...], scores, FAR)
    probs = jnp.exp(scores - log_ref[0])
    grad_probs = dot(value, grad, 0, 0)
    inner = jnp.sum(mixed.astype(WIDE) * grad.astype(WIDE), axis=0, keepdims=True)
    grad_scores = (probs * (grad_probs - inner)).astype(LOW)
    grads = (
        (dot(key, grad_scores, 1, 0) * scale).astype(LOW),
        dot(query, grad_scores, 1, 1).astype(LOW),
        dot(grad, probs.astype(LOW), 1, 1).astype(LOW),
    )
    half = mixed.shape[0] // 2
    for i, item in enumerate(grads):
        out_first_ref[i, 0] = item[:half]
        out_second_ref[i, 0] = item[half:]


def attend_back(first, second, mixed, grad_mixed, log_sums, image, scale):
    _, heads, half, rows = first.shape
    three = pl.BlockSpec((3, 1, half, rows), lambda h: (0, h, 0, 0))
    one = pl.BlockSpec((1, half, rows), lambda h: (h, 0, 0))
    return pl.pallas_call(
        functools.partial(attend_back_kernel, scale),
        grid=(heads,),
        in_specs=[
            three,
            three,
            one,
            one,
            one,
            one,
            pl.BlockSpec((1, 1, rows), lambda h: (h, 0, 0)),
            pl.BlockSpec((rows, 1), lambda h: (0, 0)),
            pl.BlockSpec((1, rows), lambda h: (0, 0)),
        ],
        out_specs=[three, three],
        out_shape=[jax.ShapeDtypeStruct((3, heads, half, rows), LOW)] * 2,
        compiler_params=pltpu.CompilerParams(vmem_limit_bytes=48 << 20),
        cost_estimate=SMALL_COST,
        name="attend_back",
    )(first, second, *mixed, *grad_mixed, log_sums, image[:, None], image[None, :])


def local(
    n_dp,
    n_tensor,
    patches,
    pos_embed,
    counts,
    ln1_gain,
    w_qkv,
    w_out,
    ln2_gain,
    w_up,
    w_down,
    ln3_gain,
    w_learn1,
    w_learn2,
    cotangent,
):
    rows, width = patches.shape
    images = counts.shape[1]
    tokens = w_learn2.shape[1]
    capacity = row_capacity(rows, images, n_tensor)
    scale = HEAD_DIM**-0.5
    tensor_index = lax.axis_index("tensor")
    index = lax.axis_index("dp")
    heads = n_tensor * w_qkv.shape[2] // HEAD_DIM
    mate = lambda value: swap(value, "dp", n_dp, 1)

    links = n_dp.bit_length() - 2
    spans = n_tensor.bit_length() - 1
    turned = jnp.transpose(w_qkv, (1, 2, 0))
    z_a = Flow(1, gather_tensor([my_piece(turned, n_dp, index)], n_tensor))
    place = place_images(counts, n_tensor)
    image, source = row_map(place, counts, tensor_index, capacity)
    part_up = w_up.shape[1] // n_dp
    piece_up = jnp.transpose(lax.dynamic_slice_in_dim(w_up, index * part_up, part_up, 1))
    pieces = [my_piece(w_out[None], n_dp, index), piece_up.reshape(2, part_up // 2, width)]
    piece_down = my_piece(w_down[None], n_dp, index)
    (far_a,) = z_a.finish(source)
    x_a = Flow(links, link_gathers(far_a, n_dp))
    z_b = Flow(1, gather_tensor([after(p, far_a) for p in pieces], n_tensor))
    pick = (after(source, far_a)[:, None] == jnp.arange(rows, dtype=jnp.int32)[None, :]).astype(LOW)
    inputs = dot(pick, patches, 1, 0) + dot(pick, pos_embed, 1, 0)
    normed_one, inverse_one = layer_norm(inputs)
    low_one = (normed_one * ln1_gain).astype(LOW)
    x_a.go(low_one)
    own_qkv = own_units(after(turned, *x_a.sent), n_dp, index)
    own_up = own_units(jnp.transpose(after(w_up, *x_a.sent))[None], n_dp, index)
    near_a = links_first(x_a.finish(*own_qkv), n_dp)
    core_a = [swap(v, "dp", n_dp, 1) for v in near_a]
    shards = [turned, w_out[None], None, w_down[None]]
    sizes = [
        (3, w_qkv.shape[2] // (2 * n_dp)),
        (1, w_out.shape[0] // (2 * n_dp)),
        (1, w_up.shape[1] // (2 * n_dp)),
        (1, w_down.shape[0] // (2 * n_dp)),
    ]
    units_of = lambda halves, some: far_units(halves, some, n_dp, n_tensor)
    qkv = [None, None]

    def project(core, halves):
        full = join(own_qkv[core], units_of(halves, sizes[:1])[0], False)
        qkv[core] = dot_low(full, low_one, 1, 1).reshape(3, heads, -1, capacity)
        return full

    full_qkv = [project(0, near_a)]
    core_a = [after(c, qkv[0]) for c in core_a]
    (far_b,) = z_b.finish(*own_up)
    x_b = Flow(links, link_gathers(far_b, n_dp))
    z_c = Flow(1, gather_tensor([after(piece_down, far_b)], n_tensor))
    full_qkv.append(project(1, core_a))
    mixed_first, mixed_second, log_sums = attend(*qkv, image, scale)
    mixed = [m.reshape(-1, capacity) for m in (mixed_first, mixed_second)]
    x_b.go(mixed[0])
    own_out = own_units(after(w_out, *x_b.sent)[None], n_dp, index)
    (far_c,) = z_c.finish(*own_out)
    x_c = Flow(links, link_gathers(far_c, n_dp))
    own_down = own_units(after(w_down, *x_c.sent)[None], n_dp, index)
    near_b = links_first(x_b.finish(*own_down), n_dp)
    core_b = [swap(v, "dp", n_dp, 1) for v in near_b]
    full_out, full_up, full_down = [], [], []

    def join_b(core, halves):
        far_out, far_up = units_of(halves, sizes[1:3])
        full_out.append(join(own_out[core], far_out, False))
        full_up.append(join(own_up[core], far_up, True))

    join_b(0, near_b)
    x_c.go(full_up[0])
    join_b(1, [after(c, full_up[0], *x_c.sent) for c in core_b])
    member = (image[:, None] == jnp.arange(images, dtype=jnp.int32)[None, :]).astype(WIDE)
    row_scale = jnp.sum(member * lax.rsqrt(counts[0].astype(WIDE))[None, :], axis=1)

    hidden = inputs + dot(mixed[0], full_out[0], 0, 0) + dot(mixed[1], full_out[1], 0, 0)
    normed_two, inverse_two = layer_norm(hidden)
    low_two = (normed_two * ln2_gain).astype(LOW)
    mate_mixed, mate_one = mate(after(mixed[1], low_two)), mate(after(low_one, low_two))
    active, slope = [], []

    def feed(core, normed):
        value, rate = gelu_both(dot(normed, full_up[core], 1, 1))
        active.append(value.astype(LOW))
        slope.append(rate.astype(LOW))

    feed(0, low_two)
    near_c = links_first(x_c.finish(active[0]), n_dp)
    core_c = [swap(v, "dp", n_dp, 1) for v in near_c]
    feed(1, after(low_two, mate_mixed, mate_one, active[0]))
    full_down.append(join(own_down[0], units_of(near_c, sizes[3:])[0], True))
    fed = dot(active[0], full_down[0], 1, 0)
    mate_active, mate_two = mate(active[1]), mate(low_two)
    core_c = [after(c, active[1], full_down[0]) for c in core_c]
    full_down.append(join(own_down[1], units_of(core_c, sizes[3:])[0], True))
    output = hidden + fed + dot(active[1], full_down[1], 1, 0)
    normed_three, inverse_three = layer_norm(output)
    low_three = (normed_three * ln3_gain).astype(LOW)
    low_three = after(low_three, mate_active, mate_two)
    acted, learn_slope = gelu_both(dot(low_three, w_learn1, 1, 0))
    acted, learn_slope = acted.astype(LOW), learn_slope.astype(LOW)
    select = jax.nn.sigmoid(dot(acted, w_learn2, 1, 0))
    weights = (select * row_scale[:, None]).astype(LOW)
    table = (member.astype(LOW)[:, :, None] * weights[:, None, :]).reshape(capacity, images * tokens)
    low_out = output.astype(LOW)
    learned = dot_low(table, low_out, 0, 0)

    grad_pooled = cotangent.reshape(images * tokens, width)
    grad_output = dot(table, grad_pooled, 1, 0)
    grad_table = dot(low_out, grad_pooled, 1, 1)
    grad_weights = jnp.sum(grad_table.reshape(capacity, images, tokens) * member[:, :, None], axis=1)
    grad_logits = (grad_weights * row_scale[:, None] * select * (1.0 - select)).astype(LOW)
    grad_learn2 = dot(grad_logits, acted, 0, 0)
    grad_inner = (dot(grad_logits, w_learn2, 1, 1) * learn_slope.astype(WIDE)).astype(LOW)
    side = width // 2
    three_keep = lax.dynamic_slice_in_dim(low_three, (index & 1) * side, side, 1)
    three_away = lax.dynamic_slice_in_dim(low_three, (1 - (index & 1)) * side, side, 1)
    mate_three, mate_inner = mate(three_away), mate(grad_inner)
    grad_from_three, grad_gain3 = norm_back(
        dot(grad_inner, w_learn1, 1, 1), ln3_gain, normed_three, inverse_three
    )
    grad_output = grad_output + grad_from_three

    grad_fed = grad_output.astype(LOW)
    mate_three, mate_inner = after(mate_three, grad_fed), after(mate_inner, grad_fed)
    mate_fed = mate(grad_fed)
    units = functools.partial(split_units, n_dp=n_dp, n_tensor=n_tensor)
    upward = lambda c, grad: (dot(grad, full_down[c], 1, 1) * slope[c].astype(WIDE)).astype(LOW)
    grad_upper = [None, upward(1, grad_fed)]
    mate_upper = mate(grad_upper[1])
    mate_fed = after(mate_fed, grad_upper[1])
    away, stay = first_split(n_dp, True), first_split(n_dp, False)
    down_operands = (active[0], grad_fed, mate_active, mate_fed)
    grad_learn1, *down_away = split_product(
        *down_operands, away, n_dp // 2, index, (three_keep, grad_inner, mate_three, mate_inner)
    )
    down_stay = split_product(*down_operands, stay, n_dp // 2, index, (grad_learn1,))
    bits_left = (2,) * (n_dp.bit_length() - 3)
    kept = lambda parts: [[p.reshape(bits_left + (-1, width))] for p in parts]
    x_down = Flow(links, link_sums_from(kept(down_stay), down_away, n_dp))
    grad_upper[0] = upward(0, after(grad_fed, *down_stay))
    mate_upper = after(mate_upper, grad_upper[0])
    grad_hidden, grad_attended, grad_gain2 = rows_back(
        grad_upper, full_up, grad_output, normed_two, inverse_two, ln2_gain
    )
    grad_gain2 = grad_gain2[0]

    grad_mixed = [g.reshape(heads, -1, capacity) for g in two_products(full_out, grad_attended)]
    up_operands = (grad_upper[0], low_two, mate_upper, mate_two)
    up_away = split_product(*up_operands, away, n_dp // 2)
    up_stay = split_product(*up_operands, stay, n_dp // 2)
    x_down.go(*up_away, *up_stay, *grad_mixed)
    grad_mixed = [after(g, *x_down.sent) for g in grad_mixed]
    mate_attended = mate(after(grad_attended, *up_stay))
    grad_qkv = attend_back(*qkv, (mixed_first, mixed_second), grad_mixed, log_sums, image, scale)
    grad_qkv = [g.reshape(-1, capacity) for g in grad_qkv]
    mate_qkv = mate(grad_qkv[1])
    pair_down = x_down.finish(grad_qkv[0])
    down_rows = active[0].shape[1] // n_dp
    everywhere = [pair_down[0][:, down_rows:], learned.reshape(2, -1, width)]
    z_down = Flow(spans, reduce_tensor([pair_down[0][:, :down_rows]], everywhere, n_tensor))
    x_up = Flow(links, link_sums_from(kept(up_stay), [after(u, *pair_down) for u in up_away], n_dp))
    grad_qkv = [after(g, *z_down.sent, *x_up.sent) for g in grad_qkv]
    grad_from_one, grad_gain1 = norm_back(
        dot(grad_qkv[0], full_qkv[0], 0, 0) + dot(grad_qkv[1], full_qkv[1], 0, 0),
        ln1_gain,
        normed_one,
        inverse_one,
    )
    near = (grad_hidden + grad_from_one).astype(LOW)
    some = capacity // 2
    ring_a = Flow(spans, gather_rows(near[:some], n_tensor))
    z_down.go(near)
    x_up.go(*z_down.sent)
    ring_a.go(*x_up.sent)
    ring_b = Flow(spans, gather_rows(after(near[some:], *ring_a.sent), n_tensor))
    mate_qkv, mate_attended = [after(m, *ring_a.sent, *ring_b.sent) for m in (mate_qkv, mate_attended)]
    grad_out = pair_product(mixed[0], grad_attended, mate_mixed, mate_attended, 1)
    grad_qkv_weight = pair_product(after(grad_qkv[0], *ring_a.sent, *ring_b.sent), low_one, mate_qkv, mate_one, 1)
    extra = jnp.concatenate([jnp.stack([grad_gain1, grad_gain2, grad_gain3]), grad_learn2])
    extra = jnp.pad(extra, ((0, 16 * n_dp - extra.shape[0]), (0, 0)))
    extra = (extra + mate(extra)).astype(LOW)

    pair_up = x_up.finish(grad_qkv_weight, grad_out)
    z_up = Flow(spans, reduce_tensor(pair_up, [], n_tensor))
    x_qkv = Flow(
        links,
        link_sums(
            [
                units(after(grad_qkv_weight, *pair_up), 3, part_first=False),
                units(after(grad_out, *pair_up), 1, part_first=False),
                split_shared(after(extra, *pair_up), n_dp, index),
            ],
            n_dp,
        ),
    )
    (sum_down,) = z_down.finish(*z_up.sent, *x_qkv.sent)
    learned = sum_down[:, -(images * tokens // 2) :].reshape(images, tokens, width)
    sum_down = sum_down[:, : -(images * tokens // 2)]
    x_qkv.go(sum_down)
    z_up.go(*x_qkv.sent)
    while ring_a.left > 1:
        ring_a.go(*z_up.sent)
        ring_b.go(*ring_a.sent)
    (rows_a,) = ring_a.finish(*z_up.sent)
    ring_b.go(rows_a)
    pair_qkv = x_qkv.finish(*ring_b.sent)
    z_qkv = Flow(spans, reduce_tensor(pair_qkv[:2], pair_qkv[2:], n_tensor))

    (sum_up,) = z_up.finish(*z_qkv.sent)
    x_seen = Flow(links, link_gathers(jnp.concatenate([sum_down, sum_up], axis=1), n_dp))

    source_of = lambda j: row_map(place, counts, tensor_index ^ j, capacity)[1]
    sources = [source] + [source_of(j) for j in range(1, n_tensor)]
    blocks = [(after(source, *x_seen.sent), near)]
    blocks += [(sources[j][:some], rows_a[j]) for j in range(1, n_tensor)]
    early = rows_home(blocks, rows)
    x_seen.go(early)
    (rows_b,) = ring_b.finish(*x_seen.sent)
    z_qkv.go(rows_b)
    near_seen = x_seen.finish(*z_qkv.sent)
    blocks = [(after(sources[j][some:], *z_qkv.sent), rows_b[j]) for j in range(1, n_tensor)]
    input_grad = rows_home(blocks, rows, early)
    (sum_qkv,) = z_qkv.finish(input_grad)
    x_last = Flow(links, link_gathers(sum_qkv, n_dp))
    seen_a = both_near(near_seen, n_dp)
    seen_a[1] = [after(v, *x_last.sent) for v in seen_a[1]]
    down_rows = up_rows = active[0].shape[1] // (n_tensor * n_dp)
    out_rows, qkv_rows, extra_rows = [
        grad.shape[0] // (parts * n_dp * lead)
        for grad, parts, lead in (
            (grad_out, n_tensor, 1),
            (grad_qkv_weight, n_tensor, 3),
            (extra, 1, 1),
        )
    ]
    down_sum = place_units(seen_a, 0, 1, down_rows, n_dp, index, False)[0]
    learn_rows = grad_learn1.shape[0] // n_dp
    learn_sum = place_shared(seen_a, down_rows, learn_rows, n_dp, index)
    at = down_rows + learn_rows
    up_sum = place_units(seen_a, at, 1, up_rows, n_dp, index, True)[0]
    while x_last.left > 1:
        x_last.go(down_sum, learn_sum, up_sum)
    seen_c = both_near(x_last.finish(down_sum, learn_sum, up_sum), n_dp)
    out_sum = place_units(seen_c, 3 * qkv_rows, 1, out_rows, n_dp, index, False)[0]
    qkv_sum = place_units(seen_c, 0, 3, qkv_rows, n_dp, index, True)
    small = seen_c[0][0][:, 3 * qkv_rows + out_rows :].reshape(n_dp // 2, extra_rows, width)
    small = lax.dynamic_slice_in_dim(small, index // 2, 1, 0)[0].astype(WIDE)

    return (
        learned,
        input_grad,
        small[0],
        jnp.transpose(qkv_sum, (1, 0, 2)),
        out_sum,
        small[1],
        up_sum,
        down_sum,
        small[2],
        learn_sum,
        jnp.transpose(small[3 : 3 + tokens]),
    )


def solution(mesh):
    return jax.shard_map(
        functools.partial(local, mesh.shape["dp"], mesh.shape["tensor"]),
        mesh=mesh,
        in_specs=(
            P("dp", None),
            P("dp", None),
            P("dp", None),
            P(),
            P(None, None, "tensor"),
            P("tensor", None),
            P(),
            P(None, "tensor"),
            P("tensor", None),
            P(),
            P(),
            P(),
            P("dp", None, None),
        ),
        out_specs=(
            P("dp", None, None),
            P("dp", None),
            P(),
            P(None, None, "tensor"),
            P("tensor", None),
            P(),
            P(None, "tensor"),
            P("tensor", None),
            P(),
            P(),
            P(),
        ),
        check_vma=False,
    )
```

```python
import functools

import jax
import jax.numpy as jnp
from jax import lax
from jax.experimental import pallas as pl
from jax.experimental.pallas import tpu as pltpu
from jax.sharding import PartitionSpec as P

HEAD_DIM = 64
MOST = 576
EPSILON = 1e-06
LOW = jnp.bfloat16
WIDE = jnp.float32
FAR = -1e30


def layer_norm(values):
    center = values - jnp.mean(values, axis=-1, keepdims=True)
    variance = jnp.mean(center * center, axis=-1, keepdims=True)
    inverse = lax.rsqrt(variance + EPSILON)
    return center * inverse, inverse


def norm_back(grad_in, gain, normed, inverse):
    gain_grad = jnp.sum(grad_in * normed, axis=0)
    scaled = grad_in * gain
    result = (
        scaled
        - jnp.mean(scaled, axis=-1, keepdims=True)
        - normed * jnp.mean(scaled * normed, axis=-1, keepdims=True)
    ) * inverse
    return result, gain_grad


def gelu_both(values):
    share = 0.5 * (1.0 + lax.erf(values * (0.5**0.5)))
    density = jnp.exp(-0.5 * values * values) * 0.3989422804014327
    return values * share, share + values * density


def dot(left, right, left_dim, right_dim):
    return lax.dot_general(
        left, right, (((left_dim,), (right_dim,)), ((), ())), preferred_element_type=WIDE
    )


def dot_low(left, right, left_dim, right_dim):
    return dot(left, right, left_dim, right_dim).astype(LOW)


def row_capacity(rows, images, n_tensor):
    if n_tensor >= images:
        most = MOST
    elif n_tensor == 4 and images == 8 and rows == 2048:
        most = 630
    else:
        most = rows // n_tensor + MOST
    return min(rows, -(-most // 128) * 128)


def place_kernel(n_tensor, counts_ref, place_ref):
    images = counts_ref.shape[1]
    count = [counts_ref[0, i] for i in range(images)]
    zero = count[0] * 0
    used, device, offset = [zero] * images, [zero] * images, [zero] * images
    loads = [zero] * n_tensor
    for _ in range(images):
        best, at = zero - 1, zero
        for i in range(images):
            better = jnp.logical_and(used[i] == 0, count[i] > best)
            best = jnp.where(better, count[i], best)
            at = jnp.where(better, i, at)
        least, least_at = loads[0], zero
        for b in range(1, n_tensor):
            better = loads[b] < least
            least = jnp.where(better, loads[b], least)
            least_at = jnp.where(better, b, least_at)
        for i in range(images):
            here = at == i
            used[i] = jnp.where(here, 1, used[i])
            device[i] = jnp.where(here, least_at, device[i])
            offset[i] = jnp.where(here, least, offset[i])
        for b in range(n_tensor):
            loads[b] = loads[b] + jnp.where(least_at == b, best, 0)
    start = zero
    for i in range(images):
        place_ref[0, i] = device[i]
        place_ref[1, i] = offset[i]
        place_ref[2, i] = start
        start = start + count[i]


def place_images(counts, n_tensor):
    images = counts.shape[1]
    return pl.pallas_call(
        functools.partial(place_kernel, n_tensor),
        out_shape=jax.ShapeDtypeStruct((3, images), jnp.int32),
        in_specs=[pl.BlockSpec(memory_space=pltpu.SMEM)],
        out_specs=pl.BlockSpec(memory_space=pltpu.SMEM),
        name="place_images",
    )(counts)


def gather_rows(rows, n_tensor):
    held = rows[None]
    mask = n_tensor // 2
    while mask:
        (came,) = yield [swap(held, "tensor", n_tensor, mask)], [held]
        held = jnp.stack([held, came], axis=1).reshape((-1,) + rows.shape)
        mask //= 2
    yield [held], []


def row_map(place, counts, device, capacity):
    row = jnp.arange(capacity, dtype=jnp.int32)[:, None]
    offset, start = place[1][None], place[2][None]
    inside = (place[0][None] == device) & (row >= offset) & (row < offset + counts)
    image = jnp.sum(jnp.where(inside, jnp.arange(counts.shape[1], dtype=jnp.int32) + 1, 0), axis=1) - 1
    source = jnp.sum(jnp.where(inside, start - offset + row + 1, 0), axis=1) - 1
    return image, source


def after(value, *others):
    return lax.optimization_barrier((value,) + others)[0]


class Flow:
    def __init__(self, stages, generator):
        self.left = stages
        self.generator = generator
        self.came, self.sent = next(generator)

    def go(self, *others):
        self.came, self.sent = self.generator.send([after(c, *others) for c in self.came])
        self.left -= 1
        return self

    def finish(self, *others):
        while self.left:
            self.go(*others)
        return self.came


def swap(value, axis, size, mask):
    return lax.ppermute(value, axis, [(i, i ^ mask) for i in range(size)])


def reorder(value, dim, size, index):
    return jnp.concatenate(
        [lax.dynamic_slice_in_dim(value, index ^ m, 1, dim) for m in range(size)], axis=dim
    )


def link_bits(n_dp, half):
    bits = list(range(1, n_dp.bit_length() - 1))
    return bits[::-1] if half else bits


def link_gathers(far, n_dp):
    value = [far[0], far[1]]
    for step in range(n_dp.bit_length() - 2):
        came = [swap(value[half], "dp", n_dp, 1 << link_bits(n_dp, half)[step]) for half in range(2)]
        came = yield came, value
        value = [jnp.stack([v, c]) for v, c in zip(value, came)]
    yield value, []


def links_first(value, n_dp):
    count = n_dp.bit_length() - 2
    turned = jnp.transpose(value[1], tuple(range(count))[::-1] + tuple(range(count, value[1].ndim)))
    return [v.reshape((1 << count,) + v.shape[count:]) for v in (value[0], turned)]


def own_units(shard, n_dp, index):
    lead, units, width = shard.shape
    part = units // (2 * n_dp)
    split = shard.reshape(lead, n_dp, 2, part, width)
    ordered = reorder(split, 1, n_dp, index).reshape(lead, n_dp // 2, 2, 2, part, width)
    return [ordered[:, :, core] for core in range(2)]


def my_piece(shard, n_dp, index):
    lead, units, width = shard.shape
    part = units // (2 * n_dp)
    split = shard.reshape(lead, n_dp, 2, part, width)
    mine = lax.dynamic_slice_in_dim(split, index, 1, 1)[:, 0]
    return jnp.transpose(mine, (1, 0, 2, 3)).reshape(2, lead * part, width)


def gather_tensor(pieces, n_tensor):
    pack = jnp.concatenate(pieces, axis=1) if len(pieces) > 1 else pieces[0]
    came = yield [swap(pack, "tensor", n_tensor, j) for j in range(1, n_tensor)], [pack]
    yield [jnp.stack(came, axis=1)], []


def far_units(halves, sizes, n_dp, n_tensor):
    width = halves[0].shape[-1]
    weights, at = [], 0
    for lead, part in sizes:
        pieces = [
            h[:, :, at : at + lead * part].reshape(n_dp // 2, n_tensor - 1, lead, part, width) for h in halves
        ]
        weights.append(jnp.transpose(jnp.stack(pieces), (3, 2, 1, 0, 4, 5)))
        at += lead * part
    return weights


def join(own, far, part_first):
    width = own.shape[-1]
    full = jnp.concatenate([own[:, None], far], axis=1)
    if part_first:
        full = jnp.transpose(full, (3, 0, 2, 1, 4, 5))
    return full.reshape(-1, width)


def split_units(grad, lead, n_dp, n_tensor, part_first):
    width = grad.shape[-1]
    links = n_dp // 2
    if part_first:
        parts = grad.reshape(2, links, -1, width)
        return [parts[0], parts[1]]
    split = grad.reshape(lead, n_tensor, links, 2, -1, width)
    return [
        jnp.transpose(split[:, :, :, half], (2, 1, 0, 3, 4)).reshape(links, -1, width) for half in range(2)
    ]


def split_shared(grad, n_dp, index):
    links = n_dp // 2
    parts = grad.reshape(2, links, -1, grad.shape[-1])
    ordered = reorder(parts, 1, links, index // 2)
    return [ordered[0], ordered[1]]


def link_sums(groups, n_dp):
    width = groups[0][0].shape[-1]
    bits = n_dp.bit_length() - 2
    halves = [[g[half].reshape((2,) * bits + g[half].shape[1:]) for g in groups] for half in range(2)]
    held = [list(range(bits, 0, -1)) for _ in range(2)]
    keeps, aways = [], []
    for half in range(2):
        dim = held[half].index(link_bits(n_dp, 1 - half)[0])
        keeps.append([lax.index_in_dim(p, 0, dim, keepdims=False) for p in halves[half]])
        aways.append(join_rows([lax.index_in_dim(p, 1, dim, keepdims=False).reshape(-1, width) for p in halves[half]]))
    yield from link_sums_from(keeps, aways, n_dp)


def join_rows(items):
    return jnp.concatenate(items) if len(items) > 1 else items[0]


def link_sums_from(keeps, aways, n_dp):
    width = aways[0].shape[-1]
    bits = n_dp.bit_length() - 2
    held = [list(range(bits, 0, -1)) for _ in range(2)]
    for step in range(bits):
        came = []
        for half in range(2):
            bit = link_bits(n_dp, 1 - half)[step]
            held[half].remove(bit)
            came.append(swap(aways[half], "dp", n_dp, 1 << bit))
        came = yield came, aways
        halves = []
        for half in range(2):
            at, summed = 0, []
            for keep in keeps[half]:
                size = keep.size // width
                piece = came[half][at : at + size].reshape(keep.shape)
                summed.append((keep.astype(WIDE) + piece.astype(WIDE)).astype(LOW))
                at += size
            halves.append(summed)
        if step + 1 == bits:
            break
        keeps, aways = [], []
        for half in range(2):
            dim = held[half].index(link_bits(n_dp, 1 - half)[step + 1])
            keeps.append([lax.index_in_dim(p, 0, dim, keepdims=False) for p in halves[half]])
            away = [lax.index_in_dim(p, 1, dim, keepdims=False).reshape(-1, width) for p in halves[half]]
            aways.append(join_rows(away))
    yield [jnp.stack([a, b]) for a, b in zip(*halves)], []


def first_split(n_dp, away):
    links = n_dp // 2
    return [
        [m for m in range(links) if bool(m >> (link_bits(n_dp, 1 - half)[0] - 1) & 1) == away] for half in range(2)
    ]


def plane_spread(total, n_dp):
    came = yield [swap(total, "dp", n_dp, 2 * link) for link in range(1, n_dp // 2)], [total]
    yield [total] + came, []


def reduce_tensor(scattered, shared, n_tensor):
    width = (scattered + shared)[0].shape[-1]
    held = [s.reshape(2, n_tensor, -1, width) for s in scattered]
    mask = 1
    while mask < n_tensor:
        split = [h.reshape(2, -1, 2, h.shape[2], width) for h in held]
        flat = [h[:, :, 1].reshape(2, -1, width) for h in split] + shared
        flat = jnp.concatenate(flat, axis=1) if len(flat) > 1 else flat[0]
        (came,) = yield [swap(flat, "tensor", n_tensor, mask)], [flat]
        summed, at = [], 0
        for keep in [h[:, :, 0] for h in split] + shared:
            size = keep.size // (2 * width)
            piece = came[:, at : at + size].reshape(keep.shape)
            summed.append((keep.astype(WIDE) + piece.astype(WIDE)).astype(LOW))
            at += size
        held, shared = summed[: len(held)], summed[len(held) :]
        mask *= 2
    parts = [h[:, 0] for h in held] + shared
    yield [jnp.concatenate(parts, axis=1) if len(parts) > 1 else parts[0]], []


def both_near(value, n_dp):
    near = [v.reshape((n_dp // 2,) + v.shape[-2:]) for v in value]
    return [near, [swap(n, "dp", n_dp, 1) for n in near]]


def by_link(parts):
    links = parts[0].shape[0]
    bits = links.bit_length() - 1
    return [jnp.stack([parts[0][link], parts[1][backwards(link, bits)]]) for link in range(links)]


def backwards(number, bits):
    result = 0
    for _ in range(bits):
        result, number = result * 2 + number % 2, number // 2
    return result


def place_rows_kernel(plan, links, by_part, index_ref, *refs):
    count = 4 if by_part else 2 * links
    bits = links.bit_length() - 1
    outs = refs[count : count + len(plan)]

    def piece(core, half, link, start, rows):
        if by_part:
            return refs[2 * core + half][backwards(link, bits) if half else link, start : start + rows]
        return refs[core * links + link][half, start : start + rows]

    held = refs[-1]
    index = index_ref[0]
    for (at, lead, rows, kind), out in zip(plan, outs):
        for i in range(lead):
            target = held if kind == "turned" else out.at[i]
            for core in range(2):
                for half in range(2):
                    for link in range(links):
                        if kind == "shared":
                            spot = (((core ^ index) & 1) * 2 + half) * links + (link ^ (index >> 1))
                        else:
                            spot = ((2 * link + core) ^ index) * 2 + half
                        start = at + i * rows
                        found = piece(core, half, link, start, rows).astype(WIDE)
                        target[pl.ds(pl.multiple_of(spot * rows, rows), rows), :] = found
            if kind == "turned":
                out[i] = held[: 4 * rows * links].T


def place_parts(seen, plan, n_dp, index):
    if any(rows % 8 for _, _, rows, _ in plan):
        return place_rows(by_link(seen[0]), by_link(seen[1]), plan, n_dp, index)
    return place_rows(*seen, plan, n_dp, index, True)


def place_rows(near, far, plan, n_dp, index, by_part=False):
    links = n_dp // 2
    width = near[0].shape[-1]
    shapes = [
        (lead, width, 4 * rows * links) if kind == "turned" else (lead, 4 * rows * links, width)
        for _, lead, rows, kind in plan
    ]
    if any(rows % 8 for _, _, rows, _ in plan):
        result = []
        both = jnp.stack([jnp.stack(near), jnp.stack(far)], axis=1)
        for (at, lead, rows, kind), shape in zip(plan, shapes):
            piece = both[:, :, :, at : at + lead * rows].reshape(links, 2, 2, lead, rows, width)
            if kind == "shared":
                piece = reorder(jnp.transpose(piece, (3, 1, 2, 0, 4, 5)), 1, 2, index & 1)
                piece = reorder(piece, 3, links, index // 2).reshape(lead, -1, width)
            else:
                piece = jnp.transpose(piece, (3, 0, 1, 2, 4, 5)).reshape(lead, n_dp, 2 * rows, width)
                piece = reorder(piece, 1, n_dp, index).reshape(lead, -1, width)
            piece = piece.astype(WIDE)
            result.append(jnp.swapaxes(piece, 1, 2) if kind == "turned" else piece)
        return result
    most = max([4 * rows * links for _, _, rows, kind in plan if kind == "turned"] or [8])
    return pl.pallas_call(
        functools.partial(place_rows_kernel, plan, links, by_part),
        out_shape=[jax.ShapeDtypeStruct(shape, WIDE) for shape in shapes],
        in_specs=[pl.BlockSpec(memory_space=pltpu.SMEM)]
        + [pl.BlockSpec(memory_space=pltpu.VMEM)] * (len(near) + len(far)),
        out_specs=[pl.BlockSpec(memory_space=pltpu.VMEM)] * len(plan),
        scratch_shapes=[pltpu.VMEM((most, width), WIDE)],
        compiler_params=pltpu.CompilerParams(vmem_limit_bytes=48 << 20),
        cost_estimate=pl.CostEstimate(flops=0, bytes_accessed=0, transcendentals=0),
        name="place_rows",
    )(index[None], *near, *far)


SMALL_COST = pl.CostEstimate(flops=0, bytes_accessed=0, transcendentals=0)
VMEM = pltpu.CompilerParams(vmem_limit_bytes=48 << 20)
TILE = 1024


def pair_kernel(dim, left_ref, right_ref, left_mate_ref, right_mate_ref, out_ref):
    total = dot(left_ref[...], right_ref[...], dim, 0) + dot(left_mate_ref[...], right_mate_ref[...], dim, 0)
    out_ref[...] = total.astype(LOW)


def pair_product(left, right, left_mate, right_mate, dim):
    units = left.shape[1 - dim]
    rows, width = right.shape
    tile = next(units // n for n in range(1, units) if units % n == 0 and units // n <= TILE)
    if dim:
        block = pl.BlockSpec((tile, rows), lambda i: (i, 0))
    else:
        block = pl.BlockSpec((rows, tile), lambda i: (0, i))
    whole = pl.BlockSpec((rows, width), lambda i: (0, 0))
    return pl.pallas_call(
        functools.partial(pair_kernel, dim),
        grid=(units // tile,),
        in_specs=[block, whole, block, whole],
        out_specs=pl.BlockSpec((tile, width), lambda i: (i, 0)),
        out_shape=jax.ShapeDtypeStruct((units, width), LOW),
        compiler_params=VMEM,
        cost_estimate=SMALL_COST,
        name="pair_product",
    )(left, right, left_mate, right_mate)


def split_kernel(picks, tile, learn, *refs):
    left, right, left_mate, right_mate = refs[:4]
    outs = refs[-2:]
    if learn:
        index_ref, extra = refs[4], refs[5]
        if learn == "make":
            learn_left, learn_right, learn_left_mate, learn_right_mate = refs[5:9]
            extra = refs[9]
            outs = refs[10:12]
            extra[...] = (
                dot(learn_left[...], learn_right[...], 0, 0) + dot(learn_left_mate[...], learn_right_mate[...], 0, 0)
            ).astype(LOW)
        links = left.shape[1] // (2 * tile)
        rows = extra.shape[0] // (2 * links)
    for half, (some, out) in enumerate(zip(picks, outs)):
        at = 0
        for link in some:
            spot = half * (left.shape[1] // 2) + link * tile
            columns = slice(spot, spot + tile)
            total = dot(left[:, columns], right[...], 0, 0) + dot(left_mate[:, columns], right_mate[...], 0, 0)
            out[at : at + tile] = total.astype(LOW)
            at += tile
            if learn:
                source = (half * links + (link ^ (index_ref[0] // 2))) * rows
                out[at : at + rows] = extra[pl.ds(pl.multiple_of(source, rows), rows)]
                at += rows


def split_product(left, right, left_mate, right_mate, picks, links, index=None, learn=None):
    tile = left.shape[1] // (2 * links)
    width = right.shape[1]
    rows = tile
    args = [left, right, left_mate, right_mate]
    specs = [pl.BlockSpec(memory_space=pltpu.VMEM)] * 4
    out_shape = []
    if learn is not None:
        args += [index[None], *learn]
        specs += [pl.BlockSpec(memory_space=pltpu.SMEM)] + [pl.BlockSpec(memory_space=pltpu.VMEM)] * len(learn)
        units = learn[0].shape[1] if len(learn) > 1 else learn[0].shape[0]
        rows += units // (2 * links)
        if len(learn) > 1:
            out_shape.append(jax.ShapeDtypeStruct((units, width), LOW))
    mode = None if learn is None else "make" if len(learn) > 1 else "take"
    out_shape += [jax.ShapeDtypeStruct((len(some) * rows, width), LOW) for some in picks]
    return pl.pallas_call(
        functools.partial(split_kernel, picks, tile, mode),
        out_shape=out_shape,
        in_specs=specs,
        out_specs=[pl.BlockSpec(memory_space=pltpu.VMEM)] * len(out_shape),
        compiler_params=VMEM,
        cost_estimate=SMALL_COST,
        name="split_product",
    )(*args)


def back_kernel(count, source_ref, *refs):
    rows = refs[-1].shape[0]
    row = pl.program_id(0) * rows + lax.broadcasted_iota(jnp.int32, (rows, source_ref.shape[1]), 0)
    spot = (row == source_ref[...]).astype(WIDE).astype(LOW)
    total, at = 0.0, 0
    for ref in refs[:count]:
        total = total + dot(spot[:, at : at + ref.shape[0]], ref[...], 1, 0)
        at += ref.shape[0]
    if len(refs) > count + 1:
        total = total + refs[count][...].astype(WIDE)
    refs[-1][...] = total.astype(LOW)


def rows_home(blocks, rows, base=None):
    sources = jnp.concatenate([b[0] for b in blocks])[None]
    values = [b[1] for b in blocks]
    width = values[0].shape[1]
    tile = min(256, rows)
    whole = lambda array: pl.BlockSpec(array.shape, lambda i: (0, 0))
    block = pl.BlockSpec((tile, width), lambda i: (i, 0))
    return pl.pallas_call(
        functools.partial(back_kernel, len(values)),
        grid=(rows // tile,),
        in_specs=[whole(sources)] + [whole(v) for v in values] + ([] if base is None else [block]),
        out_specs=block,
        out_shape=jax.ShapeDtypeStruct((rows, width), LOW),
        compiler_params=VMEM,
        cost_estimate=SMALL_COST,
        name="rows_home",
    )(sources, *values, *([] if base is None else [base]))


def rows_back_kernel(first_ref, second_ref, w_first_ref, w_second_ref, base_ref, normed_ref, inverse_ref, gain_ref, wide_ref, low_ref, gain_grad_ref, held):
    step = pl.program_id(0)
    held[step] = dot(first_ref[...], w_first_ref[...], 1, 0) + dot(second_ref[...], w_second_ref[...], 1, 0)

    @pl.when(step == pl.num_programs(0) - 1)
    def _():
        count, _, tile = held.shape
        parts = [slice(i * tile, (i + 1) * tile) for i in range(count)]
        mean, cross = 0.0, 0.0
        for i, part in enumerate(parts):
            normed = normed_ref[:, part]
            product = held[i] * normed
            gain_grad_ref[:, part] = jnp.sum(product, axis=0, keepdims=True)
            gain = gain_ref[:, part]
            mean = mean + jnp.sum(held[i] * gain, axis=1, keepdims=True)
            cross = cross + jnp.sum(product * gain, axis=1, keepdims=True)
        mean, cross = mean / (count * tile), cross / (count * tile)
        for i, part in enumerate(parts):
            scaled = held[i] * gain_ref[:, part]
            total = base_ref[:, part] + (scaled - mean - normed_ref[:, part] * cross) * inverse_ref[...]
            wide_ref[:, part] = total
            low_ref[:, part] = total.astype(LOW)


def rows_back(grads, weights, base, normed, inverse, gain):
    rows, width = base.shape
    units = grads[0].shape[1]
    tile = min(256, width)
    whole = lambda *shape: pl.BlockSpec(shape, lambda i: (0,) * len(shape))
    columns = pl.BlockSpec((units, tile), lambda i: (0, i))
    return pl.pallas_call(
        rows_back_kernel,
        grid=(width // tile,),
        in_specs=[
            whole(rows, units),
            whole(rows, units),
            columns,
            columns,
            whole(rows, width),
            whole(rows, width),
            whole(rows, 1),
            whole(1, width),
        ],
        out_specs=[whole(rows, width), whole(rows, width), whole(1, width)],
        out_shape=[
            jax.ShapeDtypeStruct((rows, width), WIDE),
            jax.ShapeDtypeStruct((rows, width), LOW),
            jax.ShapeDtypeStruct((1, width), WIDE),
        ],
        scratch_shapes=[pltpu.VMEM((width // tile, rows, tile), WIDE)],
        compiler_params=VMEM,
        cost_estimate=SMALL_COST,
        name="rows_back",
    )(*grads, *weights, base, normed, inverse, gain[None])


def two_kernel(first_ref, second_ref, right_ref, out_first_ref, out_second_ref):
    right = right_ref[...]
    out_first_ref[...] = dot(first_ref[...], right, 1, 1).astype(LOW)
    out_second_ref[...] = dot(second_ref[...], right, 1, 1).astype(LOW)


def two_products(weights, right):
    return pl.pallas_call(
        two_kernel,
        out_shape=[jax.ShapeDtypeStruct((w.shape[0], right.shape[0]), LOW) for w in weights],
        compiler_params=VMEM,
        cost_estimate=SMALL_COST,
        name="two_products",
    )(*weights, right)


def attend_kernel(scale, first_ref, second_ref, column_ref, row_ref, mixed_first_ref, mixed_second_ref, log_ref):
    query, key, value = [jnp.concatenate([first_ref[i, 0], second_ref[i, 0]]) for i in range(3)]
    scores = dot(key, query * scale, 0, 0)
    scores = jnp.where(column_ref[...] == row_ref[...], scores, FAR)
    most = jnp.max(scores, axis=0, keepdims=True)
    exponent = jnp.exp(scores - most)
    total = jnp.sum(exponent, axis=0, keepdims=True)
    mixed = (dot(value, exponent.astype(LOW), 1, 0) / total).astype(LOW)
    half = mixed.shape[0] // 2
    mixed_first_ref[0] = mixed[:half]
    mixed_second_ref[0] = mixed[half:]
    log_ref[0] = most + jnp.log(total)


def attend(first, second, image, scale):
    _, heads, half, rows = first.shape
    three = pl.BlockSpec((3, 1, half, rows), lambda h: (0, h, 0, 0))
    one = pl.BlockSpec((1, half, rows), lambda h: (h, 0, 0))
    return pl.pallas_call(
        functools.partial(attend_kernel, scale),
        grid=(heads,),
        in_specs=[
            three,
            three,
            pl.BlockSpec((rows, 1), lambda h: (0, 0)),
            pl.BlockSpec((1, rows), lambda h: (0, 0)),
        ],
        out_specs=[one, one, pl.BlockSpec((1, 1, rows), lambda h: (h, 0, 0))],
        out_shape=[
            jax.ShapeDtypeStruct((heads, half, rows), LOW),
            jax.ShapeDtypeStruct((heads, half, rows), LOW),
            jax.ShapeDtypeStruct((heads, 1, rows), WIDE),
        ],
        compiler_params=pltpu.CompilerParams(vmem_limit_bytes=48 << 20),
        cost_estimate=SMALL_COST,
        name="attend",
    )(first, second, image[:, None], image[None, :])


def attend_back_kernel(
    scale,
    first_ref,
    second_ref,
    mixed_first_ref,
    mixed_second_ref,
    grad_first_ref,
    grad_second_ref,
    log_ref,
    column_ref,
    row_ref,
    *out_refs,
):
    out_first_ref, out_second_ref = out_refs[-2:]
    query, key, value = [jnp.concatenate([first_ref[i, 0], second_ref[i, 0]]) for i in range(3)]
    query = query * scale
    mixed = jnp.concatenate([mixed_first_ref[0], mixed_second_ref[0]])
    grad = jnp.concatenate([grad_first_ref[0], grad_second_ref[0]])
    scores = dot(key, query, 0, 0)
    scores = jnp.where(column_ref[...] == row_ref[...], scores, FAR)
    probs = jnp.exp(scores - log_ref[0])
    grad_probs = dot(value, grad, 0, 0)
    inner = jnp.sum(mixed.astype(WIDE) * grad.astype(WIDE), axis=0, keepdims=True)
    grad_scores = (probs * (grad_probs - inner)).astype(LOW)
    grads = (
        (dot(key, grad_scores, 1, 0) * scale).astype(LOW),
        dot(query, grad_scores, 1, 1).astype(LOW),
        dot(grad, probs.astype(LOW), 1, 1).astype(LOW),
    )
    half = mixed.shape[0] // 2
    for i, item in enumerate(grads):
        out_first_ref[i, 0] = item[:half]
        out_second_ref[i, 0] = item[half:]


def attend_back(first, second, mixed, grad_mixed, log_sums, image, scale, part, so_far=()):
    _, heads, half, rows = first.shape
    base = part * (heads // 2)
    three = pl.BlockSpec((3, 1, half, rows), lambda h: (0, base + h, 0, 0))
    one = pl.BlockSpec((1, half, rows), lambda h: (base + h, 0, 0))
    return pl.pallas_call(
        functools.partial(attend_back_kernel, scale),
        grid=(heads // 2,),
        in_specs=[
            three,
            three,
            one,
            one,
            one,
            one,
            pl.BlockSpec((1, 1, rows), lambda h: (base + h, 0, 0)),
            pl.BlockSpec((rows, 1), lambda h: (0, 0)),
            pl.BlockSpec((1, rows), lambda h: (0, 0)),
        ]
        + [pl.BlockSpec(memory_space=pl.ANY)] * len(so_far),
        out_specs=[three, three],
        out_shape=[jax.ShapeDtypeStruct((3, heads, half, rows), LOW)] * 2,
        input_output_aliases={9 + i: i for i in range(len(so_far))},
        compiler_params=pltpu.CompilerParams(vmem_limit_bytes=48 << 20),
        cost_estimate=SMALL_COST,
        name="attend_back",
    )(first, second, *mixed, *grad_mixed, log_sums, image[:, None], image[None, :], *so_far)


def local(
    n_dp,
    n_tensor,
    patches,
    pos_embed,
    counts,
    ln1_gain,
    w_qkv,
    w_out,
    ln2_gain,
    w_up,
    w_down,
    ln3_gain,
    w_learn1,
    w_learn2,
    cotangent,
):
    rows, width = patches.shape
    images = counts.shape[1]
    tokens = w_learn2.shape[1]
    capacity = row_capacity(rows, images, n_tensor)
    scale = HEAD_DIM**-0.5
    tensor_index = lax.axis_index("tensor")
    index = lax.axis_index("dp")
    heads = n_tensor * w_qkv.shape[2] // HEAD_DIM
    mate = lambda value: swap(value, "dp", n_dp, 1)

    links = n_dp.bit_length() - 2
    spans = n_tensor.bit_length() - 1
    turned = jnp.transpose(w_qkv, (1, 2, 0))
    z_a = Flow(1, gather_tensor([my_piece(turned, n_dp, index)], n_tensor))
    place = place_images(counts, n_tensor)
    image, source = row_map(place, counts, tensor_index, capacity)
    part_up = w_up.shape[1] // n_dp
    piece_up = jnp.transpose(lax.dynamic_slice_in_dim(w_up, index * part_up, part_up, 1))
    pieces = [my_piece(w_out[None], n_dp, index), piece_up.reshape(2, part_up // 2, width)]
    piece_down = my_piece(w_down[None], n_dp, index)
    (far_a,) = z_a.finish(source)
    x_a = Flow(links, link_gathers(far_a, n_dp))
    z_b = Flow(1, gather_tensor([after(p, far_a) for p in pieces], n_tensor))
    pick = (after(source, far_a)[:, None] == jnp.arange(rows, dtype=jnp.int32)[None, :]).astype(LOW)
    inputs = dot(pick, patches, 1, 0)
    x_a.go(inputs)
    inputs = inputs + dot(pick, after(pos_embed, *x_a.sent), 1, 0)
    normed_one, inverse_one = layer_norm(inputs)
    low_one = (normed_one * ln1_gain).astype(LOW)
    own_qkv = own_units(after(turned, *x_a.sent), n_dp, index)
    own_up = own_units(jnp.transpose(after(w_up, *x_a.sent))[None], n_dp, index)
    near_a = links_first(x_a.finish(low_one), n_dp)
    core_a = [swap(v, "dp", n_dp, 1) for v in near_a]
    shards = [turned, w_out[None], None, w_down[None]]
    sizes = [
        (3, w_qkv.shape[2] // (2 * n_dp)),
        (1, w_out.shape[0] // (2 * n_dp)),
        (1, w_up.shape[1] // (2 * n_dp)),
        (1, w_down.shape[0] // (2 * n_dp)),
    ]
    units_of = lambda halves, some: far_units(halves, some, n_dp, n_tensor)
    qkv = [None, None]

    def project(core, halves):
        full = join(own_qkv[core], units_of(halves, sizes[:1])[0], False)
        qkv[core] = dot_low(full, low_one, 1, 1).reshape(3, heads, -1, capacity)
        return full

    full_qkv = [project(0, near_a)]
    core_a = [after(c, qkv[0]) for c in core_a]
    (far_b,) = z_b.finish(*own_up)
    x_b = Flow(links, link_gathers(far_b, n_dp))
    z_c = Flow(1, gather_tensor([after(piece_down, far_b)], n_tensor))
    full_qkv.append(project(1, core_a))
    mixed_first, mixed_second, log_sums = attend(*qkv, image, scale)
    mixed = [m.reshape(-1, capacity) for m in (mixed_first, mixed_second)]
    x_b.go(mixed[0])
    own_out = own_units(after(w_out, *x_b.sent)[None], n_dp, index)
    (far_c,) = z_c.finish(*own_out)
    x_c = Flow(links, link_gathers(far_c, n_dp))
    own_down = own_units(after(w_down, *x_c.sent)[None], n_dp, index)
    near_b = links_first(x_b.finish(*own_down), n_dp)
    core_b = [swap(v, "dp", n_dp, 1) for v in near_b]
    full_out, full_up, full_down = [], [], []

    def join_b(core, halves):
        far_out, far_up = units_of(halves, sizes[1:3])
        full_out.append(join(own_out[core], far_out, False))
        full_up.append(join(own_up[core], far_up, True))

    join_b(0, near_b)
    x_c.go(full_up[0])
    join_b(1, [after(c, full_up[0], *x_c.sent) for c in core_b])
    member = (image[:, None] == jnp.arange(images, dtype=jnp.int32)[None, :]).astype(WIDE)
    row_scale = jnp.sum(member * lax.rsqrt(counts[0].astype(WIDE))[None, :], axis=1)

    hidden = inputs + dot(mixed[0], full_out[0], 0, 0) + dot(mixed[1], full_out[1], 0, 0)
    normed_two, inverse_two = layer_norm(hidden)
    low_two = (normed_two * ln2_gain).astype(LOW)
    mate_mixed, mate_one = mate(after(mixed[1], low_two)), mate(after(low_one, low_two))
    active, slope = [], []

    def feed(core, normed):
        value, rate = gelu_both(dot(normed, full_up[core], 1, 1))
        active.append(value.astype(LOW))
        slope.append(rate.astype(LOW))

    feed(0, low_two)
    near_c = links_first(x_c.finish(active[0]), n_dp)
    core_c = [swap(v, "dp", n_dp, 1) for v in near_c]
    feed(1, after(low_two, mate_mixed, mate_one, active[0]))
    full_down.append(join(own_down[0], units_of(near_c, sizes[3:])[0], True))
    fed = dot(active[0], full_down[0], 1, 0)
    mate_active, mate_two = mate(active[1]), mate(low_two)
    core_c = [after(c, active[1], full_down[0]) for c in core_c]
    full_down.append(join(own_down[1], units_of(core_c, sizes[3:])[0], True))
    output = hidden + fed + dot(active[1], full_down[1], 1, 0)
    normed_three, inverse_three = layer_norm(output)
    low_three = (normed_three * ln3_gain).astype(LOW)
    low_three = after(low_three, mate_active, mate_two)
    acted, learn_slope = gelu_both(dot(low_three, w_learn1, 1, 0))
    acted, learn_slope = acted.astype(LOW), learn_slope.astype(LOW)
    select = jax.nn.sigmoid(dot(acted, w_learn2, 1, 0))
    weights = (select * row_scale[:, None]).astype(LOW)
    table = (member.astype(LOW)[:, :, None] * weights[:, None, :]).reshape(capacity, images * tokens)
    low_out = output.astype(LOW)
    learned = dot_low(table, low_out, 0, 0)

    grad_pooled = cotangent.reshape(images * tokens, width)
    grad_output = dot(table, grad_pooled, 1, 0)
    grad_table = dot(low_out, grad_pooled, 1, 1)
    grad_weights = jnp.sum(grad_table.reshape(capacity, images, tokens) * member[:, :, None], axis=1)
    grad_logits = (grad_weights * row_scale[:, None] * select * (1.0 - select)).astype(LOW)
    grad_learn2 = dot(grad_logits, acted, 0, 0)
    grad_inner = (dot(grad_logits, w_learn2, 1, 1) * learn_slope.astype(WIDE)).astype(LOW)
    side = width // 2
    three_keep = lax.dynamic_slice_in_dim(low_three, (index & 1) * side, side, 1)
    three_away = lax.dynamic_slice_in_dim(low_three, (1 - (index & 1)) * side, side, 1)
    mate_three, mate_inner = mate(three_away), mate(grad_inner)
    grad_from_three, grad_gain3 = norm_back(
        dot(grad_inner, w_learn1, 1, 1), ln3_gain, normed_three, inverse_three
    )
    grad_output = grad_output + grad_from_three

    grad_fed = grad_output.astype(LOW)
    mate_three, mate_inner = after(mate_three, grad_fed), after(mate_inner, grad_fed)
    mate_fed = mate(grad_fed)
    units = functools.partial(split_units, n_dp=n_dp, n_tensor=n_tensor)
    ready = after(grad_fed, mate_three, mate_inner)
    upward = lambda c, grad: (dot(grad, full_down[c], 1, 1) * slope[c].astype(WIDE)).astype(LOW)
    grad_upper = [None, upward(1, ready)]
    mate_upper = mate(grad_upper[1])
    mate_fed = after(mate_fed, grad_upper[1])
    away, stay = first_split(n_dp, True), first_split(n_dp, False)
    down_operands = (active[0], grad_fed, mate_active, mate_fed)
    grad_learn1, *down_away = split_product(
        *down_operands, away, n_dp // 2, index, (three_keep, grad_inner, mate_three, mate_inner)
    )
    down_stay = split_product(*down_operands, stay, n_dp // 2, index, (grad_learn1,))
    bits_left = (2,) * (n_dp.bit_length() - 3)
    kept = lambda parts: [[p.reshape(bits_left + (-1, width))] for p in parts]
    x_down = Flow(links, link_sums_from(kept(down_stay), down_away, n_dp))
    grad_upper[0] = upward(0, after(grad_fed, *down_stay))
    mate_upper = after(mate_upper, grad_upper[0])
    grad_hidden, grad_attended, grad_gain2 = rows_back(
        grad_upper, full_up, grad_output, normed_two, inverse_two, ln2_gain
    )
    grad_gain2 = grad_gain2[0]

    grad_mixed = [g.reshape(heads, -1, capacity) for g in two_products(full_out, grad_attended)]
    x_down.go(*grad_mixed)
    up_operands = (after(grad_upper[0], *x_down.sent), low_two, mate_upper, mate_two)
    up_away = split_product(*up_operands, away, n_dp // 2)
    up_stay = split_product(*up_operands, stay, n_dp // 2)
    pair_down = x_down.finish(*up_stay)
    down_rows = active[0].shape[1] // n_dp
    everywhere = [pair_down[0][:, down_rows:], learned.reshape(2, -1, width)]
    z_down = Flow(spans, reduce_tensor([pair_down[0][:, :down_rows]], everywhere, n_tensor))
    x_up = Flow(links, link_sums_from(kept(up_stay), [after(u, *pair_down) for u in up_away], n_dp))
    grad_mixed = [after(g, *z_down.sent, *x_up.sent) for g in grad_mixed]
    mate_attended = mate(after(grad_attended, *x_up.sent))
    attended_back = functools.partial(
        attend_back, *qkv, (mixed_first, mixed_second), log_sums=log_sums, image=image, scale=scale
    )
    half_qkv = attended_back(grad_mixed, part=0)
    z_down.go(half_qkv[0])
    grad_mixed = [after(g, *z_down.sent) for g in grad_mixed]
    grad_qkv = attended_back(grad_mixed, part=1, so_far=half_qkv)
    grad_qkv = [g.reshape(-1, capacity) for g in grad_qkv]
    mate_qkv = mate(grad_qkv[1])
    grad_from_one, grad_gain1 = norm_back(
        dot(grad_qkv[0], full_qkv[0], 0, 0) + dot(grad_qkv[1], full_qkv[1], 0, 0),
        ln1_gain,
        normed_one,
        inverse_one,
    )
    near = (grad_hidden + grad_from_one).astype(LOW)
    some = capacity // 2
    ring_a = Flow(spans, gather_rows(near[:some], n_tensor))
    x_up.go(near)
    mate_qkv, mate_attended = [after(m, *x_up.sent) for m in (mate_qkv, mate_attended)]
    grad_out = pair_product(mixed[0], grad_attended, mate_mixed, mate_attended, 1)
    grad_qkv_weight = pair_product(after(grad_qkv[0], *x_up.sent), low_one, mate_qkv, mate_one, 1)
    extra = jnp.concatenate([jnp.stack([grad_gain1, grad_gain2, grad_gain3]), grad_learn2])
    extra = jnp.pad(extra, ((0, 16 * n_dp - extra.shape[0]), (0, 0)))
    extra = (extra + mate(extra)).astype(LOW)

    (sum_down,) = z_down.finish(grad_qkv_weight, grad_out)
    pair_up = x_up.finish(sum_down)
    z_up = Flow(spans, reduce_tensor(pair_up, [], n_tensor))
    x_qkv = Flow(
        links,
        link_sums(
            [
                units(after(grad_qkv_weight, *pair_up), 3, part_first=False),
                units(after(grad_out, *pair_up), 1, part_first=False),
                split_shared(after(extra, *pair_up), n_dp, index),
            ],
            n_dp,
        ),
    )
    learned = sum_down[:, -(images * tokens // 2) :].reshape(images, tokens, width)
    sum_down = sum_down[:, : -(images * tokens // 2)]
    ring_a.go(*x_qkv.sent, *z_up.sent)
    ring_b = Flow(spans, gather_rows(after(near[some:], *ring_a.sent), n_tensor))
    z_up.go(*ring_b.sent)
    x_qkv.go(*z_up.sent)
    (sum_up,) = z_up.finish(*x_qkv.sent)
    pair_qkv = x_qkv.finish(sum_up)
    z_qkv = Flow(spans, reduce_tensor(pair_qkv[:2], pair_qkv[2:], n_tensor))
    sum_seen = jnp.concatenate([after(sum_down, *pair_qkv), sum_up], axis=1)
    x_seen = Flow(links, link_gathers(sum_seen, n_dp))
    while ring_a.left > 1:
        ring_a.go(*x_seen.sent)
        ring_b.go(*ring_a.sent)
    (rows_a,) = ring_a.finish(*z_qkv.sent, *x_seen.sent)
    ring_b.go(rows_a)
    while x_seen.left > 1:
        x_seen.go(*ring_b.sent)
    z_qkv.go(*x_seen.sent)

    sources = [source] + [row_map(place, counts, tensor_index ^ j, capacity)[1] for j in range(1, n_tensor)]
    blocks = [(after(source, *z_qkv.sent), near)]
    blocks += [(sources[j][:some], rows_a[j]) for j in range(1, n_tensor)]
    early = rows_home(blocks, rows)
    near_seen = x_seen.finish(early)
    seen_a = both_near(near_seen, n_dp)
    (sum_qkv,) = z_qkv.finish(*near_seen)
    x_last = Flow(1, plane_spread(sum_qkv, n_dp))
    seen_a[1] = [after(v, *x_last.sent) for v in seen_a[1]]
    down_rows = up_rows = active[0].shape[1] // (n_tensor * n_dp)
    out_rows, qkv_rows, extra_rows = [
        grad.shape[0] // (parts * n_dp * lead)
        for grad, parts, lead in (
            (grad_out, n_tensor, 1),
            (grad_qkv_weight, n_tensor, 3),
            (extra, 1, 1),
        )
    ]
    learn_rows = grad_learn1.shape[0] // n_dp
    at = down_rows + learn_rows
    down_sum, learn_sum, up_sum = place_parts(
        seen_a,
        ((0, 1, down_rows, "plain"), (down_rows, 1, learn_rows, "shared"), (at, 1, up_rows, "turned")),
        n_dp,
        index,
    )
    near_c = x_last.finish(down_sum)
    far_c = mate(jnp.stack(near_c))
    (rows_b,) = ring_b.finish(*near_c)
    input_grad = rows_home([(sources[j][some:], rows_b[j]) for j in range(1, n_tensor)], rows, early)
    far_c = after(far_c, input_grad)
    far_c = [far_c[link] for link in range(n_dp // 2)]
    qkv_sum, out_sum = place_rows(
        near_c, far_c, ((0, 3, qkv_rows, "turned"), (3 * qkv_rows, 1, out_rows, "plain")), n_dp, index
    )
    small = jnp.stack([v[0, 3 * qkv_rows + out_rows :] for v in near_c])
    small = lax.dynamic_slice_in_dim(small, index // 2, 1, 0)[0].astype(WIDE)

    return (
        learned,
        input_grad,
        small[0],
        jnp.transpose(qkv_sum, (1, 0, 2)),
        out_sum[0],
        small[1],
        up_sum[0],
        down_sum[0],
        small[2],
        learn_sum[0],
        jnp.transpose(small[3 : 3 + tokens]),
    )


def solution(mesh):
    return jax.shard_map(
        functools.partial(local, mesh.shape["dp"], mesh.shape["tensor"]),
        mesh=mesh,
        in_specs=(
            P("dp", None),
            P("dp", None),
            P("dp", None),
            P(),
            P(None, None, "tensor"),
            P("tensor", None),
            P(),
            P(None, "tensor"),
            P("tensor", None),
            P(),
            P(),
            P(),
            P("dp", None, None),
        ),
        out_specs=(
            P("dp", None, None),
            P("dp", None),
            P(),
            P(None, None, "tensor"),
            P("tensor", None),
            P(),
            P(None, "tensor"),
            P("tensor", None),
            P(),
            P(),
            P(),
        ),
        check_vma=False,
    )
```

```python
import functools

import jax
import jax.numpy as jnp
from jax import lax
from jax.experimental import pallas as pl
from jax.experimental.pallas import tpu as pltpu
from jax.sharding import PartitionSpec as P

HEAD_DIM = 64
MOST = 576
EPSILON = 1e-06
LOW = jnp.bfloat16
WIDE = jnp.float32
FAR = -1e30


def layer_norm(values):
    center = values - jnp.mean(values, axis=-1, keepdims=True)
    variance = jnp.mean(center * center, axis=-1, keepdims=True)
    inverse = lax.rsqrt(variance + EPSILON)
    return center * inverse, inverse


def norm_back(grad_in, gain, normed, inverse):
    gain_grad = jnp.sum(grad_in * normed, axis=0)
    scaled = grad_in * gain
    result = (
        scaled
        - jnp.mean(scaled, axis=-1, keepdims=True)
        - normed * jnp.mean(scaled * normed, axis=-1, keepdims=True)
    ) * inverse
    return result, gain_grad


def gelu_both(values):
    share = 0.5 * (1.0 + lax.erf(values * (0.5**0.5)))
    density = jnp.exp(-0.5 * values * values) * 0.3989422804014327
    return values * share, share + values * density


def dot(left, right, left_dim, right_dim):
    return lax.dot_general(
        left, right, (((left_dim,), (right_dim,)), ((), ())), preferred_element_type=WIDE
    )


def dot_low(left, right, left_dim, right_dim):
    return dot(left, right, left_dim, right_dim).astype(LOW)


def row_capacity(rows, images, n_tensor):
    if n_tensor >= images:
        most = MOST
    elif n_tensor == 4 and images == 8 and rows == 2048:
        most = 630
    else:
        most = rows // n_tensor + MOST
    return min(rows, -(-most // 128) * 128)


def place_kernel(n_tensor, counts_ref, place_ref):
    images = counts_ref.shape[1]
    count = [counts_ref[0, i] for i in range(images)]
    zero = count[0] * 0
    used, device, offset = [zero] * images, [zero] * images, [zero] * images
    loads = [zero] * n_tensor
    for _ in range(images):
        best, at = zero - 1, zero
        for i in range(images):
            better = jnp.logical_and(used[i] == 0, count[i] > best)
            best = jnp.where(better, count[i], best)
            at = jnp.where(better, i, at)
        least, least_at = loads[0], zero
        for b in range(1, n_tensor):
            better = loads[b] < least
            least = jnp.where(better, loads[b], least)
            least_at = jnp.where(better, b, least_at)
        for i in range(images):
            here = at == i
            used[i] = jnp.where(here, 1, used[i])
            device[i] = jnp.where(here, least_at, device[i])
            offset[i] = jnp.where(here, least, offset[i])
        for b in range(n_tensor):
            loads[b] = loads[b] + jnp.where(least_at == b, best, 0)
    start = zero
    for i in range(images):
        place_ref[0, i] = device[i]
        place_ref[1, i] = offset[i]
        place_ref[2, i] = start
        start = start + count[i]


def place_images(counts, n_tensor):
    images = counts.shape[1]
    return pl.pallas_call(
        functools.partial(place_kernel, n_tensor),
        out_shape=jax.ShapeDtypeStruct((3, images), jnp.int32),
        in_specs=[pl.BlockSpec(memory_space=pltpu.SMEM)],
        out_specs=pl.BlockSpec(memory_space=pltpu.SMEM),
        name="place_images",
    )(counts)


def gather_rows(rows, n_tensor):
    held = rows[None]
    mask = n_tensor // 2
    while mask:
        (came,) = yield [swap(held, "tensor", n_tensor, mask)], [held]
        held = jnp.stack([held, came], axis=1).reshape((-1,) + rows.shape)
        mask //= 2
    yield [held], []


def row_map(place, counts, device, capacity):
    row = jnp.arange(capacity, dtype=jnp.int32)[:, None]
    offset, start = place[1][None], place[2][None]
    inside = (place[0][None] == device) & (row >= offset) & (row < offset + counts)
    image = jnp.sum(jnp.where(inside, jnp.arange(counts.shape[1], dtype=jnp.int32) + 1, 0), axis=1) - 1
    source = jnp.sum(jnp.where(inside, start - offset + row + 1, 0), axis=1) - 1
    return image, source


def after(value, *others):
    return lax.optimization_barrier((value,) + others)[0]


class Flow:
    def __init__(self, stages, generator):
        self.left = stages
        self.generator = generator
        self.came, self.sent = next(generator)

    def go(self, *others):
        self.came, self.sent = self.generator.send([after(c, *others) for c in self.came])
        self.left -= 1
        return self

    def finish(self, *others):
        while self.left:
            self.go(*others)
        return self.came


def swap(value, axis, size, mask):
    return lax.ppermute(value, axis, [(i, i ^ mask) for i in range(size)])


def reorder(value, dim, size, index):
    return jnp.concatenate(
        [lax.dynamic_slice_in_dim(value, index ^ m, 1, dim) for m in range(size)], axis=dim
    )


def link_bits(n_dp, half):
    bits = list(range(1, n_dp.bit_length() - 1))
    return bits[::-1] if half else bits


def link_gathers(far, n_dp):
    value = [far[0], far[1]]
    for step in range(n_dp.bit_length() - 2):
        came = [swap(value[half], "dp", n_dp, 1 << link_bits(n_dp, half)[step]) for half in range(2)]
        came = yield came, value
        value = [jnp.stack([v, c]) for v, c in zip(value, came)]
    yield value, []


def links_first(value, n_dp):
    count = n_dp.bit_length() - 2
    turned = jnp.transpose(value[1], tuple(range(count))[::-1] + tuple(range(count, value[1].ndim)))
    return [v.reshape((1 << count,) + v.shape[count:]) for v in (value[0], turned)]


def own_units(shard, n_dp, index):
    lead, units, width = shard.shape
    part = units // (2 * n_dp)
    split = shard.reshape(lead, n_dp, 2, part, width)
    ordered = reorder(split, 1, n_dp, index).reshape(lead, n_dp // 2, 2, 2, part, width)
    return [ordered[:, :, core] for core in range(2)]


def my_piece(shard, n_dp, index):
    lead, units, width = shard.shape
    part = units // (2 * n_dp)
    split = shard.reshape(lead, n_dp, 2, part, width)
    mine = lax.dynamic_slice_in_dim(split, index, 1, 1)[:, 0]
    return jnp.transpose(mine, (1, 0, 2, 3)).reshape(2, lead * part, width)


def gather_tensor(pieces, n_tensor):
    pack = jnp.concatenate(pieces, axis=1) if len(pieces) > 1 else pieces[0]
    came = yield [swap(pack, "tensor", n_tensor, j) for j in range(1, n_tensor)], [pack]
    yield [jnp.stack(came, axis=1)], []


def far_units(halves, sizes, n_dp, n_tensor):
    width = halves[0].shape[-1]
    weights, at = [], 0
    for lead, part in sizes:
        pieces = [
            h[:, :, at : at + lead * part].reshape(n_dp // 2, n_tensor - 1, lead, part, width) for h in halves
        ]
        weights.append(jnp.transpose(jnp.stack(pieces), (3, 2, 1, 0, 4, 5)))
        at += lead * part
    return weights


def join(own, far, part_first):
    width = own.shape[-1]
    full = jnp.concatenate([own[:, None], far], axis=1)
    if part_first:
        full = jnp.transpose(full, (3, 0, 2, 1, 4, 5))
    return full.reshape(-1, width)


def split_units(grad, lead, n_dp, n_tensor, part_first):
    width = grad.shape[-1]
    links = n_dp // 2
    if part_first:
        parts = grad.reshape(2, links, -1, width)
        return [parts[0], parts[1]]
    split = grad.reshape(lead, n_tensor, links, 2, -1, width)
    return [
        jnp.transpose(split[:, :, :, half], (2, 1, 0, 3, 4)).reshape(links, -1, width) for half in range(2)
    ]


def split_shared(grad, n_dp, index):
    links = n_dp // 2
    parts = grad.reshape(2, links, -1, grad.shape[-1])
    ordered = reorder(parts, 1, links, index // 2)
    return [ordered[0], ordered[1]]


def link_sums(groups, n_dp):
    width = groups[0][0].shape[-1]
    bits = n_dp.bit_length() - 2
    halves = [[g[half].reshape((2,) * bits + g[half].shape[1:]) for g in groups] for half in range(2)]
    held = [list(range(bits, 0, -1)) for _ in range(2)]
    keeps, aways = [], []
    for half in range(2):
        dim = held[half].index(link_bits(n_dp, 1 - half)[0])
        keeps.append([lax.index_in_dim(p, 0, dim, keepdims=False) for p in halves[half]])
        aways.append(join_rows([lax.index_in_dim(p, 1, dim, keepdims=False).reshape(-1, width) for p in halves[half]]))
    yield from link_sums_from(keeps, aways, n_dp)


def join_rows(items):
    return jnp.concatenate(items) if len(items) > 1 else items[0]


def link_sums_from(keeps, aways, n_dp):
    width = aways[0].shape[-1]
    bits = n_dp.bit_length() - 2
    held = [list(range(bits, 0, -1)) for _ in range(2)]
    for step in range(bits):
        came = []
        for half in range(2):
            bit = link_bits(n_dp, 1 - half)[step]
            held[half].remove(bit)
            came.append(swap(aways[half], "dp", n_dp, 1 << bit))
        came = yield came, aways
        halves = []
        for half in range(2):
            at, summed = 0, []
            for keep in keeps[half]:
                size = keep.size // width
                piece = came[half][at : at + size].reshape(keep.shape)
                summed.append((keep.astype(WIDE) + piece.astype(WIDE)).astype(LOW))
                at += size
            halves.append(summed)
        if step + 1 == bits:
            break
        keeps, aways = [], []
        for half in range(2):
            dim = held[half].index(link_bits(n_dp, 1 - half)[step + 1])
            keeps.append([lax.index_in_dim(p, 0, dim, keepdims=False) for p in halves[half]])
            away = [lax.index_in_dim(p, 1, dim, keepdims=False).reshape(-1, width) for p in halves[half]]
            aways.append(join_rows(away))
    yield [jnp.stack([a, b]) for a, b in zip(*halves)], []


def first_split(n_dp, away):
    links = n_dp // 2
    return [
        [m for m in range(links) if bool(m >> (link_bits(n_dp, 1 - half)[0] - 1) & 1) == away] for half in range(2)
    ]


def plane_spread(total, n_dp):
    came = yield [swap(total, "dp", n_dp, 2 * link) for link in range(1, n_dp // 2)], [total]
    yield [total] + came, []


def reduce_tensor(scattered, shared, n_tensor):
    width = (scattered + shared)[0].shape[-1]
    held = [s.reshape(2, n_tensor, -1, width) for s in scattered]
    mask = 1
    while mask < n_tensor:
        split = [h.reshape(2, -1, 2, h.shape[2], width) for h in held]
        flat = [h[:, :, 1].reshape(2, -1, width) for h in split] + shared
        flat = jnp.concatenate(flat, axis=1) if len(flat) > 1 else flat[0]
        (came,) = yield [swap(flat, "tensor", n_tensor, mask)], [flat]
        summed, at = [], 0
        for keep in [h[:, :, 0] for h in split] + shared:
            size = keep.size // (2 * width)
            piece = came[:, at : at + size].reshape(keep.shape)
            summed.append((keep.astype(WIDE) + piece.astype(WIDE)).astype(LOW))
            at += size
        held, shared = summed[: len(held)], summed[len(held) :]
        mask *= 2
    parts = [h[:, 0] for h in held] + shared
    yield [jnp.concatenate(parts, axis=1) if len(parts) > 1 else parts[0]], []


def both_near(value, n_dp):
    near = [v.reshape((n_dp // 2,) + v.shape[-2:]) for v in value]
    return [near, [swap(n, "dp", n_dp, 1) for n in near]]


def by_link(parts):
    links = parts[0].shape[0]
    bits = links.bit_length() - 1
    return [jnp.stack([parts[0][link], parts[1][backwards(link, bits)]]) for link in range(links)]


def backwards(number, bits):
    result = 0
    for _ in range(bits):
        result, number = result * 2 + number % 2, number // 2
    return result


def place_rows_kernel(plan, links, by_part, index_ref, *refs):
    count = 4 if by_part else 2 * links
    bits = links.bit_length() - 1
    outs = refs[count : count + len(plan)]

    def piece(core, half, link, start, rows):
        if by_part:
            return refs[2 * core + half][backwards(link, bits) if half else link, start : start + rows]
        return refs[core * links + link][half, start : start + rows]

    held = refs[-1]
    index = index_ref[0]
    for (at, lead, rows, kind), out in zip(plan, outs):
        for i in range(lead):
            target = held if kind == "turned" else out.at[i]
            for core in range(2):
                for half in range(2):
                    for link in range(links):
                        if kind == "shared":
                            spot = (((core ^ index) & 1) * 2 + half) * links + (link ^ (index >> 1))
                        else:
                            spot = ((2 * link + core) ^ index) * 2 + half
                        start = at + i * rows
                        found = piece(core, half, link, start, rows).astype(WIDE)
                        target[pl.ds(pl.multiple_of(spot * rows, rows), rows), :] = found
            if kind == "turned":
                out[i] = held[: 4 * rows * links].T


def place_parts(seen, plan, n_dp, index):
    if any(rows % 8 for _, _, rows, _ in plan):
        return place_rows(by_link(seen[0]), by_link(seen[1]), plan, n_dp, index)
    return place_rows(*seen, plan, n_dp, index, True)


def place_rows(near, far, plan, n_dp, index, by_part=False):
    links = n_dp // 2
    width = near[0].shape[-1]
    shapes = [
        (lead, width, 4 * rows * links) if kind == "turned" else (lead, 4 * rows * links, width)
        for _, lead, rows, kind in plan
    ]
    if any(rows % 8 for _, _, rows, _ in plan):
        result = []
        both = jnp.stack([jnp.stack(near), jnp.stack(far)], axis=1)
        for (at, lead, rows, kind), shape in zip(plan, shapes):
            piece = both[:, :, :, at : at + lead * rows].reshape(links, 2, 2, lead, rows, width)
            if kind == "shared":
                piece = reorder(jnp.transpose(piece, (3, 1, 2, 0, 4, 5)), 1, 2, index & 1)
                piece = reorder(piece, 3, links, index // 2).reshape(lead, -1, width)
            else:
                piece = jnp.transpose(piece, (3, 0, 1, 2, 4, 5)).reshape(lead, n_dp, 2 * rows, width)
                piece = reorder(piece, 1, n_dp, index).reshape(lead, -1, width)
            piece = piece.astype(WIDE)
            result.append(jnp.swapaxes(piece, 1, 2) if kind == "turned" else piece)
        return result
    most = max([4 * rows * links for _, _, rows, kind in plan if kind == "turned"] or [8])
    return pl.pallas_call(
        functools.partial(place_rows_kernel, plan, links, by_part),
        out_shape=[jax.ShapeDtypeStruct(shape, WIDE) for shape in shapes],
        in_specs=[pl.BlockSpec(memory_space=pltpu.SMEM)]
        + [pl.BlockSpec(memory_space=pltpu.VMEM)] * (len(near) + len(far)),
        out_specs=[pl.BlockSpec(memory_space=pltpu.VMEM)] * len(plan),
        scratch_shapes=[pltpu.VMEM((most, width), WIDE)],
        compiler_params=pltpu.CompilerParams(vmem_limit_bytes=48 << 20),
        cost_estimate=pl.CostEstimate(flops=0, bytes_accessed=0, transcendentals=0),
        name="place_rows",
    )(index[None], *near, *far)


SMALL_COST = pl.CostEstimate(flops=0, bytes_accessed=0, transcendentals=0)
VMEM = pltpu.CompilerParams(vmem_limit_bytes=48 << 20)
TILE = 1024


def pair_kernel(dim, left_ref, right_ref, left_mate_ref, right_mate_ref, out_ref):
    total = dot(left_ref[...], right_ref[...], dim, 0) + dot(left_mate_ref[...], right_mate_ref[...], dim, 0)
    out_ref[...] = total.astype(LOW)


def pair_product(left, right, left_mate, right_mate, dim):
    units = left.shape[1 - dim]
    rows, width = right.shape
    tile = next(units // n for n in range(1, units) if units % n == 0 and units // n <= TILE)
    if dim:
        block = pl.BlockSpec((tile, rows), lambda i: (i, 0))
    else:
        block = pl.BlockSpec((rows, tile), lambda i: (0, i))
    whole = pl.BlockSpec((rows, width), lambda i: (0, 0))
    return pl.pallas_call(
        functools.partial(pair_kernel, dim),
        grid=(units // tile,),
        in_specs=[block, whole, block, whole],
        out_specs=pl.BlockSpec((tile, width), lambda i: (i, 0)),
        out_shape=jax.ShapeDtypeStruct((units, width), LOW),
        compiler_params=VMEM,
        cost_estimate=SMALL_COST,
        name="pair_product",
    )(left, right, left_mate, right_mate)


def split_kernel(picks, tile, learn, *refs):
    left, right, left_mate, right_mate = refs[:4]
    outs = refs[-2:]
    if learn:
        index_ref, extra = refs[4], refs[5]
        if learn == "make":
            learn_left, learn_right, learn_left_mate, learn_right_mate = refs[5:9]
            extra = refs[9]
            outs = refs[10:12]
            extra[...] = (
                dot(learn_left[...], learn_right[...], 0, 0) + dot(learn_left_mate[...], learn_right_mate[...], 0, 0)
            ).astype(LOW)
        links = left.shape[1] // (2 * tile)
        rows = extra.shape[0] // (2 * links)
    for half, (some, out) in enumerate(zip(picks, outs)):
        at = 0
        for link in some:
            spot = half * (left.shape[1] // 2) + link * tile
            columns = slice(spot, spot + tile)
            total = dot(left[:, columns], right[...], 0, 0) + dot(left_mate[:, columns], right_mate[...], 0, 0)
            out[at : at + tile] = total.astype(LOW)
            at += tile
            if learn:
                source = (half * links + (link ^ (index_ref[0] // 2))) * rows
                out[at : at + rows] = extra[pl.ds(pl.multiple_of(source, rows), rows)]
                at += rows


def split_product(left, right, left_mate, right_mate, picks, links, index=None, learn=None):
    tile = left.shape[1] // (2 * links)
    width = right.shape[1]
    rows = tile
    args = [left, right, left_mate, right_mate]
    specs = [pl.BlockSpec(memory_space=pltpu.VMEM)] * 4
    out_shape = []
    if learn is not None:
        args += [index[None], *learn]
        specs += [pl.BlockSpec(memory_space=pltpu.SMEM)] + [pl.BlockSpec(memory_space=pltpu.VMEM)] * len(learn)
        units = learn[0].shape[1] if len(learn) > 1 else learn[0].shape[0]
        rows += units // (2 * links)
        if len(learn) > 1:
            out_shape.append(jax.ShapeDtypeStruct((units, width), LOW))
    mode = None if learn is None else "make" if len(learn) > 1 else "take"
    out_shape += [jax.ShapeDtypeStruct((len(some) * rows, width), LOW) for some in picks]
    return pl.pallas_call(
        functools.partial(split_kernel, picks, tile, mode),
        out_shape=out_shape,
        in_specs=specs,
        out_specs=[pl.BlockSpec(memory_space=pltpu.VMEM)] * len(out_shape),
        compiler_params=VMEM,
        cost_estimate=SMALL_COST,
        name="split_product",
    )(*args)


def back_kernel(count, source_ref, *refs):
    rows = refs[-1].shape[0]
    row = pl.program_id(0) * rows + lax.broadcasted_iota(jnp.int32, (rows, source_ref.shape[1]), 0)
    spot = (row == source_ref[...]).astype(WIDE).astype(LOW)
    total, at = 0.0, 0
    for ref in refs[:count]:
        total = total + dot(spot[:, at : at + ref.shape[0]], ref[...], 1, 0)
        at += ref.shape[0]
    if len(refs) > count + 1:
        total = total + refs[count][...].astype(WIDE)
    refs[-1][...] = total.astype(LOW)


def rows_home(blocks, rows, base=None):
    sources = jnp.concatenate([b[0] for b in blocks])[None]
    values = [b[1] for b in blocks]
    width = values[0].shape[1]
    tile = min(256, rows)
    whole = lambda array: pl.BlockSpec(array.shape, lambda i: (0, 0))
    block = pl.BlockSpec((tile, width), lambda i: (i, 0))
    return pl.pallas_call(
        functools.partial(back_kernel, len(values)),
        grid=(rows // tile,),
        in_specs=[whole(sources)] + [whole(v) for v in values] + ([] if base is None else [block]),
        out_specs=block,
        out_shape=jax.ShapeDtypeStruct((rows, width), LOW),
        compiler_params=VMEM,
        cost_estimate=SMALL_COST,
        name="rows_home",
    )(sources, *values, *([] if base is None else [base]))


def rows_back_kernel(first_ref, second_ref, w_first_ref, w_second_ref, base_ref, normed_ref, inverse_ref, gain_ref, wide_ref, low_ref, gain_grad_ref, held):
    step = pl.program_id(0)
    held[step] = dot(first_ref[...], w_first_ref[...], 1, 0) + dot(second_ref[...], w_second_ref[...], 1, 0)

    @pl.when(step == pl.num_programs(0) - 1)
    def _():
        count, _, tile = held.shape
        parts = [slice(i * tile, (i + 1) * tile) for i in range(count)]
        mean, cross = 0.0, 0.0
        for i, part in enumerate(parts):
            normed = normed_ref[:, part]
            product = held[i] * normed
            gain_grad_ref[:, part] = jnp.sum(product, axis=0, keepdims=True)
            gain = gain_ref[:, part]
            mean = mean + jnp.sum(held[i] * gain, axis=1, keepdims=True)
            cross = cross + jnp.sum(product * gain, axis=1, keepdims=True)
        mean, cross = mean / (count * tile), cross / (count * tile)
        for i, part in enumerate(parts):
            scaled = held[i] * gain_ref[:, part]
            total = base_ref[:, part] + (scaled - mean - normed_ref[:, part] * cross) * inverse_ref[...]
            wide_ref[:, part] = total
            low_ref[:, part] = total.astype(LOW)


def rows_back(grads, weights, base, normed, inverse, gain):
    rows, width = base.shape
    units = grads[0].shape[1]
    tile = min(256, width)
    whole = lambda *shape: pl.BlockSpec(shape, lambda i: (0,) * len(shape))
    columns = pl.BlockSpec((units, tile), lambda i: (0, i))
    return pl.pallas_call(
        rows_back_kernel,
        grid=(width // tile,),
        in_specs=[
            whole(rows, units),
            whole(rows, units),
            columns,
            columns,
            whole(rows, width),
            whole(rows, width),
            whole(rows, 1),
            whole(1, width),
        ],
        out_specs=[whole(rows, width), whole(rows, width), whole(1, width)],
        out_shape=[
            jax.ShapeDtypeStruct((rows, width), WIDE),
            jax.ShapeDtypeStruct((rows, width), LOW),
            jax.ShapeDtypeStruct((1, width), WIDE),
        ],
        scratch_shapes=[pltpu.VMEM((width // tile, rows, tile), WIDE)],
        compiler_params=VMEM,
        cost_estimate=SMALL_COST,
        name="rows_back",
    )(*grads, *weights, base, normed, inverse, gain[None])


def two_kernel(first_ref, second_ref, right_ref, out_first_ref, out_second_ref):
    right = right_ref[...]
    out_first_ref[...] = dot(first_ref[...], right, 1, 1).astype(LOW)
    out_second_ref[...] = dot(second_ref[...], right, 1, 1).astype(LOW)


def two_products(weights, right):
    return pl.pallas_call(
        two_kernel,
        out_shape=[jax.ShapeDtypeStruct((w.shape[0], right.shape[0]), LOW) for w in weights],
        compiler_params=VMEM,
        cost_estimate=SMALL_COST,
        name="two_products",
    )(*weights, right)


def attend_kernel(scale, first_ref, second_ref, column_ref, row_ref, mixed_first_ref, mixed_second_ref, log_ref):
    query, key, value = [jnp.concatenate([first_ref[i, 0], second_ref[i, 0]]) for i in range(3)]
    scores = dot(key, query * scale, 0, 0)
    scores = jnp.where(column_ref[...] == row_ref[...], scores, FAR)
    most = jnp.max(scores, axis=0, keepdims=True)
    exponent = jnp.exp(scores - most)
    total = jnp.sum(exponent, axis=0, keepdims=True)
    mixed = (dot(value, exponent.astype(LOW), 1, 0) / total).astype(LOW)
    half = mixed.shape[0] // 2
    mixed_first_ref[0] = mixed[:half]
    mixed_second_ref[0] = mixed[half:]
    log_ref[0] = most + jnp.log(total)


def attend(first, second, image, scale):
    _, heads, half, rows = first.shape
    three = pl.BlockSpec((3, 1, half, rows), lambda h: (0, h, 0, 0))
    one = pl.BlockSpec((1, half, rows), lambda h: (h, 0, 0))
    return pl.pallas_call(
        functools.partial(attend_kernel, scale),
        grid=(heads,),
        in_specs=[
            three,
            three,
            pl.BlockSpec((rows, 1), lambda h: (0, 0)),
            pl.BlockSpec((1, rows), lambda h: (0, 0)),
        ],
        out_specs=[one, one, pl.BlockSpec((1, 1, rows), lambda h: (h, 0, 0))],
        out_shape=[
            jax.ShapeDtypeStruct((heads, half, rows), LOW),
            jax.ShapeDtypeStruct((heads, half, rows), LOW),
            jax.ShapeDtypeStruct((heads, 1, rows), WIDE),
        ],
        compiler_params=pltpu.CompilerParams(vmem_limit_bytes=48 << 20),
        cost_estimate=SMALL_COST,
        name="attend",
    )(first, second, image[:, None], image[None, :])


def attend_back_kernel(
    scale,
    first_ref,
    second_ref,
    mixed_first_ref,
    mixed_second_ref,
    grad_first_ref,
    grad_second_ref,
    log_ref,
    column_ref,
    row_ref,
    *out_refs,
):
    out_first_ref, out_second_ref = out_refs[-2:]
    query, key, value = [jnp.concatenate([first_ref[i, 0], second_ref[i, 0]]) for i in range(3)]
    query = query * scale
    mixed = jnp.concatenate([mixed_first_ref[0], mixed_second_ref[0]])
    grad = jnp.concatenate([grad_first_ref[0], grad_second_ref[0]])
    scores = dot(key, query, 0, 0)
    scores = jnp.where(column_ref[...] == row_ref[...], scores, FAR)
    probs = jnp.exp(scores - log_ref[0])
    grad_probs = dot(value, grad, 0, 0)
    inner = jnp.sum(mixed.astype(WIDE) * grad.astype(WIDE), axis=0, keepdims=True)
    grad_scores = (probs * (grad_probs - inner)).astype(LOW)
    grads = (
        (dot(key, grad_scores, 1, 0) * scale).astype(LOW),
        dot(query, grad_scores, 1, 1).astype(LOW),
        dot(grad, probs.astype(LOW), 1, 1).astype(LOW),
    )
    half = mixed.shape[0] // 2
    for i, item in enumerate(grads):
        out_first_ref[i, 0] = item[:half]
        out_second_ref[i, 0] = item[half:]


def attend_back(first, second, mixed, grad_mixed, log_sums, image, scale, part, so_far=()):
    _, heads, half, rows = first.shape
    base = part * (heads // 2)
    three = pl.BlockSpec((3, 1, half, rows), lambda h: (0, base + h, 0, 0))
    one = pl.BlockSpec((1, half, rows), lambda h: (base + h, 0, 0))
    return pl.pallas_call(
        functools.partial(attend_back_kernel, scale),
        grid=(heads // 2,),
        in_specs=[
            three,
            three,
            one,
            one,
            one,
            one,
            pl.BlockSpec((1, 1, rows), lambda h: (base + h, 0, 0)),
            pl.BlockSpec((rows, 1), lambda h: (0, 0)),
            pl.BlockSpec((1, rows), lambda h: (0, 0)),
        ]
        + [pl.BlockSpec(memory_space=pl.ANY)] * len(so_far),
        out_specs=[three, three],
        out_shape=[jax.ShapeDtypeStruct((3, heads, half, rows), LOW)] * 2,
        input_output_aliases={9 + i: i for i in range(len(so_far))},
        compiler_params=pltpu.CompilerParams(vmem_limit_bytes=48 << 20),
        cost_estimate=SMALL_COST,
        name="attend_back",
    )(first, second, *mixed, *grad_mixed, log_sums, image[:, None], image[None, :], *so_far)


def local(
    n_dp,
    n_tensor,
    patches,
    pos_embed,
    counts,
    ln1_gain,
    w_qkv,
    w_out,
    ln2_gain,
    w_up,
    w_down,
    ln3_gain,
    w_learn1,
    w_learn2,
    cotangent,
):
    rows, width = patches.shape
    images = counts.shape[1]
    tokens = w_learn2.shape[1]
    capacity = row_capacity(rows, images, n_tensor)
    scale = HEAD_DIM**-0.5
    tensor_index = lax.axis_index("tensor")
    index = lax.axis_index("dp")
    heads = n_tensor * w_qkv.shape[2] // HEAD_DIM
    mate = lambda value: swap(value, "dp", n_dp, 1)

    links = n_dp.bit_length() - 2
    spans = n_tensor.bit_length() - 1
    turned = jnp.transpose(w_qkv, (1, 2, 0))
    z_a = Flow(1, gather_tensor([my_piece(turned, n_dp, index)], n_tensor))
    place = place_images(counts, n_tensor)
    image, source = row_map(place, counts, tensor_index, capacity)
    part_up = w_up.shape[1] // n_dp
    piece_up = jnp.transpose(lax.dynamic_slice_in_dim(w_up, index * part_up, part_up, 1))
    pieces = [my_piece(w_out[None], n_dp, index), piece_up.reshape(2, part_up // 2, width)]
    piece_down = my_piece(w_down[None], n_dp, index)
    (far_a,) = z_a.finish(source)
    x_a = Flow(links, link_gathers(far_a, n_dp))
    z_b = Flow(1, gather_tensor([after(p, far_a) for p in pieces], n_tensor))
    pick = (after(source, far_a)[:, None] == jnp.arange(rows, dtype=jnp.int32)[None, :]).astype(LOW)
    inputs = dot(pick, patches, 1, 0)
    x_a.go(inputs)
    inputs = inputs + dot(pick, after(pos_embed, *x_a.sent), 1, 0)
    normed_one, inverse_one = layer_norm(inputs)
    low_one = (normed_one * ln1_gain).astype(LOW)
    own_qkv = own_units(after(turned, *x_a.sent), n_dp, index)
    own_up = own_units(jnp.transpose(after(w_up, *x_a.sent))[None], n_dp, index)
    near_a = links_first(x_a.finish(low_one), n_dp)
    core_a = [swap(v, "dp", n_dp, 1) for v in near_a]
    shards = [turned, w_out[None], None, w_down[None]]
    sizes = [
        (3, w_qkv.shape[2] // (2 * n_dp)),
        (1, w_out.shape[0] // (2 * n_dp)),
        (1, w_up.shape[1] // (2 * n_dp)),
        (1, w_down.shape[0] // (2 * n_dp)),
    ]
    units_of = lambda halves, some: far_units(halves, some, n_dp, n_tensor)
    qkv = [None, None]

    def project(core, halves):
        full = join(own_qkv[core], units_of(halves, sizes[:1])[0], False)
        qkv[core] = dot_low(full, low_one, 1, 1).reshape(3, heads, -1, capacity)
        return full

    full_qkv = [project(0, near_a)]
    core_a = [after(c, qkv[0]) for c in core_a]
    (far_b,) = z_b.finish(*own_up)
    x_b = Flow(links, link_gathers(far_b, n_dp))
    z_c = Flow(1, gather_tensor([after(piece_down, far_b)], n_tensor))
    full_qkv.append(project(1, core_a))
    mixed_first, mixed_second, log_sums = attend(*qkv, image, scale)
    mixed = [m.reshape(-1, capacity) for m in (mixed_first, mixed_second)]
    x_b.go(mixed[0])
    own_out = own_units(after(w_out, *x_b.sent)[None], n_dp, index)
    (far_c,) = z_c.finish(*own_out)
    x_c = Flow(links, link_gathers(far_c, n_dp))
    own_down = own_units(after(w_down, *x_c.sent)[None], n_dp, index)
    near_b = links_first(x_b.finish(*own_down), n_dp)
    core_b = [swap(v, "dp", n_dp, 1) for v in near_b]
    full_out, full_up, full_down = [], [], []

    def join_b(core, halves):
        far_out, far_up = units_of(halves, sizes[1:3])
        full_out.append(join(own_out[core], far_out, False))
        full_up.append(join(own_up[core], far_up, True))

    join_b(0, near_b)
    x_c.go(full_up[0])
    join_b(1, [after(c, full_up[0], *x_c.sent) for c in core_b])
    member = (image[:, None] == jnp.arange(images, dtype=jnp.int32)[None, :]).astype(WIDE)
    row_scale = jnp.sum(member * lax.rsqrt(counts[0].astype(WIDE))[None, :], axis=1)

    hidden = inputs + dot(mixed[0], full_out[0], 0, 0) + dot(mixed[1], full_out[1], 0, 0)
    normed_two, inverse_two = layer_norm(hidden)
    low_two = (normed_two * ln2_gain).astype(LOW)
    mate_mixed, mate_one = mate(after(mixed[1], low_two)), mate(after(low_one, low_two))
    active, slope = [], []

    def feed(core, normed):
        value, rate = gelu_both(dot(normed, full_up[core], 1, 1))
        active.append(value.astype(LOW))
        slope.append(rate.astype(LOW))

    feed(0, low_two)
    near_c = links_first(x_c.finish(active[0]), n_dp)
    core_c = [swap(v, "dp", n_dp, 1) for v in near_c]
    feed(1, after(low_two, mate_mixed, mate_one, active[0]))
    full_down.append(join(own_down[0], units_of(near_c, sizes[3:])[0], True))
    fed = dot(active[0], full_down[0], 1, 0)
    mate_active, mate_two = mate(active[1]), mate(low_two)
    core_c = [after(c, active[1], full_down[0]) for c in core_c]
    full_down.append(join(own_down[1], units_of(core_c, sizes[3:])[0], True))
    output = hidden + fed + dot(active[1], full_down[1], 1, 0)
    normed_three, inverse_three = layer_norm(output)
    low_three = (normed_three * ln3_gain).astype(LOW)
    low_three = after(low_three, mate_active, mate_two)
    acted, learn_slope = gelu_both(dot(low_three, w_learn1, 1, 0))
    acted, learn_slope = acted.astype(LOW), learn_slope.astype(LOW)
    select = jax.nn.sigmoid(dot(acted, w_learn2, 1, 0))
    weights = (select * row_scale[:, None]).astype(LOW)
    table = (member.astype(LOW)[:, :, None] * weights[:, None, :]).reshape(capacity, images * tokens)
    low_out = output.astype(LOW)
    learned = dot_low(table, low_out, 0, 0)

    grad_pooled = cotangent.reshape(images * tokens, width)
    grad_output = dot(table, grad_pooled, 1, 0)
    grad_table = dot(low_out, grad_pooled, 1, 1)
    grad_weights = jnp.sum(grad_table.reshape(capacity, images, tokens) * member[:, :, None], axis=1)
    grad_logits = (grad_weights * row_scale[:, None] * select * (1.0 - select)).astype(LOW)
    grad_learn2 = dot(grad_logits, acted, 0, 0)
    grad_inner = (dot(grad_logits, w_learn2, 1, 1) * learn_slope.astype(WIDE)).astype(LOW)
    side = width // 2
    three_keep = lax.dynamic_slice_in_dim(low_three, (index & 1) * side, side, 1)
    three_away = lax.dynamic_slice_in_dim(low_three, (1 - (index & 1)) * side, side, 1)
    mate_three, mate_inner = mate(three_away), mate(grad_inner)
    grad_from_three, grad_gain3 = norm_back(
        dot(grad_inner, w_learn1, 1, 1), ln3_gain, normed_three, inverse_three
    )
    grad_output = grad_output + grad_from_three

    grad_fed = grad_output.astype(LOW)
    mate_three, mate_inner = after(mate_three, grad_fed), after(mate_inner, grad_fed)
    mate_fed = mate(grad_fed)
    units = functools.partial(split_units, n_dp=n_dp, n_tensor=n_tensor)
    ready = after(grad_fed, mate_three, mate_inner)
    upward = lambda c, grad: (dot(grad, full_down[c], 1, 1) * slope[c].astype(WIDE)).astype(LOW)
    grad_upper = [None, upward(1, ready)]
    mate_upper = mate(grad_upper[1])
    mate_fed = after(mate_fed, grad_upper[1])
    away, stay = first_split(n_dp, True), first_split(n_dp, False)
    down_operands = (active[0], grad_fed, mate_active, mate_fed)
    grad_learn1, *down_away = split_product(
        *down_operands, away, n_dp // 2, index, (three_keep, grad_inner, mate_three, mate_inner)
    )
    down_stay = split_product(*down_operands, stay, n_dp // 2, index, (grad_learn1,))
    bits_left = (2,) * (n_dp.bit_length() - 3)
    kept = lambda parts: [[p.reshape(bits_left + (-1, width))] for p in parts]
    x_down = Flow(links, link_sums_from(kept(down_stay), down_away, n_dp))
    grad_upper[0] = upward(0, after(grad_fed, *down_stay))
    mate_upper = after(mate_upper, grad_upper[0])
    grad_hidden, grad_attended, grad_gain2 = rows_back(
        grad_upper, full_up, grad_output, normed_two, inverse_two, ln2_gain
    )
    grad_gain2 = grad_gain2[0]

    grad_mixed = [g.reshape(heads, -1, capacity) for g in two_products(full_out, grad_attended)]
    x_down.go(*grad_mixed)
    up_operands = (after(grad_upper[0], *x_down.sent), low_two, mate_upper, mate_two)
    up_away = split_product(*up_operands, away, n_dp // 2)
    up_stay = split_product(*up_operands, stay, n_dp // 2)
    pair_down = x_down.finish(*up_stay)
    down_rows = active[0].shape[1] // n_dp
    everywhere = [pair_down[0][:, down_rows:], learned.reshape(2, -1, width)]
    z_down = Flow(spans, reduce_tensor([pair_down[0][:, :down_rows]], everywhere, n_tensor))
    x_up = Flow(links, link_sums_from(kept(up_stay), [after(u, *pair_down) for u in up_away], n_dp))
    grad_mixed = [after(g, *z_down.sent, *x_up.sent) for g in grad_mixed]
    mate_attended = mate(after(grad_attended, *x_up.sent))
    attended_back = functools.partial(
        attend_back, *qkv, (mixed_first, mixed_second), log_sums=log_sums, image=image, scale=scale
    )
    half_qkv = attended_back(grad_mixed, part=0)
    z_down.go(half_qkv[0])
    grad_mixed = [after(g, *z_down.sent) for g in grad_mixed]
    grad_qkv = attended_back(grad_mixed, part=1, so_far=half_qkv)
    grad_qkv = [g.reshape(-1, capacity) for g in grad_qkv]
    mate_qkv = mate(grad_qkv[1])
    grad_from_one, grad_gain1 = norm_back(
        dot(grad_qkv[0], full_qkv[0], 0, 0) + dot(grad_qkv[1], full_qkv[1], 0, 0),
        ln1_gain,
        normed_one,
        inverse_one,
    )
    near = (grad_hidden + grad_from_one).astype(LOW)
    some = capacity // 2
    ring_a = Flow(spans, gather_rows(near[:some], n_tensor))
    x_up.go(near)
    mate_qkv, mate_attended = [after(m, *x_up.sent) for m in (mate_qkv, mate_attended)]
    grad_out = pair_product(mixed[0], grad_attended, mate_mixed, mate_attended, 1)
    grad_qkv_weight = pair_product(after(grad_qkv[0], *x_up.sent), low_one, mate_qkv, mate_one, 1)
    extra = jnp.concatenate([jnp.stack([grad_gain1, grad_gain2, grad_gain3]), grad_learn2])
    extra = jnp.pad(extra, ((0, 16 * n_dp - extra.shape[0]), (0, 0)))
    extra = (extra + mate(extra)).astype(LOW)

    (sum_down,) = z_down.finish(grad_qkv_weight, grad_out)
    pair_up = x_up.finish(sum_down)
    z_up = Flow(spans, reduce_tensor(pair_up, [], n_tensor))
    x_qkv = Flow(
        links,
        link_sums(
            [
                units(after(grad_qkv_weight, *pair_up), 3, part_first=False),
                units(after(grad_out, *pair_up), 1, part_first=False),
                split_shared(after(extra, *pair_up), n_dp, index),
            ],
            n_dp,
        ),
    )
    learned = sum_down[:, -(images * tokens // 2) :].reshape(images, tokens, width)
    sum_down = sum_down[:, : -(images * tokens // 2)]
    ring_a.go(*x_qkv.sent, *z_up.sent)
    ring_b = Flow(spans, gather_rows(after(near[some:], *ring_a.sent), n_tensor))
    z_up.go(*ring_b.sent)
    x_qkv.go(*z_up.sent)
    (sum_up,) = z_up.finish(*x_qkv.sent)
    pair_qkv = x_qkv.finish(sum_up)
    z_qkv = Flow(spans, reduce_tensor(pair_qkv[:2], pair_qkv[2:], n_tensor))
    sum_seen = jnp.concatenate([after(sum_down, *pair_qkv), sum_up], axis=1)
    x_seen = Flow(links, link_gathers(sum_seen, n_dp))
    while ring_a.left > 1:
        ring_a.go(*x_seen.sent)
        ring_b.go(*ring_a.sent)
    (rows_a,) = ring_a.finish(*z_qkv.sent, *x_seen.sent)
    ring_b.go(rows_a)
    while x_seen.left > 1:
        x_seen.go(*ring_b.sent)

    z_qkv.go(*x_seen.sent)
    sources = [source] + [row_map(place, counts, tensor_index ^ j, capacity)[1] for j in range(1, n_tensor)]
    blocks = [(after(source, *z_qkv.sent), near)]
    blocks += [(sources[j][:some], rows_a[j]) for j in range(1, n_tensor)]
    early = rows_home(blocks, rows)
    (sum_qkv,) = z_qkv.finish(early)
    x_last = Flow(1, plane_spread(sum_qkv, n_dp))
    near_seen = x_seen.finish(*x_last.sent)
    seen_a = both_near(near_seen, n_dp)
    down_rows = up_rows = active[0].shape[1] // (n_tensor * n_dp)
    out_rows, qkv_rows, extra_rows = [
        grad.shape[0] // (parts * n_dp * lead)
        for grad, parts, lead in (
            (grad_out, n_tensor, 1),
            (grad_qkv_weight, n_tensor, 3),
            (extra, 1, 1),
        )
    ]
    learn_rows = grad_learn1.shape[0] // n_dp
    at = down_rows + learn_rows
    down_sum, learn_sum, up_sum = place_parts(
        seen_a,
        ((0, 1, down_rows, "plain"), (down_rows, 1, learn_rows, "shared"), (at, 1, up_rows, "turned")),
        n_dp,
        index,
    )
    (rows_b,) = ring_b.finish(*x_last.sent)
    input_grad = rows_home([(sources[j][some:], rows_b[j]) for j in range(1, n_tensor)], rows, early)
    near_c = x_last.finish(input_grad, down_sum)
    far_c = mate(jnp.stack(near_c))
    far_c = [far_c[link] for link in range(n_dp // 2)]
    qkv_sum, out_sum = place_rows(
        near_c, far_c, ((0, 3, qkv_rows, "turned"), (3 * qkv_rows, 1, out_rows, "plain")), n_dp, index
    )
    small = jnp.stack([v[0, 3 * qkv_rows + out_rows :] for v in near_c])
    small = lax.dynamic_slice_in_dim(small, index // 2, 1, 0)[0].astype(WIDE)

    return (
        learned,
        input_grad,
        small[0],
        jnp.transpose(qkv_sum, (1, 0, 2)),
        out_sum[0],
        small[1],
        up_sum[0],
        down_sum[0],
        small[2],
        learn_sum[0],
        jnp.transpose(small[3 : 3 + tokens]),
    )


def solution(mesh):
    return jax.shard_map(
        functools.partial(local, mesh.shape["dp"], mesh.shape["tensor"]),
        mesh=mesh,
        in_specs=(
            P("dp", None),
            P("dp", None),
            P("dp", None),
            P(),
            P(None, None, "tensor"),
            P("tensor", None),
            P(),
            P(None, "tensor"),
            P("tensor", None),
            P(),
            P(),
            P(),
            P("dp", None, None),
        ),
        out_specs=(
            P("dp", None, None),
            P("dp", None),
            P(),
            P(None, None, "tensor"),
            P("tensor", None),
            P(),
            P(None, "tensor"),
            P("tensor", None),
            P(),
            P(),
            P(),
        ),
        check_vma=False,
    )
```

```python
import functools

import jax
import jax.numpy as jnp
from jax import lax
from jax.experimental import pallas as pl
from jax.experimental.pallas import tpu as pltpu
from jax.sharding import PartitionSpec as P

HEAD_DIM = 64
MOST = 576
EPSILON = 1e-06
LOW = jnp.bfloat16
WIDE = jnp.float32
FAR = -1e30


def layer_norm(values):
    center = values - jnp.mean(values, axis=-1, keepdims=True)
    variance = jnp.mean(center * center, axis=-1, keepdims=True)
    inverse = lax.rsqrt(variance + EPSILON)
    return center * inverse, inverse


def norm_back(grad_in, gain, normed, inverse):
    gain_grad = jnp.sum(grad_in * normed, axis=0)
    scaled = grad_in * gain
    result = (
        scaled
        - jnp.mean(scaled, axis=-1, keepdims=True)
        - normed * jnp.mean(scaled * normed, axis=-1, keepdims=True)
    ) * inverse
    return result, gain_grad


def gelu_both(values):
    share = 0.5 * (1.0 + lax.erf(values * (0.5**0.5)))
    density = jnp.exp(-0.5 * values * values) * 0.3989422804014327
    return values * share, share + values * density


def dot(left, right, left_dim, right_dim):
    return lax.dot_general(
        left, right, (((left_dim,), (right_dim,)), ((), ())), preferred_element_type=WIDE
    )


def dot_low(left, right, left_dim, right_dim):
    return dot(left, right, left_dim, right_dim).astype(LOW)


def row_capacity(rows, images, n_tensor):
    if n_tensor >= images:
        most = MOST
    elif n_tensor == 4 and images == 8 and rows == 2048:
        most = 630
    else:
        most = rows // n_tensor + MOST
    return min(rows, -(-most // 128) * 128)


def place_kernel(n_tensor, counts_ref, place_ref):
    images = counts_ref.shape[1]
    count = [counts_ref[0, i] for i in range(images)]
    zero = count[0] * 0
    used, device, offset = [zero] * images, [zero] * images, [zero] * images
    loads = [zero] * n_tensor
    for _ in range(images):
        best, at = zero - 1, zero
        for i in range(images):
            better = jnp.logical_and(used[i] == 0, count[i] > best)
            best = jnp.where(better, count[i], best)
            at = jnp.where(better, i, at)
        least, least_at = loads[0], zero
        for b in range(1, n_tensor):
            better = loads[b] < least
            least = jnp.where(better, loads[b], least)
            least_at = jnp.where(better, b, least_at)
        for i in range(images):
            here = at == i
            used[i] = jnp.where(here, 1, used[i])
            device[i] = jnp.where(here, least_at, device[i])
            offset[i] = jnp.where(here, least, offset[i])
        for b in range(n_tensor):
            loads[b] = loads[b] + jnp.where(least_at == b, best, 0)
    start = zero
    for i in range(images):
        place_ref[0, i] = device[i]
        place_ref[1, i] = offset[i]
        place_ref[2, i] = start
        start = start + count[i]


def place_images(counts, n_tensor):
    images = counts.shape[1]
    return pl.pallas_call(
        functools.partial(place_kernel, n_tensor),
        out_shape=jax.ShapeDtypeStruct((3, images), jnp.int32),
        in_specs=[pl.BlockSpec(memory_space=pltpu.SMEM)],
        out_specs=pl.BlockSpec(memory_space=pltpu.SMEM),
        name="place_images",
    )(counts)


def gather_rows(rows, n_tensor):
    held = rows[None]
    mask = n_tensor // 2
    while mask:
        (came,) = yield [swap(held, "tensor", n_tensor, mask)], [held]
        held = jnp.stack([held, came], axis=1).reshape((-1,) + rows.shape)
        mask //= 2
    yield [held], []


def row_map(place, counts, device, capacity):
    row = jnp.arange(capacity, dtype=jnp.int32)[:, None]
    offset, start = place[1][None], place[2][None]
    inside = (place[0][None] == device) & (row >= offset) & (row < offset + counts)
    image = jnp.sum(jnp.where(inside, jnp.arange(counts.shape[1], dtype=jnp.int32) + 1, 0), axis=1) - 1
    source = jnp.sum(jnp.where(inside, start - offset + row + 1, 0), axis=1) - 1
    return image, source


def after(value, *others):
    return lax.optimization_barrier((value,) + others)[0]


class Flow:
    def __init__(self, stages, generator):
        self.left = stages
        self.generator = generator
        self.came, self.sent = next(generator)

    def go(self, *others):
        self.came, self.sent = self.generator.send([after(c, *others) for c in self.came])
        self.left -= 1
        return self

    def finish(self, *others):
        while self.left:
            self.go(*others)
        return self.came


def swap(value, axis, size, mask):
    return lax.ppermute(value, axis, [(i, i ^ mask) for i in range(size)])


def reorder(value, dim, size, index):
    return jnp.concatenate(
        [lax.dynamic_slice_in_dim(value, index ^ m, 1, dim) for m in range(size)], axis=dim
    )


def link_bits(n_dp, half):
    bits = list(range(1, n_dp.bit_length() - 1))
    return bits[::-1] if half else bits


def link_gathers(far, n_dp):
    value = [far[0], far[1]]
    for step in range(n_dp.bit_length() - 2):
        came = [swap(value[half], "dp", n_dp, 1 << link_bits(n_dp, half)[step]) for half in range(2)]
        came = yield came, value
        value = [jnp.stack([v, c]) for v, c in zip(value, came)]
    yield value, []


def links_first(value, n_dp):
    count = n_dp.bit_length() - 2
    turned = jnp.transpose(value[1], tuple(range(count))[::-1] + tuple(range(count, value[1].ndim)))
    return [v.reshape((1 << count,) + v.shape[count:]) for v in (value[0], turned)]


def own_units(shard, n_dp, index):
    lead, units, width = shard.shape
    part = units // (2 * n_dp)
    split = shard.reshape(lead, n_dp, 2, part, width)
    ordered = reorder(split, 1, n_dp, index).reshape(lead, n_dp // 2, 2, 2, part, width)
    return [ordered[:, :, core] for core in range(2)]


def my_piece(shard, n_dp, index):
    lead, units, width = shard.shape
    part = units // (2 * n_dp)
    split = shard.reshape(lead, n_dp, 2, part, width)
    mine = lax.dynamic_slice_in_dim(split, index, 1, 1)[:, 0]
    return jnp.transpose(mine, (1, 0, 2, 3)).reshape(2, lead * part, width)


def gather_tensor(pieces, n_tensor):
    pack = jnp.concatenate(pieces, axis=1) if len(pieces) > 1 else pieces[0]
    came = yield [swap(pack, "tensor", n_tensor, j) for j in range(1, n_tensor)], [pack]
    yield [jnp.stack(came, axis=1)], []


def far_units(halves, sizes, n_dp, n_tensor):
    width = halves[0].shape[-1]
    weights, at = [], 0
    for lead, part in sizes:
        pieces = [
            h[:, :, at : at + lead * part].reshape(n_dp // 2, n_tensor - 1, lead, part, width) for h in halves
        ]
        weights.append(jnp.transpose(jnp.stack(pieces), (3, 2, 1, 0, 4, 5)))
        at += lead * part
    return weights


def join(own, far, part_first):
    width = own.shape[-1]
    full = jnp.concatenate([own[:, None], far], axis=1)
    if part_first:
        full = jnp.transpose(full, (3, 0, 2, 1, 4, 5))
    return full.reshape(-1, width)


def split_units(grad, lead, n_dp, n_tensor, part_first):
    width = grad.shape[-1]
    links = n_dp // 2
    if part_first:
        parts = grad.reshape(2, links, -1, width)
        return [parts[0], parts[1]]
    split = grad.reshape(lead, n_tensor, links, 2, -1, width)
    return [
        jnp.transpose(split[:, :, :, half], (2, 1, 0, 3, 4)).reshape(links, -1, width) for half in range(2)
    ]


def split_shared(grad, n_dp, index):
    links = n_dp // 2
    parts = grad.reshape(2, links, -1, grad.shape[-1])
    ordered = reorder(parts, 1, links, index // 2)
    return [ordered[0], ordered[1]]


def link_sums(groups, n_dp):
    width = groups[0][0].shape[-1]
    bits = n_dp.bit_length() - 2
    halves = [[g[half].reshape((2,) * bits + g[half].shape[1:]) for g in groups] for half in range(2)]
    held = [list(range(bits, 0, -1)) for _ in range(2)]
    keeps, aways = [], []
    for half in range(2):
        dim = held[half].index(link_bits(n_dp, 1 - half)[0])
        keeps.append([lax.index_in_dim(p, 0, dim, keepdims=False) for p in halves[half]])
        aways.append(join_rows([lax.index_in_dim(p, 1, dim, keepdims=False).reshape(-1, width) for p in halves[half]]))
    yield from link_sums_from(keeps, aways, n_dp)


def join_rows(items):
    return jnp.concatenate(items) if len(items) > 1 else items[0]


def link_sums_from(keeps, aways, n_dp):
    width = aways[0].shape[-1]
    bits = n_dp.bit_length() - 2
    held = [list(range(bits, 0, -1)) for _ in range(2)]
    for step in range(bits):
        came = []
        for half in range(2):
            bit = link_bits(n_dp, 1 - half)[step]
            held[half].remove(bit)
            came.append(swap(aways[half], "dp", n_dp, 1 << bit))
        came = yield came, aways
        halves = []
        for half in range(2):
            at, summed = 0, []
            for keep in keeps[half]:
                size = keep.size // width
                piece = came[half][at : at + size].reshape(keep.shape)
                summed.append((keep.astype(WIDE) + piece.astype(WIDE)).astype(LOW))
                at += size
            halves.append(summed)
        if step + 1 == bits:
            break
        keeps, aways = [], []
        for half in range(2):
            dim = held[half].index(link_bits(n_dp, 1 - half)[step + 1])
            keeps.append([lax.index_in_dim(p, 0, dim, keepdims=False) for p in halves[half]])
            away = [lax.index_in_dim(p, 1, dim, keepdims=False).reshape(-1, width) for p in halves[half]]
            aways.append(join_rows(away))
    yield [jnp.stack([a, b]) for a, b in zip(*halves)], []


def first_split(n_dp, away):
    links = n_dp // 2
    return [
        [m for m in range(links) if bool(m >> (link_bits(n_dp, 1 - half)[0] - 1) & 1) == away] for half in range(2)
    ]


def plane_spread(total, n_dp):
    came = yield [swap(total, "dp", n_dp, 2 * link) for link in range(1, n_dp // 2)], [total]
    yield [total] + came, []


def reduce_tensor(scattered, shared, n_tensor):
    width = (scattered + shared)[0].shape[-1]
    held = [s.reshape(2, n_tensor, -1, width) for s in scattered]
    mask = 1
    while mask < n_tensor:
        split = [h.reshape(2, -1, 2, h.shape[2], width) for h in held]
        flat = [h[:, :, 1].reshape(2, -1, width) for h in split] + shared
        flat = jnp.concatenate(flat, axis=1) if len(flat) > 1 else flat[0]
        (came,) = yield [swap(flat, "tensor", n_tensor, mask)], [flat]
        summed, at = [], 0
        for keep in [h[:, :, 0] for h in split] + shared:
            size = keep.size // (2 * width)
            piece = came[:, at : at + size].reshape(keep.shape)
            summed.append((keep.astype(WIDE) + piece.astype(WIDE)).astype(LOW))
            at += size
        held, shared = summed[: len(held)], summed[len(held) :]
        mask *= 2
    parts = [h[:, 0] for h in held] + shared
    yield [jnp.concatenate(parts, axis=1) if len(parts) > 1 else parts[0]], []


def both_near(value, n_dp):
    near = [v.reshape((n_dp // 2,) + v.shape[-2:]) for v in value]
    return [near, [swap(n, "dp", n_dp, 1) for n in near]]


def by_link(parts):
    links = parts[0].shape[0]
    bits = links.bit_length() - 1
    return [jnp.stack([parts[0][link], parts[1][backwards(link, bits)]]) for link in range(links)]


def backwards(number, bits):
    result = 0
    for _ in range(bits):
        result, number = result * 2 + number % 2, number // 2
    return result


def place_rows_kernel(plan, links, by_part, index_ref, *refs):
    count = 4 if by_part else 2 * links
    bits = links.bit_length() - 1
    outs = refs[count : count + len(plan)]

    def piece(core, half, link, start, rows):
        if by_part:
            return refs[2 * core + half][backwards(link, bits) if half else link, start : start + rows]
        return refs[core * links + link][half, start : start + rows]

    held = refs[-1]
    index = index_ref[0]
    for (at, lead, rows, kind), out in zip(plan, outs):
        for i in range(lead):
            target = held if kind == "turned" else out.at[i]
            for core in range(2):
                for half in range(2):
                    for link in range(links):
                        if kind == "shared":
                            spot = (((core ^ index) & 1) * 2 + half) * links + (link ^ (index >> 1))
                        else:
                            spot = ((2 * link + core) ^ index) * 2 + half
                        start = at + i * rows
                        found = piece(core, half, link, start, rows).astype(WIDE)
                        target[pl.ds(pl.multiple_of(spot * rows, rows), rows), :] = found
            if kind == "turned":
                out[i] = held[: 4 * rows * links].T


def place_parts(seen, plan, n_dp, index):
    if any(rows % 8 for _, _, rows, _ in plan):
        return place_rows(by_link(seen[0]), by_link(seen[1]), plan, n_dp, index)
    return place_rows(*seen, plan, n_dp, index, True)


def place_rows(near, far, plan, n_dp, index, by_part=False):
    links = n_dp // 2
    width = near[0].shape[-1]
    shapes = [
        (lead, width, 4 * rows * links) if kind == "turned" else (lead, 4 * rows * links, width)
        for _, lead, rows, kind in plan
    ]
    if any(rows % 8 for _, _, rows, _ in plan):
        result = []
        both = jnp.stack([jnp.stack(near), jnp.stack(far)], axis=1)
        for (at, lead, rows, kind), shape in zip(plan, shapes):
            piece = both[:, :, :, at : at + lead * rows].reshape(links, 2, 2, lead, rows, width)
            if kind == "shared":
                piece = reorder(jnp.transpose(piece, (3, 1, 2, 0, 4, 5)), 1, 2, index & 1)
                piece = reorder(piece, 3, links, index // 2).reshape(lead, -1, width)
            else:
                piece = jnp.transpose(piece, (3, 0, 1, 2, 4, 5)).reshape(lead, n_dp, 2 * rows, width)
                piece = reorder(piece, 1, n_dp, index).reshape(lead, -1, width)
            piece = piece.astype(WIDE)
            result.append(jnp.swapaxes(piece, 1, 2) if kind == "turned" else piece)
        return result
    most = max([4 * rows * links for _, _, rows, kind in plan if kind == "turned"] or [8])
    return pl.pallas_call(
        functools.partial(place_rows_kernel, plan, links, by_part),
        out_shape=[jax.ShapeDtypeStruct(shape, WIDE) for shape in shapes],
        in_specs=[pl.BlockSpec(memory_space=pltpu.SMEM)]
        + [pl.BlockSpec(memory_space=pltpu.VMEM)] * (len(near) + len(far)),
        out_specs=[pl.BlockSpec(memory_space=pltpu.VMEM)] * len(plan),
        scratch_shapes=[pltpu.VMEM((most, width), WIDE)],
        compiler_params=pltpu.CompilerParams(vmem_limit_bytes=48 << 20),
        cost_estimate=pl.CostEstimate(flops=0, bytes_accessed=0, transcendentals=0),
        name="place_rows",
    )(index[None], *near, *far)


SMALL_COST = pl.CostEstimate(flops=0, bytes_accessed=0, transcendentals=0)
VMEM = pltpu.CompilerParams(vmem_limit_bytes=48 << 20)
TILE = 1024


def pair_kernel(dim, left_ref, right_ref, left_mate_ref, right_mate_ref, out_ref):
    total = dot(left_ref[...], right_ref[...], dim, 0) + dot(left_mate_ref[...], right_mate_ref[...], dim, 0)
    out_ref[...] = total.astype(LOW)


def pair_product(left, right, left_mate, right_mate, dim):
    units = left.shape[1 - dim]
    rows, width = right.shape
    tile = next(units // n for n in range(1, units) if units % n == 0 and units // n <= TILE)
    if dim:
        block = pl.BlockSpec((tile, rows), lambda i: (i, 0))
    else:
        block = pl.BlockSpec((rows, tile), lambda i: (0, i))
    whole = pl.BlockSpec((rows, width), lambda i: (0, 0))
    return pl.pallas_call(
        functools.partial(pair_kernel, dim),
        grid=(units // tile,),
        in_specs=[block, whole, block, whole],
        out_specs=pl.BlockSpec((tile, width), lambda i: (i, 0)),
        out_shape=jax.ShapeDtypeStruct((units, width), LOW),
        compiler_params=VMEM,
        cost_estimate=SMALL_COST,
        name="pair_product",
    )(left, right, left_mate, right_mate)


def split_kernel(picks, tile, learn, *refs):
    left, right, left_mate, right_mate = refs[:4]
    outs = refs[-2:]
    if learn:
        index_ref, extra = refs[4], refs[5]
        if learn == "make":
            learn_left, learn_right, learn_left_mate, learn_right_mate = refs[5:9]
            extra = refs[9]
            outs = refs[10:12]
            extra[...] = (
                dot(learn_left[...], learn_right[...], 0, 0) + dot(learn_left_mate[...], learn_right_mate[...], 0, 0)
            ).astype(LOW)
        links = left.shape[1] // (2 * tile)
        rows = extra.shape[0] // (2 * links)
    for half, (some, out) in enumerate(zip(picks, outs)):
        at = 0
        for link in some:
            spot = half * (left.shape[1] // 2) + link * tile
            columns = slice(spot, spot + tile)
            total = dot(left[:, columns], right[...], 0, 0) + dot(left_mate[:, columns], right_mate[...], 0, 0)
            out[at : at + tile] = total.astype(LOW)
            at += tile
            if learn:
                source = (half * links + (link ^ (index_ref[0] // 2))) * rows
                out[at : at + rows] = extra[pl.ds(pl.multiple_of(source, rows), rows)]
                at += rows


def split_product(left, right, left_mate, right_mate, picks, links, index=None, learn=None):
    tile = left.shape[1] // (2 * links)
    width = right.shape[1]
    rows = tile
    args = [left, right, left_mate, right_mate]
    specs = [pl.BlockSpec(memory_space=pltpu.VMEM)] * 4
    out_shape = []
    if learn is not None:
        args += [index[None], *learn]
        specs += [pl.BlockSpec(memory_space=pltpu.SMEM)] + [pl.BlockSpec(memory_space=pltpu.VMEM)] * len(learn)
        units = learn[0].shape[1] if len(learn) > 1 else learn[0].shape[0]
        rows += units // (2 * links)
        if len(learn) > 1:
            out_shape.append(jax.ShapeDtypeStruct((units, width), LOW))
    mode = None if learn is None else "make" if len(learn) > 1 else "take"
    out_shape += [jax.ShapeDtypeStruct((len(some) * rows, width), LOW) for some in picks]
    return pl.pallas_call(
        functools.partial(split_kernel, picks, tile, mode),
        out_shape=out_shape,
        in_specs=specs,
        out_specs=[pl.BlockSpec(memory_space=pltpu.VMEM)] * len(out_shape),
        compiler_params=VMEM,
        cost_estimate=SMALL_COST,
        name="split_product",
    )(*args)


def back_kernel(count, source_ref, *refs):
    rows = refs[-1].shape[0]
    row = pl.program_id(0) * rows + lax.broadcasted_iota(jnp.int32, (rows, source_ref.shape[1]), 0)
    spot = (row == source_ref[...]).astype(WIDE).astype(LOW)
    total, at = 0.0, 0
    for ref in refs[:count]:
        total = total + dot(spot[:, at : at + ref.shape[0]], ref[...], 1, 0)
        at += ref.shape[0]
    if len(refs) > count + 1:
        total = total + refs[count][...].astype(WIDE)
    refs[-1][...] = total.astype(LOW)


def rows_home(blocks, rows, base=None):
    sources = jnp.concatenate([b[0] for b in blocks])[None]
    values = [b[1] for b in blocks]
    width = values[0].shape[1]
    tile = min(256, rows)
    whole = lambda array: pl.BlockSpec(array.shape, lambda i: (0, 0))
    block = pl.BlockSpec((tile, width), lambda i: (i, 0))
    return pl.pallas_call(
        functools.partial(back_kernel, len(values)),
        grid=(rows // tile,),
        in_specs=[whole(sources)] + [whole(v) for v in values] + ([] if base is None else [block]),
        out_specs=block,
        out_shape=jax.ShapeDtypeStruct((rows, width), LOW),
        compiler_params=VMEM,
        cost_estimate=SMALL_COST,
        name="rows_home",
    )(sources, *values, *([] if base is None else [base]))


def rows_back_kernel(first_ref, second_ref, w_first_ref, w_second_ref, base_ref, normed_ref, inverse_ref, gain_ref, wide_ref, low_ref, gain_grad_ref, held):
    step = pl.program_id(0)
    held[step] = dot(first_ref[...], w_first_ref[...], 1, 0) + dot(second_ref[...], w_second_ref[...], 1, 0)

    @pl.when(step == pl.num_programs(0) - 1)
    def _():
        count, _, tile = held.shape
        parts = [slice(i * tile, (i + 1) * tile) for i in range(count)]
        mean, cross = 0.0, 0.0
        for i, part in enumerate(parts):
            normed = normed_ref[:, part]
            product = held[i] * normed
            gain_grad_ref[:, part] = jnp.sum(product, axis=0, keepdims=True)
            gain = gain_ref[:, part]
            mean = mean + jnp.sum(held[i] * gain, axis=1, keepdims=True)
            cross = cross + jnp.sum(product * gain, axis=1, keepdims=True)
        mean, cross = mean / (count * tile), cross / (count * tile)
        for i, part in enumerate(parts):
            scaled = held[i] * gain_ref[:, part]
            total = base_ref[:, part] + (scaled - mean - normed_ref[:, part] * cross) * inverse_ref[...]
            wide_ref[:, part] = total
            low_ref[:, part] = total.astype(LOW)


def rows_back(grads, weights, base, normed, inverse, gain):
    rows, width = base.shape
    units = grads[0].shape[1]
    tile = min(256, width)
    whole = lambda *shape: pl.BlockSpec(shape, lambda i: (0,) * len(shape))
    columns = pl.BlockSpec((units, tile), lambda i: (0, i))
    return pl.pallas_call(
        rows_back_kernel,
        grid=(width // tile,),
        in_specs=[
            whole(rows, units),
            whole(rows, units),
            columns,
            columns,
            whole(rows, width),
            whole(rows, width),
            whole(rows, 1),
            whole(1, width),
        ],
        out_specs=[whole(rows, width), whole(rows, width), whole(1, width)],
        out_shape=[
            jax.ShapeDtypeStruct((rows, width), WIDE),
            jax.ShapeDtypeStruct((rows, width), LOW),
            jax.ShapeDtypeStruct((1, width), WIDE),
        ],
        scratch_shapes=[pltpu.VMEM((width // tile, rows, tile), WIDE)],
        compiler_params=VMEM,
        cost_estimate=SMALL_COST,
        name="rows_back",
    )(*grads, *weights, base, normed, inverse, gain[None])


def two_kernel(first_ref, second_ref, right_ref, out_first_ref, out_second_ref):
    right = right_ref[...]
    out_first_ref[...] = dot(first_ref[...], right, 1, 1).astype(LOW)
    out_second_ref[...] = dot(second_ref[...], right, 1, 1).astype(LOW)


def two_products(weights, right):
    return pl.pallas_call(
        two_kernel,
        out_shape=[jax.ShapeDtypeStruct((w.shape[0], right.shape[0]), LOW) for w in weights],
        compiler_params=VMEM,
        cost_estimate=SMALL_COST,
        name="two_products",
    )(*weights, right)


def attend_kernel(scale, first_ref, second_ref, column_ref, row_ref, mixed_first_ref, mixed_second_ref, log_ref):
    query, key, value = [jnp.concatenate([first_ref[i, 0], second_ref[i, 0]]) for i in range(3)]
    scores = dot(key, query * scale, 0, 0)
    scores = jnp.where(column_ref[...] == row_ref[...], scores, FAR)
    most = jnp.max(scores, axis=0, keepdims=True)
    exponent = jnp.exp(scores - most)
    total = jnp.sum(exponent, axis=0, keepdims=True)
    mixed = (dot(value, exponent.astype(LOW), 1, 0) / total).astype(LOW)
    half = mixed.shape[0] // 2
    mixed_first_ref[0] = mixed[:half]
    mixed_second_ref[0] = mixed[half:]
    log_ref[0] = most + jnp.log(total)


def attend(first, second, image, scale):
    _, heads, half, rows = first.shape
    three = pl.BlockSpec((3, 1, half, rows), lambda h: (0, h, 0, 0))
    one = pl.BlockSpec((1, half, rows), lambda h: (h, 0, 0))
    return pl.pallas_call(
        functools.partial(attend_kernel, scale),
        grid=(heads,),
        in_specs=[
            three,
            three,
            pl.BlockSpec((rows, 1), lambda h: (0, 0)),
            pl.BlockSpec((1, rows), lambda h: (0, 0)),
        ],
        out_specs=[one, one, pl.BlockSpec((1, 1, rows), lambda h: (h, 0, 0))],
        out_shape=[
            jax.ShapeDtypeStruct((heads, half, rows), LOW),
            jax.ShapeDtypeStruct((heads, half, rows), LOW),
            jax.ShapeDtypeStruct((heads, 1, rows), WIDE),
        ],
        compiler_params=pltpu.CompilerParams(vmem_limit_bytes=48 << 20),
        cost_estimate=SMALL_COST,
        name="attend",
    )(first, second, image[:, None], image[None, :])


def attend_back_kernel(
    scale,
    first_ref,
    second_ref,
    mixed_first_ref,
    mixed_second_ref,
    grad_first_ref,
    grad_second_ref,
    log_ref,
    column_ref,
    row_ref,
    *out_refs,
):
    out_first_ref, out_second_ref = out_refs[-2:]
    query, key, value = [jnp.concatenate([first_ref[i, 0], second_ref[i, 0]]) for i in range(3)]
    query = query * scale
    mixed = jnp.concatenate([mixed_first_ref[0], mixed_second_ref[0]])
    grad = jnp.concatenate([grad_first_ref[0], grad_second_ref[0]])
    scores = dot(key, query, 0, 0)
    scores = jnp.where(column_ref[...] == row_ref[...], scores, FAR)
    probs = jnp.exp(scores - log_ref[0])
    grad_probs = dot(value, grad, 0, 0)
    inner = jnp.sum(mixed.astype(WIDE) * grad.astype(WIDE), axis=0, keepdims=True)
    grad_scores = (probs * (grad_probs - inner)).astype(LOW)
    grads = (
        (dot(key, grad_scores, 1, 0) * scale).astype(LOW),
        dot(query, grad_scores, 1, 1).astype(LOW),
        dot(grad, probs.astype(LOW), 1, 1).astype(LOW),
    )
    half = mixed.shape[0] // 2
    for i, item in enumerate(grads):
        out_first_ref[i, 0] = item[:half]
        out_second_ref[i, 0] = item[half:]


def attend_back(first, second, mixed, grad_mixed, log_sums, image, scale, part, so_far=()):
    _, heads, half, rows = first.shape
    base = part * (heads // 2)
    three = pl.BlockSpec((3, 1, half, rows), lambda h: (0, base + h, 0, 0))
    one = pl.BlockSpec((1, half, rows), lambda h: (base + h, 0, 0))
    return pl.pallas_call(
        functools.partial(attend_back_kernel, scale),
        grid=(heads // 2,),
        in_specs=[
            three,
            three,
            one,
            one,
            one,
            one,
            pl.BlockSpec((1, 1, rows), lambda h: (base + h, 0, 0)),
            pl.BlockSpec((rows, 1), lambda h: (0, 0)),
            pl.BlockSpec((1, rows), lambda h: (0, 0)),
        ]
        + [pl.BlockSpec(memory_space=pl.ANY)] * len(so_far),
        out_specs=[three, three],
        out_shape=[jax.ShapeDtypeStruct((3, heads, half, rows), LOW)] * 2,
        input_output_aliases={9 + i: i for i in range(len(so_far))},
        compiler_params=pltpu.CompilerParams(vmem_limit_bytes=48 << 20),
        cost_estimate=SMALL_COST,
        name="attend_back",
    )(first, second, *mixed, *grad_mixed, log_sums, image[:, None], image[None, :], *so_far)


def local(
    n_dp,
    n_tensor,
    patches,
    pos_embed,
    counts,
    ln1_gain,
    w_qkv,
    w_out,
    ln2_gain,
    w_up,
    w_down,
    ln3_gain,
    w_learn1,
    w_learn2,
    cotangent,
):
    rows, width = patches.shape
    images = counts.shape[1]
    tokens = w_learn2.shape[1]
    capacity = row_capacity(rows, images, n_tensor)
    scale = HEAD_DIM**-0.5
    tensor_index = lax.axis_index("tensor")
    index = lax.axis_index("dp")
    heads = n_tensor * w_qkv.shape[2] // HEAD_DIM
    mate = lambda value: swap(value, "dp", n_dp, 1)

    links = n_dp.bit_length() - 2
    spans = n_tensor.bit_length() - 1
    turned = jnp.transpose(w_qkv, (1, 2, 0))
    z_a = Flow(1, gather_tensor([my_piece(turned, n_dp, index)], n_tensor))
    place = place_images(counts, n_tensor)
    image, source = row_map(place, counts, tensor_index, capacity)
    part_up = w_up.shape[1] // n_dp
    piece_up = jnp.transpose(lax.dynamic_slice_in_dim(w_up, index * part_up, part_up, 1))
    pieces = [my_piece(w_out[None], n_dp, index), piece_up.reshape(2, part_up // 2, width)]
    piece_down = my_piece(w_down[None], n_dp, index)
    (far_a,) = z_a.finish(source)
    x_a = Flow(links, link_gathers(far_a, n_dp))
    z_b = Flow(1, gather_tensor([after(p, far_a) for p in pieces], n_tensor))
    pick = (after(source, far_a)[:, None] == jnp.arange(rows, dtype=jnp.int32)[None, :]).astype(LOW)
    inputs = dot(pick, patches, 1, 0)
    x_a.go(inputs)
    inputs = inputs + dot(pick, after(pos_embed, *x_a.sent), 1, 0)
    normed_one, inverse_one = layer_norm(inputs)
    low_one = (normed_one * ln1_gain).astype(LOW)
    own_qkv = own_units(after(turned, *x_a.sent), n_dp, index)
    own_up = own_units(jnp.transpose(after(w_up, *x_a.sent))[None], n_dp, index)
    near_a = links_first(x_a.finish(low_one), n_dp)
    core_a = [swap(v, "dp", n_dp, 1) for v in near_a]
    shards = [turned, w_out[None], None, w_down[None]]
    sizes = [
        (3, w_qkv.shape[2] // (2 * n_dp)),
        (1, w_out.shape[0] // (2 * n_dp)),
        (1, w_up.shape[1] // (2 * n_dp)),
        (1, w_down.shape[0] // (2 * n_dp)),
    ]
    units_of = lambda halves, some: far_units(halves, some, n_dp, n_tensor)
    qkv = [None, None]

    def project(core, halves):
        full = join(own_qkv[core], units_of(halves, sizes[:1])[0], False)
        qkv[core] = dot_low(full, low_one, 1, 1).reshape(3, heads, -1, capacity)
        return full

    full_qkv = [project(0, near_a)]
    core_a = [after(c, qkv[0]) for c in core_a]
    (far_b,) = z_b.finish(*own_up)
    x_b = Flow(links, link_gathers(far_b, n_dp))
    z_c = Flow(1, gather_tensor([after(piece_down, far_b)], n_tensor))
    full_qkv.append(project(1, core_a))
    mixed_first, mixed_second, log_sums = attend(*qkv, image, scale)
    mixed = [m.reshape(-1, capacity) for m in (mixed_first, mixed_second)]
    x_b.go(mixed[0])
    own_out = own_units(after(w_out, *x_b.sent)[None], n_dp, index)
    (far_c,) = z_c.finish(*own_out)
    x_c = Flow(links, link_gathers(far_c, n_dp))
    own_down = own_units(after(w_down, *x_c.sent)[None], n_dp, index)
    near_b = links_first(x_b.finish(*own_down), n_dp)
    core_b = [swap(v, "dp", n_dp, 1) for v in near_b]
    full_out, full_up, full_down = [], [], []

    def join_b(core, halves):
        far_out, far_up = units_of(halves, sizes[1:3])
        full_out.append(join(own_out[core], far_out, False))
        full_up.append(join(own_up[core], far_up, True))

    join_b(0, near_b)
    x_c.go(full_up[0])
    join_b(1, [after(c, full_up[0], *x_c.sent) for c in core_b])
    member = (image[:, None] == jnp.arange(images, dtype=jnp.int32)[None, :]).astype(WIDE)
    row_scale = jnp.sum(member * lax.rsqrt(counts[0].astype(WIDE))[None, :], axis=1)

    hidden = inputs + dot(mixed[0], full_out[0], 0, 0) + dot(mixed[1], full_out[1], 0, 0)
    normed_two, inverse_two = layer_norm(hidden)
    low_two = (normed_two * ln2_gain).astype(LOW)
    mate_mixed, mate_one = mate(after(mixed[1], low_two)), mate(after(low_one, low_two))
    active, slope = [], []

    def feed(core, normed):
        value, rate = gelu_both(dot(normed, full_up[core], 1, 1))
        active.append(value.astype(LOW))
        slope.append(rate.astype(LOW))

    feed(0, low_two)
    near_c = links_first(x_c.finish(active[0]), n_dp)
    core_c = [swap(v, "dp", n_dp, 1) for v in near_c]
    feed(1, after(low_two, mate_mixed, mate_one, active[0]))
    full_down.append(join(own_down[0], units_of(near_c, sizes[3:])[0], True))
    fed = dot(active[0], full_down[0], 1, 0)
    mate_active, mate_two = mate(active[1]), mate(low_two)
    core_c = [after(c, active[1], full_down[0]) for c in core_c]
    full_down.append(join(own_down[1], units_of(core_c, sizes[3:])[0], True))
    output = hidden + fed + dot(active[1], full_down[1], 1, 0)
    normed_three, inverse_three = layer_norm(output)
    low_three = (normed_three * ln3_gain).astype(LOW)
    low_three = after(low_three, mate_active, mate_two)
    acted, learn_slope = gelu_both(dot(low_three, w_learn1, 1, 0))
    acted, learn_slope = acted.astype(LOW), learn_slope.astype(LOW)
    select = jax.nn.sigmoid(dot(acted, w_learn2, 1, 0))
    weights = (select * row_scale[:, None]).astype(LOW)
    table = (member.astype(LOW)[:, :, None] * weights[:, None, :]).reshape(capacity, images * tokens)
    low_out = output.astype(LOW)
    learned = dot_low(table, low_out, 0, 0)

    grad_pooled = cotangent.reshape(images * tokens, width)
    grad_output = dot(table, grad_pooled, 1, 0)
    grad_table = dot(low_out, grad_pooled, 1, 1)
    grad_weights = jnp.sum(grad_table.reshape(capacity, images, tokens) * member[:, :, None], axis=1)
    grad_logits = (grad_weights * row_scale[:, None] * select * (1.0 - select)).astype(LOW)
    grad_learn2 = dot(grad_logits, acted, 0, 0)
    grad_inner = (dot(grad_logits, w_learn2, 1, 1) * learn_slope.astype(WIDE)).astype(LOW)
    side = width // 2
    three_keep = lax.dynamic_slice_in_dim(low_three, (index & 1) * side, side, 1)
    three_away = lax.dynamic_slice_in_dim(low_three, (1 - (index & 1)) * side, side, 1)
    mate_three, mate_inner = mate(three_away), mate(grad_inner)
    grad_from_three, grad_gain3 = norm_back(
        dot(grad_inner, w_learn1, 1, 1), ln3_gain, normed_three, inverse_three
    )
    grad_output = grad_output + grad_from_three

    grad_fed = grad_output.astype(LOW)
    mate_three, mate_inner = after(mate_three, grad_fed), after(mate_inner, grad_fed)
    mate_fed = mate(grad_fed)
    units = functools.partial(split_units, n_dp=n_dp, n_tensor=n_tensor)
    ready = after(grad_fed, mate_three, mate_inner)
    upward = lambda c, grad: (dot(grad, full_down[c], 1, 1) * slope[c].astype(WIDE)).astype(LOW)
    grad_upper = [None, upward(1, ready)]
    mate_upper = mate(grad_upper[1])
    mate_fed = after(mate_fed, grad_upper[1])
    away, stay = first_split(n_dp, True), first_split(n_dp, False)
    down_operands = (active[0], grad_fed, mate_active, mate_fed)
    grad_learn1, *down_away = split_product(
        *down_operands, away, n_dp // 2, index, (three_keep, grad_inner, mate_three, mate_inner)
    )
    down_stay = split_product(*down_operands, stay, n_dp // 2, index, (grad_learn1,))
    bits_left = (2,) * (n_dp.bit_length() - 3)
    kept = lambda parts: [[p.reshape(bits_left + (-1, width))] for p in parts]
    x_down = Flow(links, link_sums_from(kept(down_stay), down_away, n_dp))
    grad_upper[0] = upward(0, after(grad_fed, *down_stay))
    mate_upper = after(mate_upper, grad_upper[0])
    grad_hidden, grad_attended, grad_gain2 = rows_back(
        grad_upper, full_up, grad_output, normed_two, inverse_two, ln2_gain
    )
    grad_gain2 = grad_gain2[0]

    grad_mixed = [g.reshape(heads, -1, capacity) for g in two_products(full_out, grad_attended)]
    x_down.go(*grad_mixed)
    up_operands = (after(grad_upper[0], *x_down.sent), low_two, mate_upper, mate_two)
    up_away = split_product(*up_operands, away, n_dp // 2)
    up_stay = split_product(*up_operands, stay, n_dp // 2)
    pair_down = x_down.finish(*up_stay)
    down_rows = active[0].shape[1] // n_dp
    everywhere = [pair_down[0][:, down_rows:], learned.reshape(2, -1, width)]
    z_down = Flow(spans, reduce_tensor([pair_down[0][:, :down_rows]], everywhere, n_tensor))
    x_up = Flow(links, link_sums_from(kept(up_stay), [after(u, *pair_down) for u in up_away], n_dp))
    grad_mixed = [after(g, *z_down.sent, *x_up.sent) for g in grad_mixed]
    mate_attended = mate(after(grad_attended, *x_up.sent))
    attended_back = functools.partial(
        attend_back, *qkv, (mixed_first, mixed_second), log_sums=log_sums, image=image, scale=scale
    )
    half_qkv = attended_back(grad_mixed, part=0)
    z_down.go(half_qkv[0])
    grad_mixed = [after(g, *z_down.sent) for g in grad_mixed]
    grad_qkv = attended_back(grad_mixed, part=1, so_far=half_qkv)
    grad_qkv = [g.reshape(-1, capacity) for g in grad_qkv]
    mate_qkv = mate(grad_qkv[1])
    grad_from_one, grad_gain1 = norm_back(
        dot(grad_qkv[0], full_qkv[0], 0, 0) + dot(grad_qkv[1], full_qkv[1], 0, 0),
        ln1_gain,
        normed_one,
        inverse_one,
    )
    near = (grad_hidden + grad_from_one).astype(LOW)
    some = capacity // 2
    ring_a = Flow(spans, gather_rows(near[:some], n_tensor))
    x_up.go(near)
    mate_qkv, mate_attended = [after(m, *x_up.sent) for m in (mate_qkv, mate_attended)]
    grad_out = pair_product(mixed[0], grad_attended, mate_mixed, mate_attended, 1)
    grad_qkv_weight = pair_product(after(grad_qkv[0], *x_up.sent), low_one, mate_qkv, mate_one, 1)
    extra = jnp.concatenate([jnp.stack([grad_gain1, grad_gain2, grad_gain3]), grad_learn2])
    extra = jnp.pad(extra, ((0, 16 * n_dp - extra.shape[0]), (0, 0)))
    extra = (extra + mate(extra)).astype(LOW)

    (sum_down,) = z_down.finish(grad_qkv_weight, grad_out)
    pair_up = x_up.finish(sum_down)
    z_up = Flow(spans, reduce_tensor(pair_up, [], n_tensor))
    x_qkv = Flow(
        links,
        link_sums(
            [
                units(after(grad_qkv_weight, *pair_up), 3, part_first=False),
                units(after(grad_out, *pair_up), 1, part_first=False),
                split_shared(after(extra, *pair_up), n_dp, index),
            ],
            n_dp,
        ),
    )
    learned = sum_down[:, -(images * tokens // 2) :].reshape(images, tokens, width)
    sum_down = sum_down[:, : -(images * tokens // 2)]
    ring_a.go(*x_qkv.sent, *z_up.sent)
    ring_b = Flow(spans, gather_rows(after(near[some:], *ring_a.sent), n_tensor))
    z_up.go(*ring_b.sent)
    x_qkv.go(*z_up.sent)
    pair_qkv = x_qkv.finish()
    z_qkv = Flow(spans, reduce_tensor(pair_qkv[:2], pair_qkv[2:], n_tensor))
    (sum_up,) = z_up.finish(*z_qkv.sent)
    sum_seen = jnp.concatenate([after(sum_down, *pair_qkv), sum_up], axis=1)
    x_seen = Flow(links, link_gathers(sum_seen, n_dp))
    while ring_a.left > 1:
        ring_a.go(*x_seen.sent)
        ring_b.go(*ring_a.sent)
    (rows_a,) = ring_a.finish(*z_qkv.sent, *x_seen.sent)
    ring_b.go(rows_a)
    while x_seen.left > 1:
        x_seen.go(*ring_b.sent)

    z_qkv.go(*x_seen.sent)
    sources = [source] + [row_map(place, counts, tensor_index ^ j, capacity)[1] for j in range(1, n_tensor)]
    blocks = [(after(source, *z_qkv.sent), near)]
    blocks += [(sources[j][:some], rows_a[j]) for j in range(1, n_tensor)]
    early = rows_home(blocks, rows)
    (sum_qkv,) = z_qkv.finish(early)
    x_last = Flow(1, plane_spread(sum_qkv, n_dp))
    near_seen = x_seen.finish(*x_last.sent)
    seen_a = both_near(near_seen, n_dp)
    down_rows = up_rows = active[0].shape[1] // (n_tensor * n_dp)
    out_rows, qkv_rows, extra_rows = [
        grad.shape[0] // (parts * n_dp * lead)
        for grad, parts, lead in (
            (grad_out, n_tensor, 1),
            (grad_qkv_weight, n_tensor, 3),
            (extra, 1, 1),
        )
    ]
    learn_rows = grad_learn1.shape[0] // n_dp
    at = down_rows + learn_rows
    down_sum, learn_sum, up_sum = place_parts(
        seen_a,
        ((0, 1, down_rows, "plain"), (down_rows, 1, learn_rows, "shared"), (at, 1, up_rows, "turned")),
        n_dp,
        index,
    )
    (rows_b,) = ring_b.finish(*x_last.sent)
    input_grad = rows_home([(sources[j][some:], rows_b[j]) for j in range(1, n_tensor)], rows, early)
    near_c = x_last.finish(input_grad, down_sum)
    far_c = mate(jnp.stack(near_c))
    far_c = [far_c[link] for link in range(n_dp // 2)]
    qkv_sum, out_sum = place_rows(
        near_c, far_c, ((0, 3, qkv_rows, "turned"), (3 * qkv_rows, 1, out_rows, "plain")), n_dp, index
    )
    small = jnp.stack([v[0, 3 * qkv_rows + out_rows :] for v in near_c])
    small = lax.dynamic_slice_in_dim(small, index // 2, 1, 0)[0].astype(WIDE)

    return (
        learned,
        input_grad,
        small[0],
        jnp.transpose(qkv_sum, (1, 0, 2)),
        out_sum[0],
        small[1],
        up_sum[0],
        down_sum[0],
        small[2],
        learn_sum[0],
        jnp.transpose(small[3 : 3 + tokens]),
    )


def solution(mesh):
    return jax.shard_map(
        functools.partial(local, mesh.shape["dp"], mesh.shape["tensor"]),
        mesh=mesh,
        in_specs=(
            P("dp", None),
            P("dp", None),
            P("dp", None),
            P(),
            P(None, None, "tensor"),
            P("tensor", None),
            P(),
            P(None, "tensor"),
            P("tensor", None),
            P(),
            P(),
            P(),
            P("dp", None, None),
        ),
        out_specs=(
            P("dp", None, None),
            P("dp", None),
            P(),
            P(None, None, "tensor"),
            P("tensor", None),
            P(),
            P(None, "tensor"),
            P("tensor", None),
            P(),
            P(),
            P(),
        ),
        check_vma=False,
    )
```

```python
import functools

import jax
import jax.numpy as jnp
from jax import lax
from jax.experimental import pallas as pl
from jax.experimental.pallas import tpu as pltpu
from jax.sharding import PartitionSpec as P

HEAD_DIM = 64
MOST = 576
EPSILON = 1e-06
LOW = jnp.bfloat16
WIDE = jnp.float32
FAR = -1e30


def layer_norm(values):
    center = values - jnp.mean(values, axis=-1, keepdims=True)
    variance = jnp.mean(center * center, axis=-1, keepdims=True)
    inverse = lax.rsqrt(variance + EPSILON)
    return center * inverse, inverse


def norm_back(grad_in, gain, normed, inverse):
    gain_grad = jnp.sum(grad_in * normed, axis=0)
    scaled = grad_in * gain
    result = (
        scaled
        - jnp.mean(scaled, axis=-1, keepdims=True)
        - normed * jnp.mean(scaled * normed, axis=-1, keepdims=True)
    ) * inverse
    return result, gain_grad


def gelu_both(values):
    share = 0.5 * (1.0 + lax.erf(values * (0.5**0.5)))
    density = jnp.exp(-0.5 * values * values) * 0.3989422804014327
    return values * share, share + values * density


def dot(left, right, left_dim, right_dim):
    return lax.dot_general(
        left, right, (((left_dim,), (right_dim,)), ((), ())), preferred_element_type=WIDE
    )


def dot_low(left, right, left_dim, right_dim):
    return dot(left, right, left_dim, right_dim).astype(LOW)


def row_capacity(rows, images, n_tensor):
    if n_tensor >= images:
        most = MOST
    elif n_tensor == 4 and images == 8 and rows == 2048:
        most = 630
    else:
        most = rows // n_tensor + MOST
    return min(rows, -(-most // 128) * 128)


def place_kernel(n_tensor, counts_ref, place_ref):
    images = counts_ref.shape[1]
    count = [counts_ref[0, i] for i in range(images)]
    zero = count[0] * 0
    used, device, offset = [zero] * images, [zero] * images, [zero] * images
    loads = [zero] * n_tensor
    for _ in range(images):
        best, at = zero - 1, zero
        for i in range(images):
            better = jnp.logical_and(used[i] == 0, count[i] > best)
            best = jnp.where(better, count[i], best)
            at = jnp.where(better, i, at)
        least, least_at = loads[0], zero
        for b in range(1, n_tensor):
            better = loads[b] < least
            least = jnp.where(better, loads[b], least)
            least_at = jnp.where(better, b, least_at)
        for i in range(images):
            here = at == i
            used[i] = jnp.where(here, 1, used[i])
            device[i] = jnp.where(here, least_at, device[i])
            offset[i] = jnp.where(here, least, offset[i])
        for b in range(n_tensor):
            loads[b] = loads[b] + jnp.where(least_at == b, best, 0)
    start = zero
    for i in range(images):
        place_ref[0, i] = device[i]
        place_ref[1, i] = offset[i]
        place_ref[2, i] = start
        start = start + count[i]


def place_images(counts, n_tensor):
    images = counts.shape[1]
    return pl.pallas_call(
        functools.partial(place_kernel, n_tensor),
        out_shape=jax.ShapeDtypeStruct((3, images), jnp.int32),
        in_specs=[pl.BlockSpec(memory_space=pltpu.SMEM)],
        out_specs=pl.BlockSpec(memory_space=pltpu.SMEM),
        name="place_images",
    )(counts)


def gather_rows(rows, n_tensor):
    held = rows[None]
    mask = n_tensor // 2
    while mask:
        (came,) = yield [swap(held, "tensor", n_tensor, mask)], [held]
        held = jnp.stack([held, came], axis=1).reshape((-1,) + rows.shape)
        mask //= 2
    yield [held], []


def row_map(place, counts, device, capacity):
    row = jnp.arange(capacity, dtype=jnp.int32)[:, None]
    offset, start = place[1][None], place[2][None]
    inside = (place[0][None] == device) & (row >= offset) & (row < offset + counts)
    image = jnp.sum(jnp.where(inside, jnp.arange(counts.shape[1], dtype=jnp.int32) + 1, 0), axis=1) - 1
    source = jnp.sum(jnp.where(inside, start - offset + row + 1, 0), axis=1) - 1
    return image, source


def after(value, *others):
    return lax.optimization_barrier((value,) + others)[0]


class Flow:
    def __init__(self, stages, generator):
        self.left = stages
        self.generator = generator
        self.came, self.sent = next(generator)

    def go(self, *others):
        self.came, self.sent = self.generator.send([after(c, *others) for c in self.came])
        self.left -= 1
        return self

    def finish(self, *others):
        while self.left:
            self.go(*others)
        return self.came


def swap(value, axis, size, mask):
    return lax.ppermute(value, axis, [(i, i ^ mask) for i in range(size)])


def reorder(value, dim, size, index):
    return jnp.concatenate(
        [lax.dynamic_slice_in_dim(value, index ^ m, 1, dim) for m in range(size)], axis=dim
    )


def link_bits(n_dp, half):
    bits = list(range(1, n_dp.bit_length() - 1))
    return bits[::-1] if half else bits


def link_gathers(far, n_dp):
    value = [far[0], far[1]]
    for step in range(n_dp.bit_length() - 2):
        came = [swap(value[half], "dp", n_dp, 1 << link_bits(n_dp, half)[step]) for half in range(2)]
        came = yield came, value
        value = [jnp.stack([v, c]) for v, c in zip(value, came)]
    yield value, []


def links_first(value, n_dp):
    count = n_dp.bit_length() - 2
    turned = jnp.transpose(value[1], tuple(range(count))[::-1] + tuple(range(count, value[1].ndim)))
    return [v.reshape((1 << count,) + v.shape[count:]) for v in (value[0], turned)]


def own_units(shard, n_dp, index):
    lead, units, width = shard.shape
    part = units // (2 * n_dp)
    split = shard.reshape(lead, n_dp, 2, part, width)
    ordered = reorder(split, 1, n_dp, index).reshape(lead, n_dp // 2, 2, 2, part, width)
    return [ordered[:, :, core] for core in range(2)]


def my_piece(shard, n_dp, index):
    lead, units, width = shard.shape
    part = units // (2 * n_dp)
    split = shard.reshape(lead, n_dp, 2, part, width)
    mine = lax.dynamic_slice_in_dim(split, index, 1, 1)[:, 0]
    return jnp.transpose(mine, (1, 0, 2, 3)).reshape(2, lead * part, width)


def gather_tensor(pieces, n_tensor):
    pack = jnp.concatenate(pieces, axis=1) if len(pieces) > 1 else pieces[0]
    came = yield [swap(pack, "tensor", n_tensor, j) for j in range(1, n_tensor)], [pack]
    yield [jnp.stack(came, axis=1)], []


def far_units(halves, sizes, n_dp, n_tensor):
    width = halves[0].shape[-1]
    weights, at = [], 0
    for lead, part in sizes:
        pieces = [
            h[:, :, at : at + lead * part].reshape(n_dp // 2, n_tensor - 1, lead, part, width) for h in halves
        ]
        weights.append(jnp.transpose(jnp.stack(pieces), (3, 2, 1, 0, 4, 5)))
        at += lead * part
    return weights


def join(own, far, part_first):
    width = own.shape[-1]
    full = jnp.concatenate([own[:, None], far], axis=1)
    if part_first:
        full = jnp.transpose(full, (3, 0, 2, 1, 4, 5))
    return full.reshape(-1, width)


def split_units(grad, lead, n_dp, n_tensor, part_first):
    width = grad.shape[-1]
    links = n_dp // 2
    if part_first:
        parts = grad.reshape(2, links, -1, width)
        return [parts[0], parts[1]]
    split = grad.reshape(lead, n_tensor, links, 2, -1, width)
    return [
        jnp.transpose(split[:, :, :, half], (2, 1, 0, 3, 4)).reshape(links, -1, width) for half in range(2)
    ]


def split_shared(grad, n_dp, index):
    links = n_dp // 2
    parts = grad.reshape(2, links, -1, grad.shape[-1])
    ordered = reorder(parts, 1, links, index // 2)
    return [ordered[0], ordered[1]]


def link_sums(groups, n_dp):
    width = groups[0][0].shape[-1]
    bits = n_dp.bit_length() - 2
    halves = [[g[half].reshape((2,) * bits + g[half].shape[1:]) for g in groups] for half in range(2)]
    held = [list(range(bits, 0, -1)) for _ in range(2)]
    keeps, aways = [], []
    for half in range(2):
        dim = held[half].index(link_bits(n_dp, 1 - half)[0])
        keeps.append([lax.index_in_dim(p, 0, dim, keepdims=False) for p in halves[half]])
        aways.append(join_rows([lax.index_in_dim(p, 1, dim, keepdims=False).reshape(-1, width) for p in halves[half]]))
    yield from link_sums_from(keeps, aways, n_dp)


def join_rows(items):
    return jnp.concatenate(items) if len(items) > 1 else items[0]


def link_sums_from(keeps, aways, n_dp):
    width = aways[0].shape[-1]
    bits = n_dp.bit_length() - 2
    held = [list(range(bits, 0, -1)) for _ in range(2)]
    for step in range(bits):
        came = []
        for half in range(2):
            bit = link_bits(n_dp, 1 - half)[step]
            held[half].remove(bit)
            came.append(swap(aways[half], "dp", n_dp, 1 << bit))
        came = yield came, aways
        halves = []
        for half in range(2):
            at, summed = 0, []
            for keep in keeps[half]:
                size = keep.size // width
                piece = came[half][at : at + size].reshape(keep.shape)
                summed.append((keep.astype(WIDE) + piece.astype(WIDE)).astype(LOW))
                at += size
            halves.append(summed)
        if step + 1 == bits:
            break
        keeps, aways = [], []
        for half in range(2):
            dim = held[half].index(link_bits(n_dp, 1 - half)[step + 1])
            keeps.append([lax.index_in_dim(p, 0, dim, keepdims=False) for p in halves[half]])
            away = [lax.index_in_dim(p, 1, dim, keepdims=False).reshape(-1, width) for p in halves[half]]
            aways.append(join_rows(away))
    yield [jnp.stack([a, b]) for a, b in zip(*halves)], []


def first_split(n_dp, away):
    links = n_dp // 2
    return [
        [m for m in range(links) if bool(m >> (link_bits(n_dp, 1 - half)[0] - 1) & 1) == away] for half in range(2)
    ]


def plane_spread(total, n_dp):
    came = yield [swap(total, "dp", n_dp, 2 * link) for link in range(1, n_dp // 2)], [total]
    yield [total] + came, []


def reduce_tensor(scattered, shared, n_tensor):
    width = (scattered + shared)[0].shape[-1]
    held = [s.reshape(2, n_tensor, -1, width) for s in scattered]
    mask = 1
    while mask < n_tensor:
        split = [h.reshape(2, -1, 2, h.shape[2], width) for h in held]
        flat = [h[:, :, 1].reshape(2, -1, width) for h in split] + shared
        flat = jnp.concatenate(flat, axis=1) if len(flat) > 1 else flat[0]
        (came,) = yield [swap(flat, "tensor", n_tensor, mask)], [flat]
        summed, at = [], 0
        for keep in [h[:, :, 0] for h in split] + shared:
            size = keep.size // (2 * width)
            piece = came[:, at : at + size].reshape(keep.shape)
            summed.append((keep.astype(WIDE) + piece.astype(WIDE)).astype(LOW))
            at += size
        held, shared = summed[: len(held)], summed[len(held) :]
        mask *= 2
    parts = [h[:, 0] for h in held] + shared
    yield [jnp.concatenate(parts, axis=1) if len(parts) > 1 else parts[0]], []


def both_near(value, n_dp):
    near = [v.reshape((n_dp // 2,) + v.shape[-2:]) for v in value]
    return [near, [swap(n, "dp", n_dp, 1) for n in near]]


def by_link(parts):
    links = parts[0].shape[0]
    bits = links.bit_length() - 1
    return [jnp.stack([parts[0][link], parts[1][backwards(link, bits)]]) for link in range(links)]


def backwards(number, bits):
    result = 0
    for _ in range(bits):
        result, number = result * 2 + number % 2, number // 2
    return result


def place_rows_kernel(plan, links, by_part, index_ref, *refs):
    count = 4 if by_part else 2 * links
    bits = links.bit_length() - 1
    outs = refs[count : count + len(plan)]

    def piece(core, half, link, start, rows):
        if by_part:
            return refs[2 * core + half][backwards(link, bits) if half else link, start : start + rows]
        return refs[core * links + link][half, start : start + rows]

    held = refs[-1]
    index = index_ref[0]
    for (at, lead, rows, kind), out in zip(plan, outs):
        for i in range(lead):
            target = held if kind == "turned" else out.at[i]
            for core in range(2):
                for half in range(2):
                    for link in range(links):
                        if kind == "shared":
                            spot = (((core ^ index) & 1) * 2 + half) * links + (link ^ (index >> 1))
                        else:
                            spot = ((2 * link + core) ^ index) * 2 + half
                        start = at + i * rows
                        found = piece(core, half, link, start, rows).astype(WIDE)
                        target[pl.ds(pl.multiple_of(spot * rows, rows), rows), :] = found
            if kind == "turned":
                out[i] = held[: 4 * rows * links].T


def place_parts(seen, plan, n_dp, index):
    if any(rows % 8 for _, _, rows, _ in plan):
        return place_rows(by_link(seen[0]), by_link(seen[1]), plan, n_dp, index)
    return place_rows(*seen, plan, n_dp, index, True)


def place_rows(near, far, plan, n_dp, index, by_part=False):
    links = n_dp // 2
    width = near[0].shape[-1]
    shapes = [
        (lead, width, 4 * rows * links) if kind == "turned" else (lead, 4 * rows * links, width)
        for _, lead, rows, kind in plan
    ]
    if any(rows % 8 for _, _, rows, _ in plan):
        result = []
        both = jnp.stack([jnp.stack(near), jnp.stack(far)], axis=1)
        for (at, lead, rows, kind), shape in zip(plan, shapes):
            piece = both[:, :, :, at : at + lead * rows].reshape(links, 2, 2, lead, rows, width)
            if kind == "shared":
                piece = reorder(jnp.transpose(piece, (3, 1, 2, 0, 4, 5)), 1, 2, index & 1)
                piece = reorder(piece, 3, links, index // 2).reshape(lead, -1, width)
            else:
                piece = jnp.transpose(piece, (3, 0, 1, 2, 4, 5)).reshape(lead, n_dp, 2 * rows, width)
                piece = reorder(piece, 1, n_dp, index).reshape(lead, -1, width)
            piece = piece.astype(WIDE)
            result.append(jnp.swapaxes(piece, 1, 2) if kind == "turned" else piece)
        return result
    most = max([4 * rows * links for _, _, rows, kind in plan if kind == "turned"] or [8])
    return pl.pallas_call(
        functools.partial(place_rows_kernel, plan, links, by_part),
        out_shape=[jax.ShapeDtypeStruct(shape, WIDE) for shape in shapes],
        in_specs=[pl.BlockSpec(memory_space=pltpu.SMEM)]
        + [pl.BlockSpec(memory_space=pltpu.VMEM)] * (len(near) + len(far)),
        out_specs=[pl.BlockSpec(memory_space=pltpu.VMEM)] * len(plan),
        scratch_shapes=[pltpu.VMEM((most, width), WIDE)],
        compiler_params=pltpu.CompilerParams(vmem_limit_bytes=48 << 20),
        cost_estimate=pl.CostEstimate(flops=0, bytes_accessed=0, transcendentals=0),
        name="place_rows",
    )(index[None], *near, *far)


SMALL_COST = pl.CostEstimate(flops=0, bytes_accessed=0, transcendentals=0)
VMEM = pltpu.CompilerParams(vmem_limit_bytes=48 << 20)
TILE = 1024


def pair_kernel(dim, left_ref, right_ref, left_mate_ref, right_mate_ref, out_ref):
    total = dot(left_ref[...], right_ref[...], dim, 0) + dot(left_mate_ref[...], right_mate_ref[...], dim, 0)
    out_ref[...] = total.astype(LOW)


def pair_product(left, right, left_mate, right_mate, dim):
    units = left.shape[1 - dim]
    rows, width = right.shape
    tile = next(units // n for n in range(1, units) if units % n == 0 and units // n <= TILE)
    if dim:
        block = pl.BlockSpec((tile, rows), lambda i: (i, 0))
    else:
        block = pl.BlockSpec((rows, tile), lambda i: (0, i))
    whole = pl.BlockSpec((rows, width), lambda i: (0, 0))
    return pl.pallas_call(
        functools.partial(pair_kernel, dim),
        grid=(units // tile,),
        in_specs=[block, whole, block, whole],
        out_specs=pl.BlockSpec((tile, width), lambda i: (i, 0)),
        out_shape=jax.ShapeDtypeStruct((units, width), LOW),
        compiler_params=VMEM,
        cost_estimate=SMALL_COST,
        name="pair_product",
    )(left, right, left_mate, right_mate)


def split_kernel(picks, tile, learn, *refs):
    left, right, left_mate, right_mate = refs[:4]
    outs = refs[-2:]
    if learn:
        index_ref, extra = refs[4], refs[5]
        if learn == "make":
            learn_left, learn_right, learn_left_mate, learn_right_mate = refs[5:9]
            extra = refs[9]
            outs = refs[10:12]
            extra[...] = (
                dot(learn_left[...], learn_right[...], 0, 0) + dot(learn_left_mate[...], learn_right_mate[...], 0, 0)
            ).astype(LOW)
        links = left.shape[1] // (2 * tile)
        rows = extra.shape[0] // (2 * links)
    for half, (some, out) in enumerate(zip(picks, outs)):
        at = 0
        for link in some:
            spot = half * (left.shape[1] // 2) + link * tile
            columns = slice(spot, spot + tile)
            total = dot(left[:, columns], right[...], 0, 0) + dot(left_mate[:, columns], right_mate[...], 0, 0)
            out[at : at + tile] = total.astype(LOW)
            at += tile
            if learn:
                source = (half * links + (link ^ (index_ref[0] // 2))) * rows
                out[at : at + rows] = extra[pl.ds(pl.multiple_of(source, rows), rows)]
                at += rows


def split_product(left, right, left_mate, right_mate, picks, links, index=None, learn=None):
    tile = left.shape[1] // (2 * links)
    width = right.shape[1]
    rows = tile
    args = [left, right, left_mate, right_mate]
    specs = [pl.BlockSpec(memory_space=pltpu.VMEM)] * 4
    out_shape = []
    if learn is not None:
        args += [index[None], *learn]
        specs += [pl.BlockSpec(memory_space=pltpu.SMEM)] + [pl.BlockSpec(memory_space=pltpu.VMEM)] * len(learn)
        units = learn[0].shape[1] if len(learn) > 1 else learn[0].shape[0]
        rows += units // (2 * links)
        if len(learn) > 1:
            out_shape.append(jax.ShapeDtypeStruct((units, width), LOW))
    mode = None if learn is None else "make" if len(learn) > 1 else "take"
    out_shape += [jax.ShapeDtypeStruct((len(some) * rows, width), LOW) for some in picks]
    return pl.pallas_call(
        functools.partial(split_kernel, picks, tile, mode),
        out_shape=out_shape,
        in_specs=specs,
        out_specs=[pl.BlockSpec(memory_space=pltpu.VMEM)] * len(out_shape),
        compiler_params=VMEM,
        cost_estimate=SMALL_COST,
        name="split_product",
    )(*args)


def back_kernel(count, source_ref, *refs):
    rows = refs[-1].shape[0]
    row = pl.program_id(0) * rows + lax.broadcasted_iota(jnp.int32, (rows, source_ref.shape[1]), 0)
    spot = (row == source_ref[...]).astype(WIDE).astype(LOW)
    total, at = 0.0, 0
    for ref in refs[:count]:
        total = total + dot(spot[:, at : at + ref.shape[0]], ref[...], 1, 0)
        at += ref.shape[0]
    if len(refs) > count + 1:
        total = total + refs[count][...].astype(WIDE)
    refs[-1][...] = total.astype(LOW)


def rows_home(blocks, rows, base=None):
    sources = jnp.concatenate([b[0] for b in blocks])[None]
    values = [b[1] for b in blocks]
    width = values[0].shape[1]
    tile = min(512, rows)
    whole = lambda array: pl.BlockSpec(array.shape, lambda i: (0, 0))
    block = pl.BlockSpec((tile, width), lambda i: (i, 0))
    return pl.pallas_call(
        functools.partial(back_kernel, len(values)),
        grid=(rows // tile,),
        in_specs=[whole(sources)] + [whole(v) for v in values] + ([] if base is None else [block]),
        out_specs=block,
        out_shape=jax.ShapeDtypeStruct((rows, width), LOW),
        compiler_params=VMEM,
        cost_estimate=SMALL_COST,
        name="rows_home",
    )(sources, *values, *([] if base is None else [base]))


def rows_back_kernel(first_ref, second_ref, w_first_ref, w_second_ref, base_ref, normed_ref, inverse_ref, gain_ref, wide_ref, low_ref, gain_grad_ref, held):
    step = pl.program_id(0)
    held[step] = dot(first_ref[...], w_first_ref[...], 1, 0) + dot(second_ref[...], w_second_ref[...], 1, 0)

    @pl.when(step == pl.num_programs(0) - 1)
    def _():
        count, _, tile = held.shape
        parts = [slice(i * tile, (i + 1) * tile) for i in range(count)]
        mean, cross = 0.0, 0.0
        for i, part in enumerate(parts):
            normed = normed_ref[:, part]
            product = held[i] * normed
            gain_grad_ref[:, part] = jnp.sum(product, axis=0, keepdims=True)
            gain = gain_ref[:, part]
            mean = mean + jnp.sum(held[i] * gain, axis=1, keepdims=True)
            cross = cross + jnp.sum(product * gain, axis=1, keepdims=True)
        mean, cross = mean / (count * tile), cross / (count * tile)
        for i, part in enumerate(parts):
            scaled = held[i] * gain_ref[:, part]
            total = base_ref[:, part] + (scaled - mean - normed_ref[:, part] * cross) * inverse_ref[...]
            wide_ref[:, part] = total
            low_ref[:, part] = total.astype(LOW)


def rows_back(grads, weights, base, normed, inverse, gain):
    rows, width = base.shape
    units = grads[0].shape[1]
    tile = min(256, width)
    whole = lambda *shape: pl.BlockSpec(shape, lambda i: (0,) * len(shape))
    columns = pl.BlockSpec((units, tile), lambda i: (0, i))
    return pl.pallas_call(
        rows_back_kernel,
        grid=(width // tile,),
        in_specs=[
            whole(rows, units),
            whole(rows, units),
            columns,
            columns,
            whole(rows, width),
            whole(rows, width),
            whole(rows, 1),
            whole(1, width),
        ],
        out_specs=[whole(rows, width), whole(rows, width), whole(1, width)],
        out_shape=[
            jax.ShapeDtypeStruct((rows, width), WIDE),
            jax.ShapeDtypeStruct((rows, width), LOW),
            jax.ShapeDtypeStruct((1, width), WIDE),
        ],
        scratch_shapes=[pltpu.VMEM((width // tile, rows, tile), WIDE)],
        compiler_params=VMEM,
        cost_estimate=SMALL_COST,
        name="rows_back",
    )(*grads, *weights, base, normed, inverse, gain[None])


def two_kernel(first_ref, second_ref, right_ref, out_first_ref, out_second_ref):
    right = right_ref[...]
    out_first_ref[...] = dot(first_ref[...], right, 1, 1).astype(LOW)
    out_second_ref[...] = dot(second_ref[...], right, 1, 1).astype(LOW)


def two_products(weights, right):
    return pl.pallas_call(
        two_kernel,
        out_shape=[jax.ShapeDtypeStruct((w.shape[0], right.shape[0]), LOW) for w in weights],
        compiler_params=VMEM,
        cost_estimate=SMALL_COST,
        name="two_products",
    )(*weights, right)


def attend_kernel(scale, first_ref, second_ref, column_ref, row_ref, mixed_first_ref, mixed_second_ref, log_ref):
    query, key, value = [jnp.concatenate([first_ref[i, 0], second_ref[i, 0]]) for i in range(3)]
    scores = dot(key, query * scale, 0, 0)
    scores = jnp.where(column_ref[...] == row_ref[...], scores, FAR)
    most = jnp.max(scores, axis=0, keepdims=True)
    exponent = jnp.exp(scores - most)
    total = jnp.sum(exponent, axis=0, keepdims=True)
    mixed = (dot(value, exponent.astype(LOW), 1, 0) / total).astype(LOW)
    half = mixed.shape[0] // 2
    mixed_first_ref[0] = mixed[:half]
    mixed_second_ref[0] = mixed[half:]
    log_ref[0] = most + jnp.log(total)


def attend(first, second, image, scale):
    _, heads, half, rows = first.shape
    three = pl.BlockSpec((3, 1, half, rows), lambda h: (0, h, 0, 0))
    one = pl.BlockSpec((1, half, rows), lambda h: (h, 0, 0))
    return pl.pallas_call(
        functools.partial(attend_kernel, scale),
        grid=(heads,),
        in_specs=[
            three,
            three,
            pl.BlockSpec((rows, 1), lambda h: (0, 0)),
            pl.BlockSpec((1, rows), lambda h: (0, 0)),
        ],
        out_specs=[one, one, pl.BlockSpec((1, 1, rows), lambda h: (h, 0, 0))],
        out_shape=[
            jax.ShapeDtypeStruct((heads, half, rows), LOW),
            jax.ShapeDtypeStruct((heads, half, rows), LOW),
            jax.ShapeDtypeStruct((heads, 1, rows), WIDE),
        ],
        compiler_params=pltpu.CompilerParams(vmem_limit_bytes=48 << 20),
        cost_estimate=SMALL_COST,
        name="attend",
    )(first, second, image[:, None], image[None, :])


def attend_back_kernel(
    scale,
    first_ref,
    second_ref,
    mixed_first_ref,
    mixed_second_ref,
    grad_first_ref,
    grad_second_ref,
    log_ref,
    column_ref,
    row_ref,
    *out_refs,
):
    out_first_ref, out_second_ref = out_refs[-2:]
    query, key, value = [jnp.concatenate([first_ref[i, 0], second_ref[i, 0]]) for i in range(3)]
    query = query * scale
    mixed = jnp.concatenate([mixed_first_ref[0], mixed_second_ref[0]])
    grad = jnp.concatenate([grad_first_ref[0], grad_second_ref[0]])
    scores = dot(key, query, 0, 0)
    scores = jnp.where(column_ref[...] == row_ref[...], scores, FAR)
    probs = jnp.exp(scores - log_ref[0])
    grad_probs = dot(value, grad, 0, 0)
    inner = jnp.sum(mixed.astype(WIDE) * grad.astype(WIDE), axis=0, keepdims=True)
    grad_scores = (probs * (grad_probs - inner)).astype(LOW)
    grads = (
        (dot(key, grad_scores, 1, 0) * scale).astype(LOW),
        dot(query, grad_scores, 1, 1).astype(LOW),
        dot(grad, probs.astype(LOW), 1, 1).astype(LOW),
    )
    half = mixed.shape[0] // 2
    for i, item in enumerate(grads):
        out_first_ref[i, 0] = item[:half]
        out_second_ref[i, 0] = item[half:]


def attend_back(first, second, mixed, grad_mixed, log_sums, image, scale, part, so_far=()):
    _, heads, half, rows = first.shape
    base = part * (heads // 2)
    three = pl.BlockSpec((3, 1, half, rows), lambda h: (0, base + h, 0, 0))
    one = pl.BlockSpec((1, half, rows), lambda h: (base + h, 0, 0))
    return pl.pallas_call(
        functools.partial(attend_back_kernel, scale),
        grid=(heads // 2,),
        in_specs=[
            three,
            three,
            one,
            one,
            one,
            one,
            pl.BlockSpec((1, 1, rows), lambda h: (base + h, 0, 0)),
            pl.BlockSpec((rows, 1), lambda h: (0, 0)),
            pl.BlockSpec((1, rows), lambda h: (0, 0)),
        ]
        + [pl.BlockSpec(memory_space=pl.ANY)] * len(so_far),
        out_specs=[three, three],
        out_shape=[jax.ShapeDtypeStruct((3, heads, half, rows), LOW)] * 2,
        input_output_aliases={9 + i: i for i in range(len(so_far))},
        compiler_params=pltpu.CompilerParams(vmem_limit_bytes=48 << 20),
        cost_estimate=SMALL_COST,
        name="attend_back",
    )(first, second, *mixed, *grad_mixed, log_sums, image[:, None], image[None, :], *so_far)


def local(
    n_dp,
    n_tensor,
    patches,
    pos_embed,
    counts,
    ln1_gain,
    w_qkv,
    w_out,
    ln2_gain,
    w_up,
    w_down,
    ln3_gain,
    w_learn1,
    w_learn2,
    cotangent,
):
    rows, width = patches.shape
    images = counts.shape[1]
    tokens = w_learn2.shape[1]
    capacity = row_capacity(rows, images, n_tensor)
    scale = HEAD_DIM**-0.5
    tensor_index = lax.axis_index("tensor")
    index = lax.axis_index("dp")
    heads = n_tensor * w_qkv.shape[2] // HEAD_DIM
    mate = lambda value: swap(value, "dp", n_dp, 1)

    links = n_dp.bit_length() - 2
    spans = n_tensor.bit_length() - 1
    turned = jnp.transpose(w_qkv, (1, 2, 0))
    z_a = Flow(1, gather_tensor([my_piece(turned, n_dp, index)], n_tensor))
    place = place_images(counts, n_tensor)
    image, source = row_map(place, counts, tensor_index, capacity)
    part_up = w_up.shape[1] // n_dp
    piece_up = jnp.transpose(lax.dynamic_slice_in_dim(w_up, index * part_up, part_up, 1))
    pieces = [my_piece(w_out[None], n_dp, index), piece_up.reshape(2, part_up // 2, width)]
    piece_down = my_piece(w_down[None], n_dp, index)
    (far_a,) = z_a.finish(source)
    x_a = Flow(links, link_gathers(far_a, n_dp))
    z_b = Flow(1, gather_tensor([after(p, far_a) for p in pieces], n_tensor))
    pick = (after(source, far_a)[:, None] == jnp.arange(rows, dtype=jnp.int32)[None, :]).astype(LOW)
    inputs = dot(pick, patches, 1, 0)
    x_a.go(inputs)
    inputs = inputs + dot(pick, after(pos_embed, *x_a.sent), 1, 0)
    normed_one, inverse_one = layer_norm(inputs)
    low_one = (normed_one * ln1_gain).astype(LOW)
    own_qkv = own_units(after(turned, *x_a.sent), n_dp, index)
    own_up = own_units(jnp.transpose(after(w_up, *x_a.sent))[None], n_dp, index)
    near_a = links_first(x_a.finish(low_one), n_dp)
    core_a = [swap(v, "dp", n_dp, 1) for v in near_a]
    shards = [turned, w_out[None], None, w_down[None]]
    sizes = [
        (3, w_qkv.shape[2] // (2 * n_dp)),
        (1, w_out.shape[0] // (2 * n_dp)),
        (1, w_up.shape[1] // (2 * n_dp)),
        (1, w_down.shape[0] // (2 * n_dp)),
    ]
    units_of = lambda halves, some: far_units(halves, some, n_dp, n_tensor)
    qkv = [None, None]

    def project(core, halves):
        full = join(own_qkv[core], units_of(halves, sizes[:1])[0], False)
        qkv[core] = dot_low(full, low_one, 1, 1).reshape(3, heads, -1, capacity)
        return full

    full_qkv = [project(0, near_a)]
    core_a = [after(c, qkv[0]) for c in core_a]
    (far_b,) = z_b.finish(*own_up)
    x_b = Flow(links, link_gathers(far_b, n_dp))
    z_c = Flow(1, gather_tensor([after(piece_down, far_b)], n_tensor))
    full_qkv.append(project(1, core_a))
    mixed_first, mixed_second, log_sums = attend(*qkv, image, scale)
    mixed = [m.reshape(-1, capacity) for m in (mixed_first, mixed_second)]
    x_b.go(mixed[0])
    own_out = own_units(after(w_out, *x_b.sent)[None], n_dp, index)
    (far_c,) = z_c.finish(*own_out)
    x_c = Flow(links, link_gathers(far_c, n_dp))
    own_down = own_units(after(w_down, *x_c.sent)[None], n_dp, index)
    near_b = links_first(x_b.finish(*own_down), n_dp)
    core_b = [swap(v, "dp", n_dp, 1) for v in near_b]
    full_out, full_up, full_down = [], [], []

    def join_b(core, halves):
        far_out, far_up = units_of(halves, sizes[1:3])
        full_out.append(join(own_out[core], far_out, False))
        full_up.append(join(own_up[core], far_up, True))

    join_b(0, near_b)
    x_c.go(full_up[0])
    join_b(1, [after(c, full_up[0], *x_c.sent) for c in core_b])
    member = (image[:, None] == jnp.arange(images, dtype=jnp.int32)[None, :]).astype(WIDE)
    row_scale = jnp.sum(member * lax.rsqrt(counts[0].astype(WIDE))[None, :], axis=1)

    hidden = inputs + dot(mixed[0], full_out[0], 0, 0) + dot(mixed[1], full_out[1], 0, 0)
    normed_two, inverse_two = layer_norm(hidden)
    low_two = (normed_two * ln2_gain).astype(LOW)
    mate_mixed, mate_one = mate(after(mixed[1], low_two)), mate(after(low_one, low_two))
    active, slope = [], []

    def feed(core, normed):
        value, rate = gelu_both(dot(normed, full_up[core], 1, 1))
        active.append(value.astype(LOW))
        slope.append(rate.astype(LOW))

    feed(0, low_two)
    near_c = links_first(x_c.finish(active[0]), n_dp)
    core_c = [swap(v, "dp", n_dp, 1) for v in near_c]
    feed(1, after(low_two, mate_mixed, mate_one, active[0]))
    full_down.append(join(own_down[0], units_of(near_c, sizes[3:])[0], True))
    fed = dot(active[0], full_down[0], 1, 0)
    mate_active, mate_two = mate(active[1]), mate(low_two)
    core_c = [after(c, active[1], full_down[0]) for c in core_c]
    full_down.append(join(own_down[1], units_of(core_c, sizes[3:])[0], True))
    output = hidden + fed + dot(active[1], full_down[1], 1, 0)
    normed_three, inverse_three = layer_norm(output)
    low_three = (normed_three * ln3_gain).astype(LOW)
    low_three = after(low_three, mate_active, mate_two)
    acted, learn_slope = gelu_both(dot(low_three, w_learn1, 1, 0))
    acted, learn_slope = acted.astype(LOW), learn_slope.astype(LOW)
    select = jax.nn.sigmoid(dot(acted, w_learn2, 1, 0))
    weights = (select * row_scale[:, None]).astype(LOW)
    table = (member.astype(LOW)[:, :, None] * weights[:, None, :]).reshape(capacity, images * tokens)
    low_out = output.astype(LOW)
    learned = dot_low(table, low_out, 0, 0)

    grad_pooled = cotangent.reshape(images * tokens, width)
    grad_output = dot(table, grad_pooled, 1, 0)
    grad_table = dot(low_out, grad_pooled, 1, 1)
    grad_weights = jnp.sum(grad_table.reshape(capacity, images, tokens) * member[:, :, None], axis=1)
    grad_logits = (grad_weights * row_scale[:, None] * select * (1.0 - select)).astype(LOW)
    grad_learn2 = dot(grad_logits, acted, 0, 0)
    grad_inner = (dot(grad_logits, w_learn2, 1, 1) * learn_slope.astype(WIDE)).astype(LOW)
    side = width // 2
    three_keep = lax.dynamic_slice_in_dim(low_three, (index & 1) * side, side, 1)
    three_away = lax.dynamic_slice_in_dim(low_three, (1 - (index & 1)) * side, side, 1)
    mate_three, mate_inner = mate(three_away), mate(grad_inner)
    grad_from_three, grad_gain3 = norm_back(
        dot(grad_inner, w_learn1, 1, 1), ln3_gain, normed_three, inverse_three
    )
    grad_output = grad_output + grad_from_three

    grad_fed = grad_output.astype(LOW)
    mate_three, mate_inner = after(mate_three, grad_fed), after(mate_inner, grad_fed)
    mate_fed = mate(grad_fed)
    units = functools.partial(split_units, n_dp=n_dp, n_tensor=n_tensor)
    ready = after(grad_fed, mate_three, mate_inner)
    upward = lambda c, grad: (dot(grad, full_down[c], 1, 1) * slope[c].astype(WIDE)).astype(LOW)
    grad_upper = [None, upward(1, ready)]
    mate_upper = mate(grad_upper[1])
    mate_fed = after(mate_fed, grad_upper[1])
    away, stay = first_split(n_dp, True), first_split(n_dp, False)
    down_operands = (active[0], grad_fed, mate_active, mate_fed)
    grad_learn1, *down_away = split_product(
        *down_operands, away, n_dp // 2, index, (three_keep, grad_inner, mate_three, mate_inner)
    )
    down_stay = split_product(*down_operands, stay, n_dp // 2, index, (grad_learn1,))
    bits_left = (2,) * (n_dp.bit_length() - 3)
    kept = lambda parts: [[p.reshape(bits_left + (-1, width))] for p in parts]
    x_down = Flow(links, link_sums_from(kept(down_stay), down_away, n_dp))
    grad_upper[0] = upward(0, after(grad_fed, *down_stay))
    mate_upper = after(mate_upper, grad_upper[0])
    grad_hidden, grad_attended, grad_gain2 = rows_back(
        grad_upper, full_up, grad_output, normed_two, inverse_two, ln2_gain
    )
    grad_gain2 = grad_gain2[0]

    grad_mixed = [g.reshape(heads, -1, capacity) for g in two_products(full_out, grad_attended)]
    x_down.go(*grad_mixed)
    up_operands = (after(grad_upper[0], *x_down.sent), low_two, mate_upper, mate_two)
    up_away = split_product(*up_operands, away, n_dp // 2)
    up_stay = split_product(*up_operands, stay, n_dp // 2)
    pair_down = x_down.finish(*up_stay)
    down_rows = active[0].shape[1] // n_dp
    everywhere = [pair_down[0][:, down_rows:], learned.reshape(2, -1, width)]
    z_down = Flow(spans, reduce_tensor([pair_down[0][:, :down_rows]], everywhere, n_tensor))
    x_up = Flow(links, link_sums_from(kept(up_stay), [after(u, *pair_down) for u in up_away], n_dp))
    grad_mixed = [after(g, *z_down.sent, *x_up.sent) for g in grad_mixed]
    mate_attended = mate(after(grad_attended, *x_up.sent))
    attended_back = functools.partial(
        attend_back, *qkv, (mixed_first, mixed_second), log_sums=log_sums, image=image, scale=scale
    )
    half_qkv = attended_back(grad_mixed, part=0)
    z_down.go(half_qkv[0])
    grad_mixed = [after(g, *z_down.sent) for g in grad_mixed]
    grad_qkv = attended_back(grad_mixed, part=1, so_far=half_qkv)
    grad_qkv = [g.reshape(-1, capacity) for g in grad_qkv]
    mate_qkv = mate(grad_qkv[1])
    grad_from_one, grad_gain1 = norm_back(
        dot(grad_qkv[0], full_qkv[0], 0, 0) + dot(grad_qkv[1], full_qkv[1], 0, 0),
        ln1_gain,
        normed_one,
        inverse_one,
    )
    near = (grad_hidden + grad_from_one).astype(LOW)
    some = capacity // 2
    ring_a = Flow(spans, gather_rows(near[:some], n_tensor))
    x_up.go(near)
    mate_qkv, mate_attended = [after(m, *x_up.sent) for m in (mate_qkv, mate_attended)]
    grad_out = pair_product(mixed[0], grad_attended, mate_mixed, mate_attended, 1)
    grad_qkv_weight = pair_product(after(grad_qkv[0], *x_up.sent), low_one, mate_qkv, mate_one, 1)
    extra = jnp.concatenate([jnp.stack([grad_gain1, grad_gain2, grad_gain3]), grad_learn2])
    extra = jnp.pad(extra, ((0, 16 * n_dp - extra.shape[0]), (0, 0)))
    extra = (extra + mate(extra)).astype(LOW)

    (sum_down,) = z_down.finish(grad_qkv_weight, grad_out)
    pair_up = x_up.finish(sum_down)
    z_up = Flow(spans, reduce_tensor(pair_up, [], n_tensor))
    x_qkv = Flow(
        links,
        link_sums(
            [
                units(after(grad_qkv_weight, *pair_up), 3, part_first=False),
                units(after(grad_out, *pair_up), 1, part_first=False),
                split_shared(after(extra, *pair_up), n_dp, index),
            ],
            n_dp,
        ),
    )
    learned = sum_down[:, -(images * tokens // 2) :].reshape(images, tokens, width)
    sum_down = sum_down[:, : -(images * tokens // 2)]
    ring_a.go(*x_qkv.sent, *z_up.sent)
    ring_b = Flow(spans, gather_rows(after(near[some:], *ring_a.sent), n_tensor))
    z_up.go(*ring_b.sent)
    x_qkv.go(*z_up.sent)
    (sum_up,) = z_up.finish(*x_qkv.sent)
    pair_qkv = x_qkv.finish(sum_up)
    z_qkv = Flow(spans, reduce_tensor(pair_qkv[:2], pair_qkv[2:], n_tensor))
    sum_seen = jnp.concatenate([after(sum_down, *pair_qkv), sum_up], axis=1)
    x_seen = Flow(links, link_gathers(sum_seen, n_dp))
    while ring_a.left > 1:
        ring_a.go(*x_seen.sent)
        ring_b.go(*ring_a.sent)
    (rows_a,) = ring_a.finish(*z_qkv.sent, *x_seen.sent)
    ring_b.go(rows_a)
    while x_seen.left > 1:
        x_seen.go(*ring_b.sent)

    z_qkv.go(*x_seen.sent)
    sources = [source] + [row_map(place, counts, tensor_index ^ j, capacity)[1] for j in range(1, n_tensor)]
    blocks = [(after(source, *z_qkv.sent), near)]
    blocks += [(sources[j][:some], rows_a[j]) for j in range(1, n_tensor)]
    early = rows_home(blocks, rows)
    (sum_qkv,) = z_qkv.finish(early)
    x_last = Flow(1, plane_spread(sum_qkv, n_dp))
    near_seen = x_seen.finish(*x_last.sent)
    seen_a = both_near(near_seen, n_dp)
    down_rows = up_rows = active[0].shape[1] // (n_tensor * n_dp)
    out_rows, qkv_rows, extra_rows = [
        grad.shape[0] // (parts * n_dp * lead)
        for grad, parts, lead in (
            (grad_out, n_tensor, 1),
            (grad_qkv_weight, n_tensor, 3),
            (extra, 1, 1),
        )
    ]
    learn_rows = grad_learn1.shape[0] // n_dp
    at = down_rows + learn_rows
    down_sum, learn_sum, up_sum = place_parts(
        seen_a,
        ((0, 1, down_rows, "plain"), (down_rows, 1, learn_rows, "shared"), (at, 1, up_rows, "turned")),
        n_dp,
        index,
    )
    (rows_b,) = ring_b.finish(*x_last.sent)
    input_grad = rows_home([(sources[j][some:], rows_b[j]) for j in range(1, n_tensor)], rows, early)
    near_c = x_last.finish(input_grad, down_sum)
    far_c = mate(jnp.stack(near_c))
    far_c = [far_c[link] for link in range(n_dp // 2)]
    qkv_sum, out_sum = place_rows(
        near_c, far_c, ((0, 3, qkv_rows, "turned"), (3 * qkv_rows, 1, out_rows, "plain")), n_dp, index
    )
    small = jnp.stack([v[0, 3 * qkv_rows + out_rows :] for v in near_c])
    small = lax.dynamic_slice_in_dim(small, index // 2, 1, 0)[0].astype(WIDE)

    return (
        learned,
        input_grad,
        small[0],
        jnp.transpose(qkv_sum, (1, 0, 2)),
        out_sum[0],
        small[1],
        up_sum[0],
        down_sum[0],
        small[2],
        learn_sum[0],
        jnp.transpose(small[3 : 3 + tokens]),
    )


def solution(mesh):
    return jax.shard_map(
        functools.partial(local, mesh.shape["dp"], mesh.shape["tensor"]),
        mesh=mesh,
        in_specs=(
            P("dp", None),
            P("dp", None),
            P("dp", None),
            P(),
            P(None, None, "tensor"),
            P("tensor", None),
            P(),
            P(None, "tensor"),
            P("tensor", None),
            P(),
            P(),
            P(),
            P("dp", None, None),
        ),
        out_specs=(
            P("dp", None, None),
            P("dp", None),
            P(),
            P(None, None, "tensor"),
            P("tensor", None),
            P(),
            P(None, "tensor"),
            P("tensor", None),
            P(),
            P(),
            P(),
        ),
        check_vma=False,
    )
```
